32 devices in a mesh: seq: 16 (over z, y, x), head: 2 (over core).
Axes of the slice: x: 2, y: 2, z: 4, core: 2. Of those that a mesh axis runs over, the one named last changes fastest.
Arguments:
- tokens: bfloat16 [2, 2, 1024, 2048], P(None, None, 'seq', 'head'), may hold values from -6 to 6
- lengths: int32 [2, 2], replicated, may hold values from 64 to 1024, as said below
- attn_gain: bfloat16 [2048], P(('seq', 'head')), may hold values from 0.5 to 1.5
- w_query: bfloat16 [2048, 256], P('seq', 'head'), may hold values from -0.125 to 0.125
- w_key: bfloat16 [2048, 256], P('seq', 'head'), may hold values from -0.125 to 0.125
- w_value: bfloat16 [2048, 2048], P('seq', 'head'), may hold values from -0.125 to 0.125
- w_output: bfloat16 [2048, 2048], P(('head', 'seq')), may hold values from -1 to 1
- ffn_gain: bfloat16 [2048], P(('seq', 'head')), may hold values from 0.5 to 1.5
- w_gate: bfloat16 [2048, 5504], P('seq', 'head'), may hold values from -0.125 to 0.125
- w_up: bfloat16 [2048, 5504], P('seq', 'head'), may hold values from -0.125 to 0.125
- w_down: bfloat16 [5504, 2048], P(('head', 'seq')), may hold values from -0.078125 to 0.078125
- cotangent: bfloat16 [2, 2, 1024, 2048], P(None, None, 'seq', 'head'), may hold values from -6 to 6
Outputs:
- mixed: bfloat16 [2, 2, 1024, 2048], P(None, None, 'seq', 'head')
- grad_tokens: float32 [2, 2, 1024, 2048], P(None, None, 'seq', 'head')
- grad_attn_gain: float32 [2048], P(('seq', 'head'))
- grad_query: float32 [2048, 256], P('seq', 'head')
- grad_key: float32 [2048, 256], P('seq', 'head')
- grad_value: float32 [2048, 2048], P('seq', 'head')
- grad_output: float32 [2048, 2048], P(('head', 'seq'))
- grad_ffn_gain: float32 [2048], P(('seq', 'head'))
- grad_gate: float32 [2048, 5504], P('seq', 'head')
- grad_up: float32 [2048, 5504], P('seq', 'head')
- grad_down: float32 [5504, 2048], P(('head', 'seq'))
The draws below stay inside these ranges and needn't reach their ends.
Inputs may be any that keep to these rules, and one draw needn't show every extreme that they name: `lengths`: in each micro-batch one row, drawn from the seed, has length 1024 and another has length 64; positions from a row's length on are padding.
All inputs are finite; a program needn't handle non-finite values.
Results may differ from the reference program's by a relative error of at most 0.013.
Values may be sent and summed in bfloat16 or wider, within the bound.
A program may use at most 704 MiB of HBM per device.

```python
import math
import jax
import jax.numpy as jnp
from jax import lax

D = 2048
HEADS = 16
FEAT = 16
HEAD_V = 128
FF = 5504
MICRO = 2
ROWS = 2
SEQ = 1024
FEATS = 273


def draw_lengths(key, part):
    key = jax.random.fold_in(key, 7)
    keys = jax.random.split(key, 4)
    shortest = SEQ // 16
    powers = jax.random.randint(keys[0], (MICRO, ROWS), 0, 5)
    spans = jnp.left_shift(jnp.full((MICRO, ROWS), shortest, jnp.int32), powers.astype(jnp.int32))
    extra = jax.random.randint(keys[1], (MICRO, ROWS), 0, 1 << 20).astype(jnp.int32) % spans
    drawn = jnp.minimum(spans + extra, SEQ)
    longest_row = jax.random.randint(keys[2], (MICRO, 1), 0, ROWS)
    shortest_row = (longest_row + 1 + jax.random.randint(keys[3], (MICRO, 1), 0, ROWS - 1)) % ROWS
    columns = jnp.arange(ROWS)[None, :]
    drawn = jnp.where(columns == longest_row, SEQ, jnp.where(columns == shortest_row, shortest, drawn))
    return drawn.astype(jnp.int32)


def steps_of(rng, dims, pieces, least, top_value):
    level = 1.0
    for dim, blocks in pieces:
        draws = jax.random.uniform(jax.random.fold_in(jax.random.fold_in(rng, 6), dim), (blocks,), jnp.float32, least / len(pieces), top_value / len(pieces))
        level = level * jnp.repeat(jnp.exp(draws), dims[dim] // blocks).reshape((-1,) + (1,) * (len(dims) - 1 - dim))
    return level


def noise(stream_key, extent, spread, most, cuts=(), held_as=jnp.bfloat16):
    level = steps_of(stream_key, extent, cuts, -0.22, 0.18) if cuts else 1.0
    values = jax.random.normal(stream_key, extent, jnp.float32) * spread * level
    return jnp.minimum(jnp.maximum(values, -most), most).astype(held_as)


def setup_inputs(seed: int = 0) -> dict:
    seeds = jax.random.split(jax.random.key(seed), 13)
    return {
        "tokens": noise(seeds[0], (MICRO, ROWS, SEQ, D), 1.0, 6.0, ((2, 16), (3, 2))),
        "lengths": draw_lengths(jax.random.fold_in(seeds[12], 71), 0),
        "attn_gain": jnp.clip(1.0 + 0.1 * jax.random.normal(seeds[2], (D,), jnp.float32), 0.5, 1.5).astype(jnp.bfloat16),
        "w_query": noise(seeds[3], (D, HEADS * FEAT), D ** -0.5, 0.125, ((0, 16), (1, 2))),
        "w_key": noise(seeds[4], (D, HEADS * FEAT), D ** -0.5, 0.125, ((0, 16), (1, 2))),
        "w_value": noise(seeds[5], (D, HEADS * HEAD_V), D ** -0.5, 0.125, ((0, 16), (1, 2))),
        "w_output": noise(seeds[6], (HEADS * HEAD_V, D), (D // 64) ** -0.5, 1.0, ((0, 32),)),
        "ffn_gain": jnp.clip(1.0 + 0.1 * jax.random.normal(seeds[7], (D,), jnp.float32), 0.5, 1.5).astype(jnp.bfloat16),
        "w_gate": noise(seeds[8], (D, FF), D ** -0.5, 0.125, ((0, 16), (1, 2))),
        "w_up": noise(seeds[9], (D, FF), D ** -0.5, 0.125, ((0, 16), (1, 2))),
        "w_down": noise(seeds[10], (FF, D), FF ** -0.5, 0.078125, ((0, 32),)),
        "cotangent": noise(seeds[11], (MICRO, ROWS, SEQ, D), 1.0, 6.0, ((2, 16), (3, 2))),
    }


HIGH = lax.Precision.HIGHEST
EPSILON = 1e-05
SQUARE_SCALE = 1.0 / (4.0 * math.sqrt(2.0))

@jax.custom_vjp
def low(v):
    return lax.optimization_barrier(v.astype(jnp.bfloat16)).astype(jnp.float32)

@jax.custom_vjp
def low_back(v):
    return v

def low_keep(v):
    return (low(v), None)

def low_pass(kept, grad):
    return (grad,)

def back_keep(v):
    return (v, None)

def back_low(kept, grad):
    return (low(grad),)
low.defvjp(low_keep, low_pass)
low_back.defvjp(back_keep, back_low)

def product(left, right):
    return jnp.dot(left, right, precision=HIGH)

def rms_norm(values, gain):
    return values * lax.rsqrt(lax.optimization_barrier(jnp.mean(values * values, axis=-1, keepdims=True)) + EPSILON) * gain

def features(vectors):
    width = vectors.shape[-1]
    outer = (vectors[..., :, None] * vectors[..., None, :]).reshape(vectors.shape[:-1] + (width * width,))
    ones = jnp.ones(vectors.shape[:-1] + (1,), jnp.float32)
    return jnp.concatenate([ones, vectors * 0.5, outer * SQUARE_SCALE], axis=-1)

def attend(queries, keys, values, live_mask):
    block_size = math.gcd(512, SEQ)
    block_count = SEQ // block_size
    causal = (jnp.arange(block_size)[:, None] >= jnp.arange(block_size)[None, :]).astype(jnp.float32)

    @jax.checkpoint
    def advance(carry, block_item):
        key_state, normal = carry
        query_block, key_block, value_block, mask_block = block_item
        scores = jnp.einsum('thf,shf->hts', query_block, key_block, precision=HIGH)
        taylor = (1.0 + scores * 0.25 + scores * scores / 32.0) * causal[None] * mask_block[None, None, :]
        query_feat = features(query_block)
        key_feat = features(key_block) * mask_block[:, None, None]
        numerator = jnp.einsum('hts,shv->thv', taylor, value_block, precision=HIGH)
        numerator = numerator + jnp.einsum('thp,hpv->thv', query_feat, key_state, precision=HIGH)
        denominator = lax.optimization_barrier(jnp.sum(taylor, axis=-1)).T + jnp.einsum('thp,hp->th', query_feat, normal, precision=HIGH)
        key_state = key_state + jnp.einsum('shp,shv->hpv', key_feat, value_block, precision=HIGH)
        normal = normal + lax.optimization_barrier(jnp.sum(key_feat, axis=0))
        return ((key_state, normal), numerator / denominator[:, :, None])
    initial = (jnp.zeros((HEADS, FEATS, HEAD_V), jnp.float32), jnp.zeros((HEADS, FEATS), jnp.float32))
    block_items = (queries.reshape(block_count, block_size, HEADS, FEAT), keys.reshape(block_count, block_size, HEADS, FEAT), values.reshape(block_count, block_size, HEADS, HEAD_V), live_mask.reshape(block_count, block_size))
    last_state, outputs = lax.scan(advance, initial, block_items)
    return outputs.reshape(SEQ, HEADS * HEAD_V)

def layer(row_values, live_mask, attn_gain, w_query, w_key, w_value, w_output, ffn_gain, w_gate, w_up, w_down):
    normed_one = low(rms_norm(row_values, attn_gain))
    queries = low_back(low(product(normed_one, w_query)))
    keys = low_back(low(product(normed_one, w_key)))
    values = low_back(low(product(normed_one, w_value)))
    attended = attend(queries.reshape(SEQ, HEADS, FEAT), keys.reshape(SEQ, HEADS, FEAT), values.reshape(SEQ, HEADS, HEAD_V), live_mask)
    attended = low(attended)
    resid = row_values + low_back(product(attended, w_output))
    normed_two = low(rms_norm(resid, ffn_gain))
    gate = low_back(product(normed_two, w_gate))
    up_proj = low_back(product(normed_two, w_up))
    hidden = low(jax.nn.silu(gate) * up_proj)
    return resid + low_back(product(hidden, w_down))

def reference(tokens, lengths, attn_gain, w_query, w_key, w_value, w_output, ffn_gain, w_gate, w_up, w_down, cotangent):
    params = tuple((weight.astype(jnp.float32) for weight in (attn_gain, w_query, w_key, w_value, w_output, ffn_gain, w_gate, w_up, w_down)))
    flat_rows = tokens.reshape(MICRO * ROWS, SEQ, D).astype(jnp.float32)
    flat_cots = cotangent.reshape(MICRO * ROWS, SEQ, D).astype(jnp.float32)
    flat_lengths = lengths.reshape(MICRO * ROWS)

    def one_row(totals, row_item):
        row_values, row_cot, row_length = row_item
        live_mask = (jnp.arange(SEQ) < row_length).astype(jnp.float32)

        def forward(values_in, *weights):
            return layer(values_in, live_mask, *weights)
        result, pullback = jax.vjp(forward, row_values, *params)
        gradients = pullback(row_cot)
        totals = tuple((total + grad for total, grad in zip(totals, gradients[1:])))
        return (totals, (result.astype(jnp.bfloat16), gradients[0]))
    zero_grads = tuple((jnp.zeros_like(weight) for weight in params))
    totals, (outputs, input_grads) = lax.scan(one_row, zero_grads, (flat_rows, flat_cots, flat_lengths))
    return (outputs.reshape(MICRO, ROWS, SEQ, D), input_grads.reshape(MICRO, ROWS, SEQ, D), totals[0], totals[1], totals[2], totals[3], totals[4], totals[5], totals[6], totals[7], totals[8])
```

```python
import jax
import jax.numpy as jnp
from jax import lax
from jax.sharding import Mesh
from jax.sharding import PartitionSpec as P

FEAT = 16
HEAD_V = 128
PLANES = 4
EPSILON = 1e-05
F32 = jnp.float32
BF16 = jnp.bfloat16


def dot(left, right, dims=((1,), (0,))):
    return lax.dot_general(left, right, (dims, ((), ())), preferred_element_type=F32)


def gather_tokens(half):
    whole = lax.all_gather(half, "core", axis=2, tiled=True)
    whole = lax.all_gather(whole, "z", axis=1, tiled=True)
    return whole.reshape(-1, whole.shape[-1])


def scatter_tokens(part, rows):
    part = part.astype(BF16).reshape(rows, -1, part.shape[-1])
    part = lax.psum_scatter(part, "core", scatter_dimension=2, tiled=True)
    return lax.psum_scatter(part, "z", scatter_dimension=1, tiled=True).astype(F32)


def spread_rows(weights):
    sent = lax.all_to_all(jnp.swapaxes(weights, 0, 1), "z", 0, 0, tiled=True)
    whole = lax.all_gather(sent, "p", axis=1, tiled=False)
    return whole.reshape(-1, weights.shape[-1])


def collect_rows(grad, own_rows):
    planes = lax.axis_size("p")
    grad = grad.astype(BF16).reshape(PLANES, planes, own_rows, grad.shape[-1])
    part = lax.psum_scatter(grad, "p", scatter_dimension=1, tiled=True)
    part = part.reshape(PLANES, own_rows, grad.shape[-1])
    return jnp.swapaxes(lax.all_to_all(part, "z", 0, 0, tiled=True), 0, 1).astype(F32)


def pad_units(weights, axis, chunk, padded):
    shape = weights.shape
    weights = weights.reshape(shape[:axis] + (-1, chunk) + shape[axis + 1 :])
    pads = [(0, 0)] * weights.ndim
    pads[axis + 1] = (0, padded - chunk)
    return jnp.pad(weights, pads).reshape(shape[:axis] + (-1,) + shape[axis + 1 :])


def to_rows(values, rows, heads):
    count = lax.axis_size("p")
    per_row = count // rows
    groups = min(per_row, heads)
    copies = per_row // groups
    width = values.shape[-1]
    values = values.reshape(rows, -1, groups, heads // groups, width)
    values = jnp.moveaxis(values, 2, 1)
    values = jnp.repeat(values.reshape((rows * groups,) + values.shape[2:]), copies, axis=0)
    values = lax.all_to_all(values, "p", 0, 0, tiled=True)
    values = values.reshape(count, PLANES, -1, heads // groups, width)
    values = jnp.transpose(values, (3, 1, 0, 2, 4))
    return values.reshape(heads // groups, -1, width)


def from_rows(values, rows, heads):
    count = lax.axis_size("p")
    per_row = count // rows
    groups = min(per_row, heads)
    copies = per_row // groups
    width = values.shape[-1]
    values = values.reshape(heads // groups, PLANES, count, -1, width)
    values = jnp.transpose(values, (2, 1, 3, 0, 4)).reshape(count, -1, heads // groups, width)
    values = lax.all_to_all(values, "p", 0, 0, tiled=True)[::copies]
    values = jnp.moveaxis(values.reshape((rows, groups) + values.shape[1:]), 1, 2)
    return values.reshape(-1, heads * width)


def batched(left, right, contract_left, contract_right):
    return lax.dot_general(
        left,
        right,
        (((contract_left,), (contract_right,)), ((0,), (0,))),
        preferred_element_type=F32,
    )


def mask_of(start, stop, live):
    queries = start + jnp.arange(stop - start)[:, None]
    keys = jnp.arange(stop)[None, :]
    return jnp.where(queries >= keys, live[None, :stop], 0.0)


def attend(queries, keys, values, live, block):
    length = queries.shape[1]
    attended, norms = [], []
    for start in range(0, length, block):
        stop = min(start + block, length)
        scores = batched(queries[:, start:stop], keys[:, :stop], 2, 2)
        taylor = (1.0 + scores * 0.25 + scores * scores / 32.0) * mask_of(start, stop, live)
        norm = jnp.sum(taylor, axis=-1, keepdims=True)
        attended.append(batched(taylor.astype(BF16), values[:, :stop], 2, 1) / norm)
        norms.append(norm)
    return jnp.concatenate(attended, axis=1), jnp.concatenate(norms, axis=1)


def attend_back(queries, keys, values, live, attended, norms, grad, block):
    length = queries.shape[1]
    grad = grad.astype(F32)
    grad_norm = -jnp.sum(grad * attended, axis=-1, keepdims=True) / norms
    grad_num = (grad / norms).astype(BF16)
    grad_queries, grad_keys, grad_values = [], 0.0, 0.0
    for start in range(0, length, block):
        stop = min(start + block, length)
        mask = mask_of(start, stop, live)
        scores = batched(queries[:, start:stop], keys[:, :stop], 2, 2)
        taylor = (1.0 + scores * 0.25 + scores * scores / 32.0) * mask
        inner = batched(grad_num[:, start:stop], values[:, :stop], 2, 2) + grad_norm[:, start:stop]
        slope = (mask * (0.25 + scores / 16.0) * inner).astype(BF16)
        grad_queries.append(batched(slope, keys[:, :stop], 2, 1))
        pad = ((0, 0), (0, length - stop), (0, 0))
        grad_keys = grad_keys + jnp.pad(batched(slope, queries[:, start:stop], 1, 1), pad)
        grad_values = grad_values + jnp.pad(
            batched(taylor.astype(BF16), grad_num[:, start:stop], 1, 1), pad
        )
    return jnp.concatenate(grad_queries, axis=1), grad_keys, grad_values


def on_device(
    tokens,
    lengths,
    attn_gain,
    w_query,
    w_key,
    w_value,
    w_output,
    ffn_gain,
    w_gate,
    w_up,
    w_down,
    cotangent,
):
    plane, place, core = (lax.axis_index(name) for name in ("z", "p", "core"))
    count = lax.axis_size("p")
    batches, per_batch, own_len, half = tokens.shape
    rows = batches * per_batch
    width = 2 * half
    own_rows = w_query.shape[0]
    heads = w_query.shape[1] // FEAT // PLANES
    chunk = w_down.shape[0]
    padded = -(-chunk // 16) * 16
    units = count * padded
    slim, broad = heads * FEAT, heads * HEAD_V

    gains = lax.all_gather(
        jnp.stack([attn_gain, ffn_gain]), ("z", "p", "core"), axis=1, tiled=True
    ).astype(F32)
    gain_one, gain_two = gains[0], gains[1]
    half_one = lax.dynamic_slice_in_dim(gain_one, core * half, half)
    half_two = lax.dynamic_slice_in_dim(gain_two, core * half, half)

    w_qkv = spread_rows(
        jnp.concatenate(
            [
                w_query.reshape(own_rows, PLANES, slim),
                w_key.reshape(own_rows, PLANES, slim),
                w_value.reshape(own_rows, PLANES, broad),
            ],
            axis=2,
        )
    )
    w_out = lax.all_gather(w_output, "p", axis=0, tiled=True)
    w_gu = spread_rows(
        jnp.concatenate(
            [
                pad_units(w_gate, 1, chunk, padded).reshape(own_rows, PLANES, units),
                pad_units(w_up, 1, chunk, padded).reshape(own_rows, PLANES, units),
            ],
            axis=2,
        )
    )
    w_dn = lax.all_gather(pad_units(w_down, 0, chunk, padded), "p", axis=0, tiled=True)

    x_half = tokens.reshape(rows, own_len, half)
    c_half = cotangent.reshape(rows, own_len, half)
    x_all = gather_tokens(x_half).astype(F32)
    inv_one = lax.rsqrt(jnp.mean(x_all * x_all, axis=-1, keepdims=True) + EPSILON)
    normed_one = (x_all * inv_one * gain_one).astype(BF16)
    x_own = x_half.astype(F32)
    inv_one = lax.dynamic_index_in_dim(
        inv_one.reshape(rows, PLANES, own_len, 1), plane, axis=1, keepdims=False
    )

    qkv = dot(normed_one, w_qkv).astype(BF16)
    pieces = [
        qkv[:, :slim].reshape(-1, heads, FEAT),
        qkv[:, slim : 2 * slim].reshape(-1, heads, FEAT),
        qkv[:, 2 * slim :].reshape(-1, heads, HEAD_V),
    ]
    row_qkv = to_rows(jnp.concatenate(pieces, axis=2), rows, heads)
    row_q, row_k, row_v = (
        row_qkv[..., :FEAT],
        row_qkv[..., FEAT : 2 * FEAT],
        row_qkv[..., 2 * FEAT :],
    )
    length = row_q.shape[1]
    live = (
        jnp.arange(length) < lax.dynamic_index_in_dim(lengths.reshape(-1), place // (count // rows))
    ).astype(F32)
    block = min(512, length)
    row_att, row_norm = attend(row_q, row_k, row_v, live, block)
    attended = from_rows(row_att.astype(BF16), rows, heads)

    resid = x_own + scatter_tokens(dot(attended, w_out), rows)
    inv_two = lax.rsqrt(
        lax.psum(jnp.sum(resid * resid, axis=-1, keepdims=True), "core") / width + EPSILON
    )
    normed_two = gather_tokens((resid * inv_two * half_two).astype(BF16))
    gate_up = dot(normed_two, w_gu)
    gate, up = gate_up[:, :units], gate_up[:, units:]
    sigmoid = jax.nn.sigmoid(gate)
    silu = gate * sigmoid
    hidden = (silu * up).astype(BF16)
    mixed = (resid + scatter_tokens(dot(hidden, w_dn), rows)).astype(BF16)

    c_all = gather_tokens(c_half)
    grad_hidden = dot(c_all, w_dn, ((1,), (1,)))
    grad_gate = (grad_hidden * up * sigmoid * (1.0 + gate * (1.0 - sigmoid))).astype(BF16)
    grad_up = (grad_hidden * silu).astype(BF16)
    grad_gu = jnp.concatenate([grad_gate, grad_up], axis=1)
    grad_two = scatter_tokens(dot(grad_gu, w_gu, ((1,), (1,))), rows)
    scaled = half_two * grad_two
    mean = lax.psum(jnp.sum(scaled * resid, axis=-1, keepdims=True), "core") / width
    grad_resid = c_half.astype(F32) + inv_two * scaled - resid * inv_two**3 * mean
    grad_mix = gather_tokens(grad_resid.astype(BF16))

    grad_att = dot(grad_mix, w_out, ((1,), (1,))).astype(BF16)
    row_grad = to_rows(grad_att.reshape(-1, heads, HEAD_V), rows, heads)
    grads = attend_back(row_q, row_k, row_v, live, row_att, row_norm, row_grad, block)
    row_back = jnp.concatenate([part.astype(BF16) for part in grads], axis=2)
    back = from_rows(row_back, rows, heads).reshape(-1, heads, 2 * FEAT + HEAD_V)
    grad_qkv = jnp.concatenate(
        [
            back[..., :FEAT].reshape(-1, slim),
            back[..., FEAT : 2 * FEAT].reshape(-1, slim),
            back[..., 2 * FEAT :].reshape(-1, broad),
        ],
        axis=1,
    )
    grad_one = scatter_tokens(dot(grad_qkv, w_qkv, ((1,), (1,))), rows)
    scaled = half_one * grad_one
    mean = lax.psum(jnp.sum(scaled * x_own, axis=-1, keepdims=True), "core") / width
    grad_tokens = grad_resid + inv_one * scaled - x_own * inv_one**3 * mean

    turned = ((0,), (0,))
    out_qkv = collect_rows(dot(normed_one, grad_qkv, turned), own_rows)
    out_gu = collect_rows(dot(normed_two, grad_gu, turned), own_rows)
    out_output = lax.psum_scatter(
        dot(attended, grad_mix, turned).astype(BF16), "p", scatter_dimension=0, tiled=True
    )
    out_down = lax.psum_scatter(
        dot(hidden, c_all, turned).astype(BF16), "p", scatter_dimension=0, tiled=True
    )

    gain_parts = jnp.stack(
        [
            jnp.sum(grad_one * x_own * inv_one, axis=(0, 1)),
            jnp.sum(grad_two * resid * inv_two, axis=(0, 1)),
        ]
    )
    gain_parts = lax.psum(gain_parts, ("z", "p"))
    gain_parts = lax.all_gather(gain_parts, "core", axis=1, tiled=True)
    own_gain = attn_gain.shape[0]
    at = ((plane * count + place) * 2 + core) * own_gain
    out_gains = lax.dynamic_slice_in_dim(gain_parts, at, own_gain, axis=1)

    def unpad(part):
        part = part.reshape(own_rows, PLANES * count, padded)[..., :chunk]
        return part.reshape(own_rows, -1)

    return (
        mixed.reshape(tokens.shape),
        grad_tokens.reshape(tokens.shape),
        out_gains[0],
        out_qkv[..., :slim].reshape(own_rows, -1),
        out_qkv[..., slim : 2 * slim].reshape(own_rows, -1),
        out_qkv[..., 2 * slim :].reshape(own_rows, -1),
        out_output.astype(F32),
        out_gains[1],
        unpad(out_gu[..., :units]),
        unpad(out_gu[..., units:]),
        out_down[:chunk].astype(F32),
    )


def solution(mesh):
    split = Mesh(mesh.devices.reshape(PLANES, -1, 2), ("z", "p", "core"))
    seq = ("z", "p")
    both = ("z", "p", "core")
    rows, columns = P(seq, "core"), P(("core", "z", "p"), None)
    tokens = P(None, None, seq, "core")
    return jax.shard_map(
        on_device,
        mesh=split,
        in_specs=(
            tokens,
            P(),
            P(both),
            rows,
            rows,
            rows,
            columns,
            P(both),
            rows,
            rows,
            columns,
            tokens,
        ),
        out_specs=(
            tokens,
            tokens,
            P(both),
            rows,
            rows,
            rows,
            columns,
            P(both),
            rows,
            rows,
            columns,
        ),
        check_vma=False,
    )
```

```python
import jax
import jax.numpy as jnp
from jax import lax
from jax.experimental import pallas as pl
from jax.experimental.pallas import tpu as pltpu
from jax.sharding import Mesh
from jax.sharding import PartitionSpec as P

FEAT = 16
HEAD_V = 128
PLANES = 4
LANES = 128
EPSILON = 1e-05
F32 = jnp.float32
BF16 = jnp.bfloat16
MESH = pl.DeviceIdType.MESH
DMA = pltpu.SemaphoreType.DMA
VMEM_LIMIT = 56 << 20
QUERY_BLOCK = 256


def remote(source, target, send, receive, device):
    return pltpu.make_async_remote_copy(
        src_ref=source,
        dst_ref=target,
        send_sem=send,
        recv_sem=receive,
        device_id=device,
        device_id_type=MESH,
    )


def here():
    return tuple(lax.axis_index(name) for name in ("z", "p", "core"))


def signal(semaphore, device):
    pl.semaphore_signal(semaphore, inc=1, device_id=device, device_id_type=MESH)


def greet_column():
    plane, place, core = here()
    barrier = pltpu.get_barrier_semaphore()
    signal(barrier, (plane, place, 1 - core))
    pl.when(plane > 0)(lambda: signal(barrier, (plane - 1, place, core)))
    pl.when(plane < PLANES - 1)(lambda: signal(barrier, (plane + 1, place, core)))
    inner = (plane > 0).astype(jnp.int32) + (plane < PLANES - 1).astype(jnp.int32)
    pl.semaphore_wait(barrier, 1 + inner)


def greet_all():
    plane, place, core = here()
    places = lax.axis_size("p")
    barrier = pltpu.get_barrier_semaphore()
    signal(barrier, (plane, place, 1 - core))
    for step in range(1, PLANES * places):
        signal(barrier, peer(step) + (core,))
    pl.semaphore_wait(barrier, PLANES * places)


def peer(step):
    plane, place, _ = here()
    places = lax.axis_size("p")
    index = lax.rem(plane * places + place + step, PLANES * places)
    return lax.div(index, places), lax.rem(index, places)


def halves(width):
    core = lax.axis_index("core")
    half = width // 2
    return (
        pl.ds(pl.multiple_of(core * half, LANES), half),
        pl.ds(pl.multiple_of((1 - core) * half, LANES), half),
    )


def gather_scratch():
    return [DMA((PLANES,)) for _ in range(5)]


def in_turn(*steps):
    steps = list(steps)
    while steps:
        steps = [one for one in steps if next(one, steps) is not steps]


def column_gather(out, sems):
    arrive, across, up, down, over = sems
    plane, place, core = here()
    mine, other = halves(out.shape[2])

    def piece(block):
        return out.at[block, :, mine]

    def rise(block):
        return remote(
            piece(block), piece(block), up.at[block], arrive.at[block], (plane + 1, place, core)
        )

    def fall(block):
        return remote(
            piece(block), piece(block), down.at[block], arrive.at[block], (plane - 1, place, core)
        )

    def cross(block):
        return remote(
            piece(block), piece(block), over.at[block], across.at[block], (plane, place, 1 - core)
        )

    def landed(block):
        remote(
            piece(block), piece(block), over.at[block], arrive.at[block], (plane, place, 1 - core)
        ).wait_recv()

    pl.when(plane < PLANES - 1)(lambda: rise(plane).start())
    pl.when(plane > 0)(lambda: fall(plane).start())
    cross(plane).start()
    yield
    for far in range(1, PLANES):

        @pl.when(plane >= far)
        def _():
            landed(plane - far)
            pl.when(plane < PLANES - 1)(lambda: rise(plane - far).start())
            cross(plane - far).start()

        @pl.when(plane + far < PLANES)
        def _():
            landed(plane + far)
            pl.when(plane > 0)(lambda: fall(plane + far).start())
            cross(plane + far).start()

        yield

    for block in range(PLANES):
        remote(
            out.at[block, :, other],
            out.at[block, :, other],
            over.at[block],
            across.at[block],
            (plane, place, 1 - core),
        ).wait_recv()
    for block in range(PLANES):
        cross(block).wait_send()
        pl.when((plane < PLANES - 1) & (block <= plane))(lambda: rise(block).wait_send())
        pl.when((plane > 0) & (block >= plane))(lambda: fall(block).wait_send())


def scatter_scratch(tokens, half):
    blocks = [pltpu.VMEM((PLANES, tokens, half), BF16) for _ in range(4)]
    return blocks + [DMA((PLANES,)) for _ in range(6)]


def column_scatter(part, scratch, total):
    twin, below, above, sent, over_s, over_r, up_s, up_r, down_s, down_r = scratch
    plane, place, core = here()
    mine, other = halves(part.shape[2])

    def cross(block):
        return remote(
            part.at[block, :, other],
            twin.at[block],
            over_s.at[block],
            over_r.at[block],
            (plane, place, 1 - core),
        )

    def rise(block):
        return remote(
            sent.at[block], below.at[block], up_s.at[block], up_r.at[block], (plane + 1, place, core)
        )

    def fall(block):
        return remote(
            sent.at[block],
            above.at[block],
            down_s.at[block],
            down_r.at[block],
            (plane - 1, place, core),
        )

    def own(block):
        return part[block, :, mine].astype(F32) + twin[block].astype(F32)

    def pass_on(block, link, came, first):
        cross(block).wait_recv()

        @pl.when(jnp.logical_not(first))
        def _():
            link(block).wait_recv()
            sent[block] = (own(block) + came[block].astype(F32)).astype(BF16)

        @pl.when(first)
        def _():
            sent[block] = own(block).astype(BF16)

        link(block).start()

    for far in range(PLANES - 1, 0, -1):
        pl.when(plane + far < PLANES)(lambda: cross(plane + far).start())
        pl.when(plane >= far)(lambda: cross(plane - far).start())
    cross(plane).start()
    yield
    for far in range(PLANES - 1, 0, -1):
        pl.when(plane + far < PLANES)(lambda: pass_on(plane + far, rise, below, plane == 0))
        pl.when(plane >= far)(lambda: pass_on(plane - far, fall, above, plane == PLANES - 1))
        yield
    cross(plane).wait_recv()
    total[...] = own(plane)

    @pl.when(plane > 0)
    def _():
        rise(plane).wait_recv()
        total[...] += below[plane].astype(F32)

    @pl.when(plane < PLANES - 1)
    def _():
        fall(plane).wait_recv()
        total[...] += above[plane].astype(F32)

    for block in range(PLANES):
        cross(block).wait_send()
        pl.when(block > plane)(lambda: rise(block).wait_send())
        pl.when(block < plane)(lambda: fall(block).wait_send())


def fold(values):
    return sum(values[:, at : at + LANES] for at in range(0, values.shape[1], LANES))


def both_cores(local, far, send, receive):
    plane, place, core = here()
    copy = remote(local, far, send, receive, (plane, place, 1 - core))
    copy.start()
    copy.wait()
    joined = local[...] + far[...]
    return [
        jnp.sum(joined[:, at : at + LANES], axis=1, keepdims=True)
        for at in range(0, joined.shape[1], LANES)
    ]


def turn_copies(blocks, spread, send, receive):
    plane, place, core = here()
    copies = []
    for step in range(1, PLANES):
        to = lax.rem(plane + step, PLANES)
        copies.append(
            remote(blocks.at[to], spread.at[plane], send.at[step], receive.at[step], (to, place, core))
        )
    return copies


def first_kernel(tile, blocks, gains, spread, pair, twin, stay_s, tile_s, tile_r, *rest):
    plane, place, core = here()
    count = PLANES * lax.axis_size("p")
    index = plane * lax.axis_size("p") + place
    turn_s, turn_r, gain_s, gain_r = rest
    greet_all()
    swap = remote(tile, twin, tile_s, tile_r, (plane, place, 1 - core))
    swap.start()
    turns = turn_copies(blocks, spread, turn_s, turn_r)
    for copy in turns:
        copy.start()
    stay = pltpu.make_async_copy(blocks.at[plane], spread.at[plane], stay_s)
    stay.start()
    swap.wait()
    pair[...] = tile[...] + twin[...]
    gains[index] = pair[...]
    sends = []
    for step in range(1, count):
        sends.append(
            remote(pair, gains.at[index], gain_s.at[step], gain_r.at[step], peer(step) + (core,))
        )
        sends[-1].start()
    stay.wait()
    for copy in turns + sends:
        copy.wait()


def gather_kernel(own, out, local, *sems):
    mine, _ = halves(out.shape[2])
    greet_column()
    copy = pltpu.make_async_copy(own, out.at[lax.axis_index("z"), :, mine], local)
    copy.start()
    copy.wait()
    in_turn(column_gather(out, sems))


def greet_cross():
    plane, place, core = here()
    places = lax.axis_size("p")
    barrier = pltpu.get_barrier_semaphore()
    for step in range(1, places):
        signal(barrier, (plane, lax.rem(place + step, places), core))
    for step in range(1, PLANES):
        signal(barrier, (lax.rem(plane + step, PLANES), place, core))
    pl.semaphore_wait(barrier, places + PLANES - 2)


def to_rows(values, seq, send, receive, local):
    plane, place, core = here()
    places = lax.axis_size("p")
    per_row = places // values.shape[1]
    copies = []
    for step in range(1, places):
        to = lax.rem(place + step, places)
        row = lax.div(to, per_row)
        copies.append(
            remote(
                values.at[:, row], seq.at[:, place], send.at[step], receive.at[step], (plane, to, core)
            )
        )
    copies.append(
        pltpu.make_async_copy(values.at[:, lax.div(place, per_row)], seq.at[:, place], local)
    )
    return copies


def start_back(seq, out, send, receive, local):
    plane, place, core = here()
    places = lax.axis_size("p")
    rows = out.shape[1]
    per_row = places // rows
    row = lax.div(place, per_row)
    speaks = lax.rem(place, per_row) == 0

    def copy(step):
        to = lax.rem(place + step, places)
        return remote(
            seq.at[:, to], out.at[:, row], send.at[step], receive.at[row], (plane, to, core)
        )

    def stay():
        return pltpu.make_async_copy(seq.at[:, place], out.at[:, row], local)

    @pl.when(speaks)
    def _():
        for step in range(1, places):
            copy(step).start()
        stay().start()

    def finish():
        @pl.when(speaks)
        def _():
            stay().wait()
            for step in range(1, places):
                copy(step).wait_send()

        for other in range(rows):

            @pl.when(other * per_row != place)
            def _():
                remote(
                    out.at[:, other],
                    out.at[:, other],
                    send.at[0],
                    receive.at[other],
                    (plane, lax.rem(place + 1, places), core),
                ).wait_recv()

    return finish


def flat(ref):
    block = ref[...]
    return block.reshape(-1, block.shape[-1])


def columns_of(seq, heads, head):
    wide = heads * HEAD_V
    slim = seq[:, wide : wide + 2 * heads * FEAT].astype(F32)
    queries = slim[:, head * FEAT : (head + 1) * FEAT].astype(BF16)
    keys = slim[:, (heads + head) * FEAT : (heads + head + 1) * FEAT].astype(BF16)
    return queries, keys, seq[:, head * HEAD_V : (head + 1) * HEAD_V]


def causal(start, stop, values):
    queries = start + lax.broadcasted_iota(jnp.int32, values.shape, 0)
    keys = lax.broadcasted_iota(jnp.int32, values.shape, 1)
    return jnp.where(queries >= keys, values, 0.0)


def attend_kernel(qkv, live, blocks, att, norms, out, seq, spread, low, *sems):
    row_s, row_r, local, back_s, back_r, back_l, turn_s, turn_r, stay_s = sems
    plane = lax.axis_index("z")
    greet_cross()
    copies = to_rows(qkv, seq, row_s, row_r, local)
    for copy in copies:
        copy.start()
    turns = turn_copies(blocks, spread, turn_s, turn_r)
    turns.append(pltpu.make_async_copy(blocks.at[plane], spread.at[plane], stay_s))
    for copy in turns:
        copy.start()
    for copy in copies:
        copy.wait()
    everything = flat(seq)
    length = everything.shape[0]
    heads = att.shape[1] // HEAD_V
    alive = live[...].astype(BF16)
    block = min(QUERY_BLOCK, length)
    for head in range(heads):
        queries, keys, values = columns_of(everything, heads, head)
        values = jnp.concatenate([values * alive, alive], axis=1)
        wide = slice(head * HEAD_V, (head + 1) * HEAD_V)
        for start in range(0, length, block):
            stop = start + block
            scores = dot(queries[start:stop], keys[:stop], ((1,), (1,)))
            half = 1.0 + 0.25 * scores
            taylor = causal(start, stop, 0.5 + 0.5 * (half * half)).astype(BF16)
            sums = dot(taylor, values[:stop])
            norm = sums[:, HEAD_V:]
            ratio = sums[:, :HEAD_V] / norm
            att[start:stop, wide] = ratio
            norms[start:stop, wide] = norm
    low[...] = att[...].astype(BF16).reshape(low.shape)
    finish = start_back(low, out, back_s, back_r, back_l)
    for copy in turns:
        copy.wait()
    finish()


def attend_back_kernel(grad_att, seq, live, att, norms, blocks, out, spread, rows, low, keep, *sems):
    row_s, row_r, local, back_s, back_r, back_l, turn_s, turn_r, stay_s = sems
    plane = lax.axis_index("z")
    greet_cross()
    copies = to_rows(grad_att, rows, row_s, row_r, local)
    for copy in copies:
        copy.start()
    turns = turn_copies(blocks, spread, turn_s, turn_r)
    turns.append(pltpu.make_async_copy(blocks.at[plane], spread.at[plane], stay_s))
    for copy in turns:
        copy.start()
    for copy in copies:
        copy.wait()
    everything = flat(seq)
    length = everything.shape[0]
    heads = att.shape[1] // HEAD_V
    alive = live[...]
    block = min(QUERY_BLOCK, length)
    grads = flat(rows).astype(F32)
    grad_q, grad_k = [], []
    for head in range(heads):
        queries, keys, values = columns_of(everything, heads, head)
        live_keys = (keys.astype(F32) * alive[:, :FEAT]).astype(BF16)
        wide = slice(head * HEAD_V, (head + 1) * HEAD_V)
        grad = grads[:, wide]
        norm = norms[:, wide]
        grad_num = (grad / norm).astype(BF16)
        grad_norm = -jnp.sum(grad * att[:, wide] / norm, axis=1, keepdims=True)
        parts = []
        for start in range(0, length, block):
            stop = start + block
            scores = dot(queries[start:stop], keys[:stop], ((1,), (1,)))
            half = 1.0 + 0.25 * scores
            taylor = causal(start, stop, 0.5 + 0.5 * (half * half)).astype(BF16)
            inner = dot(grad_num[start:stop], values[:stop], ((1,), (1,))) + grad_norm[start:stop]
            slope = causal(start, stop, half * inner).astype(BF16)
            parts.append(dot(slope, live_keys[:stop]) * 0.25)
            from_values = dot(taylor, grad_num[start:stop], ((0,), (0,)))
            from_keys = dot(slope, queries[start:stop], ((0,), (0,)))
            if start:
                keep[:start, wide] += from_values[:start]
                keep[:start, heads * HEAD_V + head * FEAT : heads * HEAD_V + (head + 1) * FEAT] += (
                    from_keys[:start]
                )
            keep[start:stop, wide] = from_values[start:]
            keep[start:stop, heads * HEAD_V + head * FEAT : heads * HEAD_V + (head + 1) * FEAT] = (
                from_keys[start:]
            )
        grad_q.append(jnp.concatenate(parts, axis=0))
        keep[:, wide] *= alive
    wide = heads * HEAD_V
    keys = keep[:, wide : wide + heads * FEAT] * (0.25 * alive[:, : heads * FEAT])
    result = jnp.concatenate([keep[:, :wide]] + grad_q + [keys], axis=1)
    low[...] = result.astype(BF16).reshape(low.shape)
    finish = start_back(low, out, back_s, back_r, back_l)
    for copy in turns:
        copy.wait()
    finish()


def mix_kernel(
    part, values, gain, other, normed, resid, inverse, whole, local, far, send, receive, keep, *rest
):
    plane = lax.axis_index("z")
    mine, _ = halves(part.shape[2])
    greet_column()
    stay = pltpu.make_async_copy(other, whole.at[plane, :, mine], keep)
    stay.start()
    stay.wait()
    in_turn(column_scatter(part, rest[10:], resid), column_gather(whole, rest[5:10]))
    resid[...] += values[...].astype(F32)
    local[...] = fold(resid[...] * resid[...])
    (total,) = both_cores(local, far, send, receive)
    scale = lax.rsqrt(total / part.shape[2] + EPSILON)
    inverse[...] = jnp.broadcast_to(scale, inverse.shape)
    normed[plane, :, mine] = (resid[...] * scale * gain[...]).astype(BF16)
    in_turn(column_gather(normed, rest[:5]))


def back_kernel(
    part,
    resid,
    inverse,
    gain,
    cotangent,
    fed,
    low,
    grad,
    gain_sum,
    mixed,
    local,
    far,
    send,
    receive,
    *rest,
):
    plane = lax.axis_index("z")
    mine, _ = halves(part.shape[2])
    greet_column()
    in_turn(column_scatter(part, rest[5:15], grad))
    scale = inverse[:, :1]
    values, above = resid[...], grad[...]
    gain_sum[...] = jnp.sum(above * values * scale, axis=0, keepdims=True)
    scaled = above * gain[...]
    local[...] = fold(scaled * values)
    (total,) = both_cores(local, far, send, receive)
    mean = total / part.shape[2]
    grad[...] = cotangent[...].astype(F32) + scale * scaled - values * scale**3 * mean
    low[plane, :, mine] = grad[...].astype(BF16)
    in_turn(column_gather(low, rest[:5]), column_scatter(fed, rest[15:25], rest[25]))
    mixed[...] = (rest[25][...] + resid[...]).astype(BF16)


def last_kernel(part, tokens, gain, resid_grad, grad, gain_sum, local, far, send, receive, *rest):
    greet_column()
    in_turn(column_scatter(part, rest, grad))
    values, above = tokens[...].astype(F32), grad[...]
    scaled = above * gain[...]
    local[:, :LANES] = fold(scaled * values)
    local[:, LANES:] = fold(values * values)
    total, square = both_cores(local, far, send, receive)
    scale = lax.rsqrt(square / part.shape[2] + EPSILON)
    gain_sum[...] = jnp.sum(above * values * scale, axis=0, keepdims=True)
    mean = total / part.shape[2]
    grad[...] = resid_grad[...] + scale * scaled - values * scale**3 * mean


def owner_kernel(sums, out, came, send, receive):
    plane, place, core = here()
    places = lax.axis_size("p")
    count = PLANES * places
    near = count // 2
    index = plane * places + place
    side = lax.div(index, near)
    barrier = pltpu.get_barrier_semaphore()
    for step in range(count):
        pl.when((step > 0) | (side != core))(lambda: signal(barrier, peer(step) + (side,)))
    pl.semaphore_wait(barrier, count - (side == core).astype(jnp.int32))
    width = sums.shape[1] // near

    def copy(step, target):
        at = step * width // LANES * LANES
        owner = core * near + step
        device = (lax.div(owner, places), lax.rem(owner, places), target)
        return remote(
            sums.at[:, pl.ds(at, LANES)],
            came.at[index],
            send.at[2 * step + target],
            receive.at[index],
            device,
        )

    def to_self(step, target):
        return (core * near + step == index) & (core == target)

    for step in range(near):
        for target in range(2):
            local = to_self(step, target)
            pl.when(jnp.logical_not(local))(lambda: copy(step, target).start())

            @pl.when(local)
            def _():
                at = step * width // LANES * LANES
                came[index] = sums[:, at : at + LANES]

    for step in range(count):
        source = lax.rem(index + step, count)

        @pl.when((step > 0) | (side != core))
        def _():
            remote(
                came.at[source], came.at[source], send.at[0], receive.at[source], (plane, place, 1 - core)
            ).wait_recv()

    out[...] = sum(came[step] for step in range(count))
    for step in range(near):
        for target in range(2):
            local = to_self(step, target)
            pl.when(jnp.logical_not(local))(lambda: copy(step, target).wait_send())


def call(kernel, identity, micros, outs, scratch, args):
    vmem = pl.BlockSpec(memory_space=pltpu.VMEM)
    return pl.pallas_call(
        kernel,
        out_shape=outs,
        in_specs=[vmem] * len(args),
        out_specs=[vmem] * len(outs),
        scratch_shapes=scratch,
        cost_estimate=pl.CostEstimate(
            flops=micros * 10**9, bytes_accessed=micros * 10**6, transcendentals=0
        ),
        compiler_params=pltpu.CompilerParams(
            collective_id=identity, has_side_effects=True, vmem_limit_bytes=VMEM_LIMIT
        ),
    )(*args)


def shape(dims, dtype):
    return jax.ShapeDtypeStruct(dims, dtype)


def first(tile, blocks, identity):
    count = PLANES * lax.axis_size("p")
    scratch = [pltpu.VMEM(tile.shape, F32), pltpu.VMEM(tile.shape, F32), DMA, DMA, DMA]
    scratch += [DMA((PLANES,)), DMA((PLANES,)), DMA((count,)), DMA((count,))]
    return call(
        first_kernel,
        identity,
        15,
        [shape((count,) + tile.shape, F32), shape(blocks.shape, BF16)],
        scratch,
        [tile, blocks],
    )


def gather_tokens(half, identity):
    tokens, width = half.shape
    (whole,) = call(
        gather_kernel,
        identity,
        43,
        [shape((PLANES, tokens, 2 * width), BF16)],
        [DMA] + gather_scratch(),
        [half],
    )
    return whole.reshape(-1, 2 * width)


def row_sems(rows):
    places = lax.axis_size("p")
    sems = [DMA((places,)), DMA((places,)), DMA, DMA((places,)), DMA((rows,)), DMA]
    return sems + [DMA((PLANES,)), DMA((PLANES,)), DMA]


def attend(qkv, live, blocks, rows, heads, identity):
    places = lax.axis_size("p")
    qkv = qkv.reshape(PLANES, rows, -1, qkv.shape[-1])
    positions, width = qkv.shape[2:]
    length = PLANES * places * positions
    wide = heads * HEAD_V
    return call(
        attend_kernel,
        identity,
        35,
        [
            shape((length, wide), F32),
            shape((length, wide), F32),
            shape((PLANES, rows, positions, wide), BF16),
            shape((PLANES, places, positions, width), BF16),
            shape(blocks.shape, BF16),
        ],
        [pltpu.VMEM((PLANES, places, positions, wide), BF16)] + row_sems(rows),
        [qkv, live, blocks],
    )


def attend_back(grad_att, seq, live, att, norms, blocks, rows, identity):
    grad_att = grad_att.reshape(PLANES, rows, -1, grad_att.shape[-1])
    positions = grad_att.shape[2]
    wide = grad_att.shape[-1]
    width = seq.shape[-1]
    return call(
        attend_back_kernel,
        identity,
        40,
        [shape((PLANES, rows, positions, width), BF16), shape(blocks.shape, BF16)],
        [
            pltpu.VMEM(seq.shape[:-1] + (wide,), BF16),
            pltpu.VMEM(seq.shape, BF16),
            pltpu.VMEM((att.shape[0], wide + LANES), F32),
        ]
        + row_sems(rows),
        [grad_att, seq, live, att, norms, blocks],
    )


def to_owners(sums, identity):
    count = PLANES * lax.axis_size("p")
    (out,) = call(
        owner_kernel,
        identity,
        8,
        [shape((sums.shape[0], LANES), F32)],
        [pltpu.VMEM((count, sums.shape[0], LANES), F32), DMA((count,)), DMA((count,))],
        [sums],
    )
    return out


def sums_scratch(tokens, count):
    return [pltpu.VMEM((tokens, count * LANES), F32) for _ in range(2)] + [DMA, DMA]


def mix(part, values, gain, other, identity):
    tokens, half = values.shape
    normed, resid, inverse, whole = call(
        mix_kernel,
        identity,
        95,
        [
            shape((PLANES, tokens, 2 * half), BF16),
            shape((tokens, half), F32),
            shape((tokens, LANES), F32),
            shape((PLANES, tokens, 2 * half), BF16),
        ],
        sums_scratch(tokens, 1)
        + [DMA]
        + gather_scratch()
        + gather_scratch()
        + scatter_scratch(tokens, half),
        [part.reshape(PLANES, tokens, 2 * half), values, gain, other],
    )
    return normed.reshape(-1, 2 * half), resid, inverse, whole.reshape(-1, 2 * half)


def mix_back(part, resid, inverse, gain, cotangent, fed, identity):
    tokens, half = resid.shape
    low, grad, gain_sum, mixed = call(
        back_kernel,
        identity,
        95,
        [
            shape((PLANES, tokens, 2 * half), BF16),
            shape((tokens, half), F32),
            shape((1, half), F32),
            shape((tokens, half), BF16),
        ],
        sums_scratch(tokens, 1)
        + gather_scratch()
        + scatter_scratch(tokens, half)
        + scatter_scratch(tokens, half)
        + [pltpu.VMEM((tokens, half), F32)],
        [
            part.reshape(PLANES, tokens, 2 * half),
            resid,
            inverse,
            gain,
            cotangent,
            fed.reshape(PLANES, tokens, 2 * half),
        ],
    )
    return low.reshape(-1, 2 * half), grad, gain_sum, mixed


def last_back(part, tokens, gain, resid_grad, identity):
    count, half = tokens.shape
    return call(
        last_kernel,
        identity,
        48,
        [shape((count, half), F32), shape((1, half), F32)],
        sums_scratch(count, 2) + scatter_scratch(count, half),
        [part.reshape(PLANES, count, 2 * half), tokens, gain, resid_grad],
    )


def dot(left, right, dims=((1,), (0,))):
    return lax.dot_general(left, right, (dims, ((), ())), preferred_element_type=F32)


def plane_sum(grad, own_rows):
    places = lax.axis_size("p")
    grad = grad.reshape(PLANES, places, own_rows, grad.shape[-1])
    return lax.psum_scatter(jnp.swapaxes(grad, 0, 1), "p", scatter_dimension=0, tiled=False)


def pad_units(weights, axis, chunk, padded):
    shape = weights.shape
    weights = weights.reshape(shape[:axis] + (-1, chunk) + shape[axis + 1 :])
    pads = [(0, 0)] * weights.ndim
    pads[axis + 1] = (0, padded - chunk)
    return jnp.pad(weights, pads).reshape(shape[:axis] + (-1,) + shape[axis + 1 :])


def on_device(
    tokens,
    lengths,
    attn_gain,
    w_query,
    w_key,
    w_value,
    w_output,
    ffn_gain,
    w_gate,
    w_up,
    w_down,
    cotangent,
):
    plane, place, core = (lax.axis_index(name) for name in ("z", "p", "core"))
    count = lax.axis_size("p")
    batches, per_batch, own_len, half = tokens.shape
    rows = batches * per_batch
    own_rows = w_query.shape[0]
    heads = w_query.shape[1] // FEAT // PLANES
    chunk = w_down.shape[0]
    padded = -(-chunk // 16) * 16
    units = count * padded
    slim, broad = heads * FEAT, heads * HEAD_V

    own_gain = attn_gain.shape[0]
    index = plane * count + place
    tile = jnp.stack([attn_gain, ffn_gain]).astype(F32)
    tile = jnp.pad(tile, ((0, 6), (0, LANES - own_gain)))
    tile = jnp.roll(tile, core * own_gain, axis=1)
    x_half = tokens.reshape(rows * own_len, half)
    c_half = cotangent.reshape(rows * own_len, half)
    qkv_blocks = jnp.concatenate(
        [
            w_value.reshape(own_rows, PLANES, broad),
            w_query.reshape(own_rows, PLANES, slim),
            w_key.reshape(own_rows, PLANES, slim),
        ],
        axis=2,
    )
    gains, w_qkv = first(tile, jnp.swapaxes(qkv_blocks, 0, 1), 0)
    w_qkv, x_half = lax.optimization_barrier((w_qkv, x_half))
    w_qkv = lax.all_gather(w_qkv, "p", axis=1, tiled=False).reshape(-1, 2 * slim + broad)
    x_all = gather_tokens(x_half, 1)
    gains = jnp.swapaxes(gains[:, :2, : 2 * own_gain], 0, 1).reshape(2, -1)
    gain_one, gain_two = gains[0], gains[1]
    half_one = lax.dynamic_slice_in_dim(gain_one, core * half, half)
    half_two = lax.dynamic_slice_in_dim(gain_two, core * half, half)
    gu_blocks = jnp.concatenate(
        [
            pad_units(w_gate, 1, chunk, padded).reshape(own_rows, PLANES, units),
            pad_units(w_up, 1, chunk, padded).reshape(own_rows, PLANES, units),
        ],
        axis=2,
    )
    gu_blocks = jnp.swapaxes(gu_blocks, 0, 1)
    w_out = lax.all_gather(w_output, "p", axis=0, tiled=True)
    w_dn = lax.all_gather(pad_units(w_down, 0, chunk, padded), "p", axis=0, tiled=True)

    x_all = x_all.astype(F32)
    inv_one = lax.rsqrt(jnp.mean(x_all * x_all, axis=-1, keepdims=True) + EPSILON)
    normed_one = (x_all * inv_one * gain_one).astype(BF16)

    qkv = dot(normed_one, w_qkv).astype(BF16)
    length = PLANES * count * own_len
    limit = lax.dynamic_index_in_dim(lengths.reshape(-1), place // (count // rows))
    live = (jnp.arange(length) < limit).astype(F32)
    live = jnp.broadcast_to(live[:, None], (length, LANES))
    att, norms, attended, seq, w_gu = attend(qkv, live, gu_blocks, rows, heads, 2)
    attended = attended.reshape(-1, broad)
    w_gu = lax.all_gather(w_gu, "p", axis=1, tiled=False).reshape(-1, 2 * units)

    normed_two, resid, inv_two, c_all = mix(
        dot(attended, w_out).astype(BF16), x_half, half_two[None], c_half, 3
    )
    gate_up = dot(normed_two, w_gu)
    gate, up = gate_up[:, :units], gate_up[:, units:]
    sigmoid = jax.nn.sigmoid(gate)
    silu = gate * sigmoid
    hidden = (silu * up).astype(BF16)
    fed = dot(hidden, w_dn).astype(BF16)

    grad_hidden = dot(c_all, w_dn, ((1,), (1,)))
    grad_gate = (grad_hidden * up * sigmoid * (1.0 + gate * (1.0 - sigmoid))).astype(BF16)
    grad_up = (grad_hidden * silu).astype(BF16)
    grad_gu = jnp.concatenate([grad_gate, grad_up], axis=1)
    turned = ((0,), (0,))
    part = dot(grad_gu, w_gu, ((1,), (1,))).astype(BF16)
    out_gu = dot(normed_two, grad_gu, turned).astype(BF16)
    out_down = dot(hidden, c_all, turned).astype(BF16)
    part, out_gu, out_down = lax.optimization_barrier((part, out_gu, out_down))
    out_gu = plane_sum(out_gu, own_rows)
    out_down = lax.psum_scatter(out_down, "p", scatter_dimension=0, tiled=True)
    grad_mix, grad_resid, gain_sum_two, mixed = mix_back(
        part, resid, inv_two, half_two[None], c_half, fed, 4
    )

    grad_att = dot(grad_mix, w_out, ((1,), (1,))).astype(BF16)
    grad_qkv, out_gu = attend_back(grad_att, seq, live, att, norms, out_gu, rows, 5)
    grad_qkv = grad_qkv.reshape(-1, 2 * slim + broad)
    out_gu = jnp.swapaxes(out_gu, 0, 1).astype(F32)
    part = dot(grad_qkv, w_qkv, ((1,), (1,))).astype(BF16)
    out_qkv = dot(normed_one, grad_qkv, turned).astype(BF16)
    out_output = dot(attended, grad_mix, turned).astype(BF16)
    part, out_qkv, out_output = lax.optimization_barrier((part, out_qkv, out_output))
    out_qkv = plane_sum(out_qkv, own_rows)
    out_output = lax.psum_scatter(out_output, "p", scatter_dimension=0, tiled=True)
    grad_tokens, gain_sum_one = last_back(part, x_half, half_one[None], grad_resid, 6)
    out_qkv = lax.all_to_all(out_qkv, "z", 0, 0, tiled=True)
    out_qkv = jnp.swapaxes(out_qkv, 0, 1).astype(F32)

    gain_parts = jnp.concatenate([gain_sum_one, gain_sum_two, jnp.zeros((6, half), F32)], axis=0)
    at = (index * 2 + core) * own_gain
    out_gains = lax.dynamic_slice_in_dim(
        to_owners(gain_parts, 7), lax.rem(at, LANES), own_gain, axis=1
    )

    def unpad(part):
        part = part.reshape(own_rows, PLANES * count, padded)[..., :chunk]
        return part.reshape(own_rows, -1)

    return (
        mixed.reshape(tokens.shape),
        grad_tokens.reshape(tokens.shape),
        out_gains[0],
        out_qkv[..., broad : broad + slim].reshape(own_rows, -1),
        out_qkv[..., broad + slim :].reshape(own_rows, -1),
        out_qkv[..., :broad].reshape(own_rows, -1),
        out_output.astype(F32),
        out_gains[1],
        unpad(out_gu[..., :units]),
        unpad(out_gu[..., units:]),
        out_down[:chunk].astype(F32),
    )


def solution(mesh):
    split = Mesh(mesh.devices.reshape(PLANES, -1, 2), ("z", "p", "core"))
    seq = ("z", "p")
    both = ("z", "p", "core")
    rows, columns = P(seq, "core"), P(("core", "z", "p"), None)
    tokens = P(None, None, seq, "core")
    return jax.shard_map(
        on_device,
        mesh=split,
        in_specs=(
            tokens,
            P(),
            P(both),
            rows,
            rows,
            rows,
            columns,
            P(both),
            rows,
            rows,
            columns,
            tokens,
        ),
        out_specs=(
            tokens,
            tokens,
            P(both),
            rows,
            rows,
            rows,
            columns,
            P(both),
            rows,
            rows,
            columns,
        ),
        check_vma=False,
    )
```

```python
import jax
import jax.numpy as jnp
from jax import lax
from jax.experimental import pallas as pl
from jax.experimental.pallas import tpu as pltpu
from jax.sharding import Mesh
from jax.sharding import PartitionSpec as P

FEAT = 16
HEAD_V = 128
PLANES = 4
LANES = 128
EPSILON = 1e-05
F32 = jnp.float32
BF16 = jnp.bfloat16
MESH = pl.DeviceIdType.MESH
DMA = pltpu.SemaphoreType.DMA
VMEM_LIMIT = 56 << 20
QUERY_BLOCK = 256
PARTS = 2
TILE = 256
ROW_BLOCK = 32


def remote(source, target, send, receive, device):
    return pltpu.make_async_remote_copy(
        src_ref=source,
        dst_ref=target,
        send_sem=send,
        recv_sem=receive,
        device_id=device,
        device_id_type=MESH,
    )


def here():
    return tuple(lax.axis_index(name) for name in ("z", "p", "core"))


def signal(semaphore, device):
    pl.semaphore_signal(semaphore, inc=1, device_id=device, device_id_type=MESH)


def greet_column():
    plane, place, core = here()
    barrier = pltpu.get_barrier_semaphore()
    signal(barrier, (plane, place, 1 - core))
    pl.when(plane > 0)(lambda: signal(barrier, (plane - 1, place, core)))
    pl.when(plane < PLANES - 1)(lambda: signal(barrier, (plane + 1, place, core)))
    inner = (plane > 0).astype(jnp.int32) + (plane < PLANES - 1).astype(jnp.int32)
    pl.semaphore_wait(barrier, 1 + inner)


def greet_all():
    plane, place, core = here()
    places = lax.axis_size("p")
    barrier = pltpu.get_barrier_semaphore()
    signal(barrier, (plane, place, 1 - core))
    for step in range(1, PLANES * places):
        signal(barrier, peer(step) + (core,))
    pl.semaphore_wait(barrier, PLANES * places)


def peer(step):
    plane, place, _ = here()
    places = lax.axis_size("p")
    index = lax.rem(plane * places + place + step, PLANES * places)
    return lax.div(index, places), lax.rem(index, places)


def halves(width):
    core = lax.axis_index("core")
    half = width // 2
    return (
        pl.ds(pl.multiple_of(core * half, LANES), half),
        pl.ds(pl.multiple_of((1 - core) * half, LANES), half),
    )


def in_turn(*steps):
    steps = list(steps)
    while steps:
        steps = [one for one in steps if next(one, steps) is not steps]


def gather_scratch():
    return [DMA((PLANES,)) for _ in range(5)]


class Gather:
    def __init__(self, out, sems):
        self.out = out
        self.arrive, self.across, self.up, self.down, self.over = sems
        self.plane, self.place, self.core = here()
        self.mine, self.other = halves(out.shape[2])

    def send(self, block, sems, receive, device):
        piece = self.out.at[block, :, self.mine]
        return remote(piece, piece, sems.at[block], receive.at[block], device)

    def rise(self, block):
        return self.send(block, self.up, self.arrive, (self.plane + 1, self.place, self.core))

    def fall(self, block):
        return self.send(block, self.down, self.arrive, (self.plane - 1, self.place, self.core))

    def cross(self, block):
        return self.send(block, self.over, self.across, (self.plane, self.place, 1 - self.core))

    def start(self):
        plane = self.plane
        pl.when(plane < PLANES - 1)(lambda: self.rise(plane).start())
        pl.when(plane > 0)(lambda: self.fall(plane).start())
        self.cross(plane).start()

    def landed(self, block):
        partner = (self.plane, self.place, 1 - self.core)
        self.send(block, self.over, self.arrive, partner).wait_recv()

    def pass_on(self, far):
        plane = self.plane

        @pl.when(plane >= far)
        def _():
            self.landed(plane - far)
            pl.when(plane < PLANES - 1)(lambda: self.rise(plane - far).start())
            self.cross(plane - far).start()

        @pl.when(plane + far < PLANES)
        def _():
            self.landed(plane + far)
            pl.when(plane > 0)(lambda: self.fall(plane + far).start())
            self.cross(plane + far).start()

    def whole(self, block):
        piece = self.out.at[block, :, self.other]
        partner = (self.plane, self.place, 1 - self.core)
        remote(piece, piece, self.over.at[block], self.across.at[block], partner).wait_recv()

    def finish(self):
        plane = self.plane
        for block in range(PLANES):
            self.cross(block).wait_send()
            pl.when((plane < PLANES - 1) & (block <= plane))(lambda: self.rise(block).wait_send())
            pl.when((plane > 0) & (block >= plane))(lambda: self.fall(block).wait_send())

    def steps(self):
        self.start()
        yield
        for far in range(1, PLANES):
            self.pass_on(far)
            yield
        for block in range(PLANES):
            self.whole(block)
        self.finish()


def order_of_arrival(step):
    plane = lax.axis_index("z")
    nearest = [sorted(range(PLANES), key=lambda block: (abs(block - own), block)) for own in range(PLANES)]
    found = jnp.int32(0)
    for own in range(PLANES):
        for at in range(PLANES):
            found = jnp.where((plane == own) & (step == at), nearest[own][at], found)
    return found


def scatter_scratch(tokens, half):
    blocks = [pltpu.VMEM((PLANES, tokens, half), BF16) for _ in range(4)]
    return blocks + [DMA((PLANES,)) for _ in range(6)]


def column_scatter(part, scratch, total):
    twin, below, above, sent, over_s, over_r, up_s, up_r, down_s, down_r = scratch
    plane, place, core = here()
    mine, other = halves(part.shape[2])

    def cross(block):
        return remote(
            part.at[block, :, other],
            twin.at[block],
            over_s.at[block],
            over_r.at[block],
            (plane, place, 1 - core),
        )

    def rise(block):
        return remote(
            sent.at[block], below.at[block], up_s.at[block], up_r.at[block], (plane + 1, place, core)
        )

    def fall(block):
        return remote(
            sent.at[block],
            above.at[block],
            down_s.at[block],
            down_r.at[block],
            (plane - 1, place, core),
        )

    def own(block):
        return part[block, :, mine].astype(F32) + twin[block].astype(F32)

    def pass_on(block, link, came, first):
        cross(block).wait_recv()

        @pl.when(jnp.logical_not(first))
        def _():
            link(block).wait_recv()
            sent[block] = (own(block) + came[block].astype(F32)).astype(BF16)

        @pl.when(first)
        def _():
            sent[block] = own(block).astype(BF16)

        link(block).start()

    for far in range(PLANES - 1, 0, -1):
        pl.when(plane + far < PLANES)(lambda: cross(plane + far).start())
        pl.when(plane >= far)(lambda: cross(plane - far).start())
    cross(plane).start()
    yield
    for far in range(PLANES - 1, 0, -1):
        pl.when(plane + far < PLANES)(lambda: pass_on(plane + far, rise, below, plane == 0))
        pl.when(plane >= far)(lambda: pass_on(plane - far, fall, above, plane == PLANES - 1))
        yield
    cross(plane).wait_recv()
    total[...] = own(plane)

    @pl.when(plane > 0)
    def _():
        rise(plane).wait_recv()
        total[...] += below[plane].astype(F32)

    @pl.when(plane < PLANES - 1)
    def _():
        fall(plane).wait_recv()
        total[...] += above[plane].astype(F32)

    for block in range(PLANES):
        cross(block).wait_send()
        pl.when(block > plane)(lambda: rise(block).wait_send())
        pl.when(block < plane)(lambda: fall(block).wait_send())


def gathers(out, scratch):
    size = out.shape[1] // PARTS
    return [
        Gather(out.at[:, pl.ds(at * size, size)], scratch[5 * at : 5 * at + 5]).steps()
        for at in range(PARTS)
    ]


def scatters(part, scratch, total):
    size = part.shape[1] // PARTS
    return [
        column_scatter(
            part.at[:, pl.ds(at * size, size)],
            scratch[10 * at : 10 * at + 10],
            total.at[pl.ds(at * size, size)],
        )
        for at in range(PARTS)
    ]


def fold(values):
    return sum(values[:, at : at + LANES] for at in range(0, values.shape[1], LANES))


def both_cores(local, far, send, receive):
    plane, place, core = here()
    copy = remote(local, far, send, receive, (plane, place, 1 - core))
    copy.start()
    copy.wait()
    joined = local[...] + far[...]
    return [
        jnp.sum(joined[:, at : at + LANES], axis=1, keepdims=True)
        for at in range(0, joined.shape[1], LANES)
    ]


def turn_copies(blocks, spread, send, receive):
    plane, place, core = here()
    copies = []
    for step in range(1, PLANES):
        to = lax.rem(plane + step, PLANES)
        copies.append(
            remote(blocks.at[to], spread.at[plane], send.at[step], receive.at[step], (to, place, core))
        )
    return copies


def first_kernel(
    own,
    tile,
    blocks,
    normed,
    qkv,
    gains,
    weights,
    whole,
    pair,
    twin,
    tiles,
    spread,
    stay,
    swap_s,
    swap_r,
    *rest,
):
    plane, place, core = here()
    places = lax.axis_size("p")
    count = PLANES * places
    index = plane * places + place
    turn_s, turn_r, gain_s, gain_r, spread_s, spread_r = rest[:6]
    mine, _ = halves(whole.shape[2])
    gather = Gather(whole, rest[6:])
    greet_all()
    swap = remote(tile, twin, swap_s, swap_r, (plane, place, 1 - core))
    swap.start()
    turns = turn_copies(blocks, spread, turn_s, turn_r)
    for copy in turns:
        copy.start()
    keep = pltpu.make_async_copy(own, whole.at[plane, :, mine], stay.at[0])
    keep.start()
    local = pltpu.make_async_copy(blocks.at[plane], spread.at[plane], stay.at[1])
    local.start()
    keep.wait()
    gather.start()
    swap.wait()
    pair[...] = tile[...] + twin[...]
    tiles[index] = pair[...]
    sends = []
    for step in range(1, count):
        sends.append(
            remote(pair, tiles.at[index], gain_s.at[step], gain_r.at[step], peer(step) + (core,))
        )
        sends[-1].start()
    local.wait()
    for copy in turns:
        copy.wait()
    around = []
    for step in range(1, places):
        to = (plane, lax.rem(place + step, places), core)
        around.append(
            remote(spread, weights.at[:, place], spread_s.at[step], spread_r.at[step], to)
        )
        around[-1].start()
    stays = pltpu.make_async_copy(spread, weights.at[:, place], stay.at[2])
    stays.start()
    gather.pass_on(1)
    for copy in sends:
        copy.wait()
    stays.wait()
    for copy in around:
        copy.wait()
    each = whole.shape[2] // count
    for at in range(0, whole.shape[2], LANES):
        group = range(at // each, (at + LANES) // each)
        gains[:, at : at + LANES] = sum(tiles[source] for source in group)
    gain = gains[0:1, :]

    def project(block):
        gather.whole(block)
        values = whole[block].astype(F32)
        scale = lax.rsqrt(jnp.mean(values * values, axis=1, keepdims=True) + EPSILON)
        normed[block] = (values * scale * gain).astype(BF16)
        flat_weights = weights[...].reshape(whole.shape[2], qkv.shape[2])
        qkv[block] = dot(normed[block], flat_weights).astype(BF16)

    project(order_of_arrival(0))
    for far in range(2, PLANES):
        gather.pass_on(far)
        project(order_of_arrival(far - 1))
    project(order_of_arrival(PLANES - 1))
    gather.finish()


def turn_copies(blocks, spread, send, receive):
    plane, place, core = here()
    copies = []
    for step in range(1, PLANES):
        to = lax.rem(plane + step, PLANES)
        copies.append(
            remote(blocks.at[to], spread.at[plane], send.at[step], receive.at[step], (to, place, core))
        )
    return copies


def greet_cross():
    plane, place, core = here()
    places = lax.axis_size("p")
    barrier = pltpu.get_barrier_semaphore()
    for step in range(1, places):
        signal(barrier, (plane, lax.rem(place + step, places), core))
    for step in range(1, PLANES):
        signal(barrier, (lax.rem(plane + step, PLANES), place, core))
    pl.semaphore_wait(barrier, places + PLANES - 2)


def to_rows(values, seq, send, receive, local):
    plane, place, core = here()
    places = lax.axis_size("p")
    per_row = places // values.shape[1]
    copies = []
    for step in range(1, places):
        to = lax.rem(place + step, places)
        row = lax.div(to, per_row)
        copies.append(
            remote(
                values.at[:, row], seq.at[:, place], send.at[step], receive.at[step], (plane, to, core)
            )
        )
    copies.append(
        pltpu.make_async_copy(values.at[:, lax.div(place, per_row)], seq.at[:, place], local)
    )
    return copies


def start_back(seq, out, send, receive, local):
    plane, place, core = here()
    places = lax.axis_size("p")
    rows = out.shape[1]
    per_row = places // rows
    row = lax.div(place, per_row)
    speaks = lax.rem(place, per_row) == 0

    def copy(step):
        to = lax.rem(place + step, places)
        return remote(
            seq.at[:, to], out.at[:, row], send.at[step], receive.at[row], (plane, to, core)
        )

    def stay():
        return pltpu.make_async_copy(seq.at[:, place], out.at[:, row], local)

    @pl.when(speaks)
    def _():
        for step in range(1, places):
            copy(step).start()
        stay().start()

    def finish():
        @pl.when(speaks)
        def _():
            stay().wait()
            for step in range(1, places):
                copy(step).wait_send()

        for other in range(rows):

            @pl.when(other * per_row != place)
            def _():
                remote(
                    out.at[:, other],
                    out.at[:, other],
                    send.at[0],
                    receive.at[other],
                    (plane, lax.rem(place + 1, places), core),
                ).wait_recv()

    return finish


def flat(ref):
    block = ref[...]
    return block.reshape(-1, block.shape[-1])


def columns_of(seq, heads, head):
    wide = heads * HEAD_V
    slim = seq[:, wide : wide + 2 * heads * FEAT].astype(F32)
    queries = slim[:, head * FEAT : (head + 1) * FEAT].astype(BF16)
    keys = slim[:, (heads + head) * FEAT : (heads + head + 1) * FEAT].astype(BF16)
    return queries, keys, seq[:, head * HEAD_V : (head + 1) * HEAD_V]


def causal(start, stop, values):
    queries = start + lax.broadcasted_iota(jnp.int32, values.shape, 0)
    keys = lax.broadcasted_iota(jnp.int32, values.shape, 1)
    return jnp.where(queries >= keys, values, 0.0)


def attend_kernel(qkv, live, blocks, att, norms, out, seq, spread, low, *sems):
    row_s, row_r, local, back_s, back_r, back_l, turn_s, turn_r, stay_s = sems
    plane = lax.axis_index("z")
    greet_cross()
    copies = to_rows(qkv, seq, row_s, row_r, local)
    for copy in copies:
        copy.start()
    turns = turn_copies(blocks, spread, turn_s, turn_r)
    turns.append(pltpu.make_async_copy(blocks.at[plane], spread.at[plane], stay_s))
    for copy in turns:
        copy.start()
    for copy in copies:
        copy.wait()
    everything = flat(seq)
    length = everything.shape[0]
    heads = att.shape[1] // HEAD_V
    alive = live[...].astype(BF16)
    block = min(QUERY_BLOCK, length)
    for head in range(heads):
        queries, keys, values = columns_of(everything, heads, head)
        values = jnp.concatenate([values * alive, alive], axis=1)
        wide = slice(head * HEAD_V, (head + 1) * HEAD_V)
        for start in range(0, length, block):
            stop = start + block
            scores = dot(queries[start:stop], keys[:stop], ((1,), (1,)))
            half = 1.0 + 0.25 * scores
            taylor = causal(start, stop, 0.5 + 0.5 * (half * half)).astype(BF16)
            sums = dot(taylor, values[:stop])
            norm = sums[:, HEAD_V:]
            ratio = sums[:, :HEAD_V] / norm
            att[start:stop, wide] = ratio
            norms[start:stop, wide] = norm
    low[...] = att[...].astype(BF16).reshape(low.shape)
    finish = start_back(low, out, back_s, back_r, back_l)
    for copy in turns:
        copy.wait()
    finish()


def attend_back_kernel(grad_att, seq, live, att, norms, blocks, out, spread, rows, low, keep, *sems):
    row_s, row_r, local, back_s, back_r, back_l, turn_s, turn_r, stay_s = sems
    plane = lax.axis_index("z")
    greet_cross()
    copies = to_rows(grad_att, rows, row_s, row_r, local)
    for copy in copies:
        copy.start()
    turns = turn_copies(blocks, spread, turn_s, turn_r)
    turns.append(pltpu.make_async_copy(blocks.at[plane], spread.at[plane], stay_s))
    for copy in turns:
        copy.start()
    for copy in copies:
        copy.wait()
    everything = flat(seq)
    length = everything.shape[0]
    heads = att.shape[1] // HEAD_V
    alive = live[...]
    block = min(QUERY_BLOCK, length)
    grads = flat(rows).astype(F32)
    grad_q, grad_k = [], []
    for head in range(heads):
        queries, keys, values = columns_of(everything, heads, head)
        live_keys = (keys.astype(F32) * alive[:, :FEAT]).astype(BF16)
        wide = slice(head * HEAD_V, (head + 1) * HEAD_V)
        grad = grads[:, wide]
        norm = norms[:, wide]
        grad_num = (grad / norm).astype(BF16)
        grad_norm = -jnp.sum(grad * att[:, wide] / norm, axis=1, keepdims=True)
        parts = []
        for start in range(0, length, block):
            stop = start + block
            scores = dot(queries[start:stop], keys[:stop], ((1,), (1,)))
            half = 1.0 + 0.25 * scores
            taylor = causal(start, stop, 0.5 + 0.5 * (half * half)).astype(BF16)
            inner = dot(grad_num[start:stop], values[:stop], ((1,), (1,))) + grad_norm[start:stop]
            slope = causal(start, stop, half * inner).astype(BF16)
            parts.append(dot(slope, live_keys[:stop]) * 0.25)
            from_values = dot(taylor, grad_num[start:stop], ((0,), (0,)))
            from_keys = dot(slope, queries[start:stop], ((0,), (0,)))
            if start:
                keep[:start, wide] += from_values[:start]
                keep[:start, heads * HEAD_V + head * FEAT : heads * HEAD_V + (head + 1) * FEAT] += (
                    from_keys[:start]
                )
            keep[start:stop, wide] = from_values[start:]
            keep[start:stop, heads * HEAD_V + head * FEAT : heads * HEAD_V + (head + 1) * FEAT] = (
                from_keys[start:]
            )
        grad_q.append(jnp.concatenate(parts, axis=0))
        keep[:, wide] *= alive
    wide = heads * HEAD_V
    keys = keep[:, wide : wide + heads * FEAT] * (0.25 * alive[:, : heads * FEAT])
    result = jnp.concatenate([keep[:, :wide]] + grad_q + [keys], axis=1)
    low[...] = result.astype(BF16).reshape(low.shape)
    finish = start_back(low, out, back_s, back_r, back_l)
    for copy in turns:
        copy.wait()
    finish()


def mix_kernel(
    part, values, gain, other, normed, resid, inverse, whole, local, far, send, receive, keep, *rest
):
    plane = lax.axis_index("z")
    mine, _ = halves(part.shape[2])
    greet_column()
    stay = pltpu.make_async_copy(other, whole.at[plane, :, mine], keep)
    stay.start()
    stay.wait()
    in_turn(*scatters(part, rest[5 * PARTS :], resid), *gathers(whole, rest[: 5 * PARTS]))
    resid[...] += values[...].astype(F32)
    local[...] = fold(resid[...] * resid[...])
    (total,) = both_cores(local, far, send, receive)
    scale = lax.rsqrt(total / part.shape[2] + EPSILON)
    inverse[...] = jnp.broadcast_to(scale, inverse.shape)
    normed[...] = (resid[...] * scale * gain[...]).astype(BF16)


def feed_kernel(
    own,
    w_gu,
    w_dn,
    grads,
    part,
    fed,
    out_gu,
    out_dn,
    normed,
    held_gu,
    held_dn,
    held_c,
    sum_gu,
    sum_dn,
    gate_up,
    grad_hidden,
    hidden,
    grad_gu,
    stage,
    load,
    keep,
    store,
    *sems,
):
    plane = lax.axis_index("z")
    mine, _ = halves(normed.shape[2])
    units = hidden.shape[1]
    broad = units // LANES * LANES
    rest = units - broad
    rows = normed.shape[1]
    loads = [
        pltpu.make_async_copy(w_gu, held_gu, load.at[0]),
        pltpu.make_async_copy(w_dn, held_dn, load.at[1]),
        pltpu.make_async_copy(grads, held_c, load.at[2]),
    ]
    for copy in loads:
        copy.start()
    gather = Gather(normed, sems)
    greet_column()
    stay = pltpu.make_async_copy(own, normed.at[plane, :, mine], keep)
    stay.start()
    stay.wait()
    gather.start()
    sum_gu[...] = jnp.zeros_like(sum_gu)
    sum_dn[...] = jnp.zeros_like(sum_dn)
    for copy in loads:
        copy.wait()

    def tiles(width):
        return [slice(at, min(at + TILE, width)) for at in range(0, width, TILE)]

    def stores(block, slot):
        return (
            pltpu.make_async_copy(stage.at[0, slot], fed.at[block], store.at[0, slot]),
            pltpu.make_async_copy(stage.at[1, slot], part.at[block], store.at[1, slot]),
        )

    def middle(at):
        here_rows = pl.ds(pl.multiple_of(at * ROW_BLOCK, ROW_BLOCK), ROW_BLOCK)

        def parts(gate, up, above):
            sigmoid = jax.nn.sigmoid(gate)
            silu = gate * sigmoid
            slope = sigmoid * (1.0 + gate * (1.0 - sigmoid))
            return silu * up, above * up * slope, above * silu

        both = gate_up[here_rows, :]
        above = grad_hidden[here_rows, :]
        first, second, third = parts(
            both[:, :broad], both[:, broad : 2 * broad], above[:, :broad]
        )
        hidden[here_rows, :broad] = first.astype(BF16)
        grad_gu[here_rows, :broad] = second.astype(BF16)
        grad_gu[here_rows, broad : 2 * broad] = third.astype(BF16)
        if rest:
            last = both[:, 2 * broad :]
            turned = pltpu.roll(last, rest, 1)
            first, second, third = parts(last, turned, above[:, broad : broad + LANES])
            hidden[here_rows, broad:] = first[:, :rest].astype(BF16)
            lane = lax.broadcasted_iota(jnp.int32, last.shape, 1)
            joined = jnp.where(lane < rest, second, pltpu.roll(third, rest, 1))
            grad_gu[here_rows, 2 * broad :] = joined.astype(BF16)

    def through(step, carry):
        pl.when(step > 0)(lambda: gather.pass_on(step))
        block = order_of_arrival(step)
        slot = lax.rem(step, 2)
        gather.whole(block)
        for cut in tiles(2 * units):
            gate_up[:, cut] = dot(normed[block], held_gu[:, cut])
        grad_hidden[:, :units] = dot(held_c[block], held_dn[...], ((1,), (1,)))
        lax.fori_loop(0, rows // ROW_BLOCK, lambda at, none: (middle(at), none)[1], 0)

        @pl.when(step >= 2)
        def _():
            for copy in stores(order_of_arrival(step - 2), slot):
                copy.wait()

        for cut in tiles(normed.shape[2]):
            stage[0, slot, :, cut] = dot(hidden[...], held_dn[:, cut]).astype(BF16)
            stage[1, slot, :, cut] = dot(grad_gu[...], held_gu[cut, :], ((1,), (1,))).astype(BF16)
        for copy in stores(block, slot):
            copy.start()
        for cut in tiles(normed.shape[2]):
            sum_gu[cut, :] += dot(normed[block, :, cut], grad_gu[...], ((0,), (0,)))
            sum_dn[:, cut] += dot(hidden[...], held_c[block, :, cut], ((0,), (0,)))
        return carry

    lax.fori_loop(0, PLANES, through, 0)
    held_gu[...] = sum_gu[...].astype(BF16)
    ends = [pltpu.make_async_copy(held_gu, out_gu, load.at[0])]
    ends[-1].start()
    held_dn[...] = sum_dn[...].astype(BF16)
    ends.append(pltpu.make_async_copy(held_dn, out_dn, load.at[1]))
    ends[-1].start()
    for step in (PLANES - 2, PLANES - 1):
        for copy in stores(order_of_arrival(step), step % 2):
            copy.wait()
    for copy in ends:
        copy.wait()
    gather.finish()


def back_kernel(
    part,
    resid,
    inverse,
    gain,
    cotangent,
    fed,
    low,
    grad,
    gain_sum,
    mixed,
    local,
    far,
    send,
    receive,
    total_fed,
    *rest,
):
    plane = lax.axis_index("z")
    mine, _ = halves(part.shape[2])
    one, two = 5 * PARTS, 15 * PARTS
    greet_column()
    in_turn(*scatters(part, rest[one:two], grad))
    scale = inverse[:, :1]
    values, above = resid[...], grad[...]
    gain_sum[...] = jnp.sum(above * values * scale, axis=0, keepdims=True)
    scaled = above * gain[...]
    local[...] = fold(scaled * values)
    (total,) = both_cores(local, far, send, receive)
    mean = total / part.shape[2]
    grad[...] = cotangent[...].astype(F32) + scale * scaled - values * scale**3 * mean
    low[plane, :, mine] = grad[...].astype(BF16)
    in_turn(*gathers(low, rest[:one]), *scatters(fed, rest[two:], total_fed))
    mixed[...] = (total_fed[...] + resid[...]).astype(BF16)


def greet_cross_and_partner():
    plane, place, core = here()
    places = lax.axis_size("p")
    barrier = pltpu.get_barrier_semaphore()
    signal(barrier, (plane, place, 1 - core))
    for step in range(1, places):
        signal(barrier, (plane, lax.rem(place + step, places), core))
    for step in range(1, PLANES):
        signal(barrier, (lax.rem(plane + step, PLANES), place, core))
    pl.semaphore_wait(barrier, places + PLANES - 1)


def last_kernel(
    part,
    tokens,
    gain,
    resid_grad,
    parts_out,
    parts_qkv,
    grad,
    gain_sum,
    sum_out,
    spread,
    local,
    far,
    send,
    receive,
    came_out,
    came_qkv,
    blocks,
    stay,
    out_s,
    out_r,
    qkv_s,
    qkv_r,
    turn_s,
    turn_r,
    *rest,
):
    plane, place, core = here()
    places = lax.axis_size("p")
    greet_cross_and_partner()
    copies = []
    for step in range(1, places):
        to = lax.rem(place + step, places)
        device = (plane, to, core)
        copies.append(
            remote(
                parts_qkv.at[:, to], came_qkv.at[place], qkv_s.at[step], qkv_r.at[step], device
            )
        )
        copies.append(
            remote(parts_out.at[to], came_out.at[place], out_s.at[step], out_r.at[step], device)
        )
    copies.append(pltpu.make_async_copy(parts_qkv.at[:, place], came_qkv.at[place], stay.at[0]))
    copies.append(pltpu.make_async_copy(parts_out.at[place], came_out.at[place], stay.at[1]))
    for copy in copies:
        copy.start()
    moves = []

    def plane_sums():
        yield
        yield
        for copy in copies:
            copy.wait()
        blocks[...] = sum(came_qkv[other].astype(F32) for other in range(places)).astype(BF16)
        moves.extend(turn_copies(blocks, spread, turn_s, turn_r))
        moves.append(pltpu.make_async_copy(blocks.at[plane], spread.at[plane], stay.at[2]))
        for copy in moves:
            copy.start()
        yield
        sum_out[...] = sum(came_out[other].astype(F32) for other in range(places))

    in_turn(*scatters(part, rest, grad), plane_sums())
    values, above = tokens[...].astype(F32), grad[...]
    scaled = above * gain[...]
    local[:, :LANES] = fold(scaled * values)
    local[:, LANES:] = fold(values * values)
    total, square = both_cores(local, far, send, receive)
    scale = lax.rsqrt(square / part.shape[2] + EPSILON)
    gain_sum[...] = jnp.sum(above * values * scale, axis=0, keepdims=True)
    mean = total / part.shape[2]
    grad[...] = resid_grad[...] + scale * scaled - values * scale**3 * mean
    for copy in moves:
        copy.wait()


def owner_kernel(sums, out, came, send, receive):
    plane, place, core = here()
    places = lax.axis_size("p")
    count = PLANES * places
    near = count // 2
    index = plane * places + place
    side = lax.div(index, near)
    barrier = pltpu.get_barrier_semaphore()
    for step in range(count):
        pl.when((step > 0) | (side != core))(lambda: signal(barrier, peer(step) + (side,)))
    pl.semaphore_wait(barrier, count - (side == core).astype(jnp.int32))
    width = sums.shape[1] // near

    def copy(step, target):
        at = step * width // LANES * LANES
        owner = core * near + step
        device = (lax.div(owner, places), lax.rem(owner, places), target)
        return remote(
            sums.at[:, pl.ds(at, LANES)],
            came.at[index],
            send.at[2 * step + target],
            receive.at[index],
            device,
        )

    def to_self(step, target):
        return (core * near + step == index) & (core == target)

    for step in range(near):
        for target in range(2):
            local = to_self(step, target)
            pl.when(jnp.logical_not(local))(lambda: copy(step, target).start())

            @pl.when(local)
            def _():
                at = step * width // LANES * LANES
                came[index] = sums[:, at : at + LANES]

    for step in range(count):
        source = lax.rem(index + step, count)

        @pl.when((step > 0) | (side != core))
        def _():
            remote(
                came.at[source], came.at[source], send.at[0], receive.at[source], (plane, place, 1 - core)
            ).wait_recv()

    out[...] = sum(came[step] for step in range(count))
    for step in range(near):
        for target in range(2):
            local = to_self(step, target)
            pl.when(jnp.logical_not(local))(lambda: copy(step, target).wait_send())


def call(kernel, identity, micros, outs, scratch, args, far_args=(), far_outs=()):
    def spec(far):
        return pl.BlockSpec(memory_space=pl.ANY if far else pltpu.VMEM)

    return pl.pallas_call(
        kernel,
        out_shape=outs,
        in_specs=[spec(at in far_args) for at in range(len(args))],
        out_specs=[spec(at in far_outs) for at in range(len(outs))],
        scratch_shapes=scratch,
        cost_estimate=pl.CostEstimate(
            flops=micros * 10**9, bytes_accessed=micros * 10**6, transcendentals=0
        ),
        compiler_params=pltpu.CompilerParams(
            collective_id=identity, has_side_effects=True, vmem_limit_bytes=VMEM_LIMIT
        ),
    )(*args)


def shape(dims, dtype):
    return jax.ShapeDtypeStruct(dims, dtype)


def first(half, tile, blocks, identity):
    tokens, width = half.shape
    places = lax.axis_size("p")
    count = PLANES * places
    scratch = [
        pltpu.VMEM((PLANES, tokens, 2 * width), BF16),
        pltpu.VMEM(tile.shape, F32),
        pltpu.VMEM(tile.shape, F32),
        pltpu.VMEM((count,) + tile.shape, F32),
        pltpu.VMEM(blocks.shape, BF16),
    ]
    scratch += [DMA((3,)), DMA, DMA, DMA((PLANES,)), DMA((PLANES,)), DMA((count,)), DMA((count,))]
    scratch += [DMA((places,)), DMA((places,))]
    normed, qkv, gains, weights = call(
        first_kernel,
        identity,
        50,
        [
            shape((PLANES, tokens, 2 * width), BF16),
            shape((PLANES, tokens, blocks.shape[2]), BF16),
            shape((tile.shape[0], 2 * width), F32),
            shape((PLANES, places) + blocks.shape[1:], BF16),
        ],
        scratch + gather_scratch(),
        [half, tile, blocks],
    )
    return normed.reshape(-1, 2 * width), qkv.reshape(-1, blocks.shape[2]), gains, weights


def row_sems(rows):
    places = lax.axis_size("p")
    sems = [DMA((places,)), DMA((places,)), DMA, DMA((places,)), DMA((rows,)), DMA]
    return sems + [DMA((PLANES,)), DMA((PLANES,)), DMA]


def attend(qkv, live, blocks, rows, heads, identity):
    places = lax.axis_size("p")
    qkv = qkv.reshape(PLANES, rows, -1, qkv.shape[-1])
    positions, width = qkv.shape[2:]
    length = PLANES * places * positions
    wide = heads * HEAD_V
    return call(
        attend_kernel,
        identity,
        35,
        [
            shape((length, wide), F32),
            shape((length, wide), F32),
            shape((PLANES, rows, positions, wide), BF16),
            shape((PLANES, places, positions, width), BF16),
            shape(blocks.shape, BF16),
        ],
        [pltpu.VMEM((PLANES, places, positions, wide), BF16)] + row_sems(rows),
        [qkv, live, blocks],
    )


def attend_back(grad_att, seq, live, att, norms, blocks, rows, identity):
    grad_att = grad_att.reshape(PLANES, rows, -1, grad_att.shape[-1])
    positions = grad_att.shape[2]
    wide = grad_att.shape[-1]
    width = seq.shape[-1]
    return call(
        attend_back_kernel,
        identity,
        40,
        [shape((PLANES, rows, positions, width), BF16), shape(blocks.shape, BF16)],
        [
            pltpu.VMEM(seq.shape[:-1] + (wide,), BF16),
            pltpu.VMEM(seq.shape, BF16),
            pltpu.VMEM((att.shape[0], wide + LANES), F32),
        ]
        + row_sems(rows),
        [grad_att, seq, live, att, norms, blocks],
    )


def to_owners(sums, identity):
    count = PLANES * lax.axis_size("p")
    (out,) = call(
        owner_kernel,
        identity,
        8,
        [shape((sums.shape[0], LANES), F32)],
        [pltpu.VMEM((count, sums.shape[0], LANES), F32), DMA((count,)), DMA((count,))],
        [sums],
    )
    return out


def sums_scratch(tokens, count):
    return [pltpu.VMEM((tokens, count * LANES), F32) for _ in range(2)] + [DMA, DMA]


def mix(part, values, gain, other, identity):
    tokens, half = values.shape
    return call(
        mix_kernel,
        identity,
        58,
        [
            shape((tokens, half), BF16),
            shape((tokens, half), F32),
            shape((tokens, LANES), F32),
            shape((PLANES, tokens, 2 * half), BF16),
        ],
        sums_scratch(tokens, 1)
        + [DMA]
        + gather_scratch() * PARTS
        + scatter_scratch(tokens // PARTS, half) * PARTS,
        [part.reshape(PLANES, tokens, 2 * half), values, gain, other],
    )


def feed(own, w_gu, w_dn, grads, identity):
    tokens, half = own.shape
    units, width = w_dn.shape
    whole = (PLANES, tokens, width)
    return call(
        feed_kernel,
        identity,
        55,
        [shape(whole, BF16), shape(whole, BF16), shape(w_gu.shape, BF16), shape(w_dn.shape, BF16)],
        [
            pltpu.VMEM(whole, BF16),
            pltpu.VMEM(w_gu.shape, BF16),
            pltpu.VMEM(w_dn.shape, BF16),
            pltpu.VMEM(whole, BF16),
            pltpu.VMEM(w_gu.shape, F32),
            pltpu.VMEM(w_dn.shape, F32),
            pltpu.VMEM((tokens, 2 * units), F32),
            pltpu.VMEM((tokens, -(-units // LANES) * LANES), F32),
            pltpu.VMEM((tokens, units), BF16),
            pltpu.VMEM((tokens, 2 * units), BF16),
            pltpu.VMEM((2, 2, tokens, width), BF16),
            DMA((3,)),
            DMA,
            DMA((2, 2)),
        ]
        + gather_scratch(),
        [own, w_gu, w_dn, grads],
        (1, 2, 3),
        (0, 1, 2, 3),
    )


def mix_back(part, resid, inverse, gain, cotangent, fed, identity):
    tokens, half = resid.shape
    low, grad, gain_sum, mixed = call(
        back_kernel,
        identity,
        95,
        [
            shape((PLANES, tokens, 2 * half), BF16),
            shape((tokens, half), F32),
            shape((1, half), F32),
            shape((tokens, half), BF16),
        ],
        sums_scratch(tokens, 1)
        + [pltpu.VMEM((tokens, half), F32)]
        + gather_scratch() * PARTS
        + scatter_scratch(tokens // PARTS, half) * 2 * PARTS,
        [part, resid, inverse, gain, cotangent, fed],
    )
    return low.reshape(-1, 2 * half), grad, gain_sum, mixed


def last_back(part, tokens, gain, resid_grad, parts_out, parts_qkv, identity):
    count, half = tokens.shape
    places = lax.axis_size("p")
    blocks = (PLANES,) + parts_qkv.shape[2:]
    return call(
        last_kernel,
        identity,
        55,
        [
            shape((count, half), F32),
            shape((1, half), F32),
            shape(parts_out.shape[1:], F32),
            shape(blocks, BF16),
        ],
        sums_scratch(count, 2)
        + [
            pltpu.VMEM(parts_out.shape, BF16),
            pltpu.VMEM((places,) + blocks, BF16),
            pltpu.VMEM(blocks, BF16),
            DMA((3,)),
        ]
        + [DMA((places,)) for _ in range(4)]
        + [DMA((PLANES,)) for _ in range(2)]
        + scatter_scratch(count // PARTS, half) * PARTS,
        [part.reshape(PLANES, count, 2 * half), tokens, gain, resid_grad, parts_out, parts_qkv],
    )


def dot(left, right, dims=((1,), (0,))):
    return lax.dot_general(left, right, (dims, ((), ())), preferred_element_type=F32)


def join_units(gate, up):
    broad = gate.shape[-1] // LANES * LANES
    return jnp.concatenate(
        [gate[..., :broad], up[..., :broad], gate[..., broad:], up[..., broad:]], axis=-1
    )


def split_units(joined, units):
    broad = units // LANES * LANES
    rest = 2 * broad + units - broad
    return (
        jnp.concatenate([joined[..., :broad], joined[..., 2 * broad : rest]], axis=-1),
        jnp.concatenate([joined[..., broad : 2 * broad], joined[..., rest:]], axis=-1),
    )


def plane_sum(grad, own_rows):
    places = lax.axis_size("p")
    grad = grad.reshape(PLANES, places, own_rows, grad.shape[-1])
    return lax.psum_scatter(jnp.swapaxes(grad, 0, 1), "p", scatter_dimension=0, tiled=False)


def pad_units(weights, axis, chunk, padded):
    shape = weights.shape
    weights = weights.reshape(shape[:axis] + (-1, chunk) + shape[axis + 1 :])
    pads = [(0, 0)] * weights.ndim
    pads[axis + 1] = (0, padded - chunk)
    return jnp.pad(weights, pads).reshape(shape[:axis] + (-1,) + shape[axis + 1 :])


def on_device(
    tokens,
    lengths,
    attn_gain,
    w_query,
    w_key,
    w_value,
    w_output,
    ffn_gain,
    w_gate,
    w_up,
    w_down,
    cotangent,
):
    plane, place, core = (lax.axis_index(name) for name in ("z", "p", "core"))
    count = lax.axis_size("p")
    batches, per_batch, own_len, half = tokens.shape
    rows = batches * per_batch
    own_rows = w_query.shape[0]
    heads = w_query.shape[1] // FEAT // PLANES
    chunk = w_down.shape[0]
    padded = -(-chunk // 16) * 16
    units = count * padded
    slim, broad = heads * FEAT, heads * HEAD_V

    own_gain = attn_gain.shape[0]
    index = plane * count + place
    tile = jnp.stack([attn_gain, ffn_gain]).astype(F32)
    tile = jnp.pad(tile, ((0, 6), (0, LANES - own_gain)))
    tile = jnp.roll(tile, lax.rem((2 * index + core) * own_gain, LANES), axis=1)
    x_half = tokens.reshape(rows * own_len, half)
    c_half = cotangent.reshape(rows * own_len, half)
    qkv_blocks = jnp.concatenate(
        [
            w_value.reshape(own_rows, PLANES, broad),
            w_query.reshape(own_rows, PLANES, slim),
            w_key.reshape(own_rows, PLANES, slim),
        ],
        axis=2,
    )
    normed_one, qkv, gains, w_qkv = first(x_half, tile, jnp.swapaxes(qkv_blocks, 0, 1), 0)
    half_one = lax.dynamic_slice_in_dim(gains[0], core * half, half)
    half_two = lax.dynamic_slice_in_dim(gains[1], core * half, half)
    gu_blocks = jnp.swapaxes(
        join_units(
            pad_units(w_gate, 1, chunk, padded).reshape(own_rows, PLANES, units),
            pad_units(w_up, 1, chunk, padded).reshape(own_rows, PLANES, units),
        ),
        0,
        1,
    )
    w_out = lax.all_gather(w_output, "p", axis=0, tiled=True)
    w_dn = lax.all_gather(pad_units(w_down, 0, chunk, padded), "p", axis=0, tiled=True)

    length = PLANES * count * own_len
    limit = lax.dynamic_index_in_dim(lengths.reshape(-1), place // (count // rows))
    live = (jnp.arange(length) < limit).astype(F32)
    live = jnp.broadcast_to(live[:, None], (length, LANES))
    att, norms, attended, seq, w_gu = attend(qkv, live, gu_blocks, rows, heads, 2)
    attended = attended.reshape(-1, broad)
    w_gu = lax.all_gather(w_gu, "p", axis=1, tiled=False).reshape(-1, 2 * units)

    normed_two, resid, inv_two, c_all = mix(
        dot(attended, w_out).astype(BF16), x_half, half_two[None], c_half, 3
    )
    part, fed, out_gu, out_down = feed(normed_two, w_gu, w_dn, c_all, 1)
    out_gu = plane_sum(out_gu, own_rows)
    out_down = lax.psum_scatter(out_down, "p", scatter_dimension=0, tiled=True)
    grad_mix, grad_resid, gain_sum_two, mixed = mix_back(
        part, resid, inv_two, half_two[None], c_half, fed, 4
    )

    grad_att = dot(grad_mix, w_out, ((1,), (1,))).astype(BF16)
    grad_qkv, out_gu = attend_back(grad_att, seq, live, att, norms, out_gu, rows, 5)
    grad_qkv = grad_qkv.reshape(-1, 2 * slim + broad)
    out_gu = jnp.swapaxes(out_gu, 0, 1).astype(F32)
    part = dot(grad_qkv, w_qkv.reshape(2 * half, -1), ((1,), (1,))).astype(BF16)
    turned = ((0,), (0,))
    out_qkv = dot(normed_one, grad_qkv, turned).astype(BF16)
    out_output = dot(attended, grad_mix, turned).astype(BF16)
    grad_tokens, gain_sum_one, out_output, out_qkv = last_back(
        part,
        x_half,
        half_one[None],
        grad_resid,
        out_output.reshape(count, -1, 2 * half),
        out_qkv.reshape(PLANES, count, own_rows, -1),
        6,
    )
    out_qkv = jnp.swapaxes(out_qkv, 0, 1).astype(F32)

    gain_parts = jnp.concatenate([gain_sum_one, gain_sum_two, jnp.zeros((6, half), F32)], axis=0)
    at = (index * 2 + core) * own_gain
    out_gains = lax.dynamic_slice_in_dim(
        to_owners(gain_parts, 7), lax.rem(at, LANES), own_gain, axis=1
    )

    out_gate, out_up = split_units(out_gu, units)

    def unpad(part):
        part = part.reshape(own_rows, PLANES * count, padded)[..., :chunk]
        return part.reshape(own_rows, -1)

    return (
        mixed.reshape(tokens.shape),
        grad_tokens.reshape(tokens.shape),
        out_gains[0],
        out_qkv[..., broad : broad + slim].reshape(own_rows, -1),
        out_qkv[..., broad + slim :].reshape(own_rows, -1),
        out_qkv[..., :broad].reshape(own_rows, -1),
        out_output,
        out_gains[1],
        unpad(out_gate),
        unpad(out_up),
        out_down[:chunk].astype(F32),
    )


def solution(mesh):
    split = Mesh(mesh.devices.reshape(PLANES, -1, 2), ("z", "p", "core"))
    seq = ("z", "p")
    both = ("z", "p", "core")
    rows, columns = P(seq, "core"), P(("core", "z", "p"), None)
    tokens = P(None, None, seq, "core")
    return jax.shard_map(
        on_device,
        mesh=split,
        in_specs=(
            tokens,
            P(),
            P(both),
            rows,
            rows,
            rows,
            columns,
            P(both),
            rows,
            rows,
            columns,
            tokens,
        ),
        out_specs=(
            tokens,
            tokens,
            P(both),
            rows,
            rows,
            rows,
            columns,
            P(both),
            rows,
            rows,
            columns,
        ),
        check_vma=False,
    )
```

```python
import jax
import jax.numpy as jnp
from jax import lax
from jax.experimental import pallas as pl
from jax.experimental.pallas import tpu as pltpu
from jax.sharding import Mesh
from jax.sharding import PartitionSpec as P

FEAT = 16
HEAD_V = 128
PLANES = 4
LANES = 128
EPSILON = 1e-05
F32 = jnp.float32
BF16 = jnp.bfloat16
MESH = pl.DeviceIdType.MESH
DMA = pltpu.SemaphoreType.DMA
VMEM_LIMIT = 56 << 20
QUERY_BLOCK = 256
PARTS = 2
TILE = 256
ROW_BLOCK = 32


def remote(source, target, send, receive, device):
    return pltpu.make_async_remote_copy(
        src_ref=source,
        dst_ref=target,
        send_sem=send,
        recv_sem=receive,
        device_id=device,
        device_id_type=MESH,
    )


def here():
    return tuple(lax.axis_index(name) for name in ("z", "p", "core"))


def signal(semaphore, device):
    pl.semaphore_signal(semaphore, inc=1, device_id=device, device_id_type=MESH)


def greet_column():
    plane, place, core = here()
    barrier = pltpu.get_barrier_semaphore()
    signal(barrier, (plane, place, 1 - core))
    pl.when(plane > 0)(lambda: signal(barrier, (plane - 1, place, core)))
    pl.when(plane < PLANES - 1)(lambda: signal(barrier, (plane + 1, place, core)))
    inner = (plane > 0).astype(jnp.int32) + (plane < PLANES - 1).astype(jnp.int32)
    return lambda: pl.semaphore_wait(barrier, 1 + inner)


def greet_same():
    plane, place, core = here()
    places = lax.axis_size("p")
    barrier = pltpu.get_barrier_semaphore()
    signal(barrier, (plane, place, 1 - core))
    for step in range(1, PLANES * places):
        signal(barrier, peer(step) + (core,))
    return lambda: pl.semaphore_wait(barrier, PLANES * places)


def greet_all():
    plane, place, core = here()
    count = PLANES * lax.axis_size("p")
    barrier = pltpu.get_barrier_semaphore()
    signal(barrier, (plane, place, 1 - core))
    for step in range(1, count):
        signal(barrier, peer(step) + (core,))
        signal(barrier, peer(step) + (1 - core,))
    return lambda: pl.semaphore_wait(barrier, 2 * count - 1)


def greet_cross():
    plane, place, core = here()
    places = lax.axis_size("p")
    barrier = pltpu.get_barrier_semaphore()
    for step in range(1, places):
        signal(barrier, (plane, lax.rem(place + step, places), core))
    for step in range(1, PLANES):
        signal(barrier, (lax.rem(plane + step, PLANES), place, core))
    return lambda: pl.semaphore_wait(barrier, places + PLANES - 2)


def peer(step):
    plane, place, _ = here()
    places = lax.axis_size("p")
    index = lax.rem(plane * places + place + step, PLANES * places)
    return lax.div(index, places), lax.rem(index, places)


def halves(width):
    core = lax.axis_index("core")
    half = width // 2
    return (
        pl.ds(pl.multiple_of(core * half, LANES), half),
        pl.ds(pl.multiple_of((1 - core) * half, LANES), half),
    )


def in_turn(*steps):
    steps = list(steps)
    while steps:
        steps = [one for one in steps if next(one, steps) is not steps]


def gather_scratch():
    return [DMA((PLANES,)) for _ in range(5)]


class Gather:
    def __init__(self, out, sems):
        self.out = out
        self.arrive, self.across, self.up, self.down, self.over = sems
        self.plane, self.place, self.core = here()
        self.mine, self.other = halves(out.shape[2])

    def send(self, block, sems, receive, device):
        piece = self.out.at[block, :, self.mine]
        return remote(piece, piece, sems.at[block], receive.at[block], device)

    def rise(self, block):
        return self.send(block, self.up, self.arrive, (self.plane + 1, self.place, self.core))

    def fall(self, block):
        return self.send(block, self.down, self.arrive, (self.plane - 1, self.place, self.core))

    def cross(self, block):
        return self.send(block, self.over, self.across, (self.plane, self.place, 1 - self.core))

    def start(self):
        plane = self.plane
        pl.when(plane < PLANES - 1)(lambda: self.rise(plane).start())
        pl.when(plane > 0)(lambda: self.fall(plane).start())
        self.cross(plane).start()

    def landed(self, block):
        partner = (self.plane, self.place, 1 - self.core)
        self.send(block, self.over, self.arrive, partner).wait_recv()

    def pass_on(self, far):
        plane = self.plane

        @pl.when(plane >= far)
        def _():
            self.landed(plane - far)
            pl.when(plane < PLANES - 1)(lambda: self.rise(plane - far).start())
            self.cross(plane - far).start()

        @pl.when(plane + far < PLANES)
        def _():
            self.landed(plane + far)
            pl.when(plane > 0)(lambda: self.fall(plane + far).start())
            self.cross(plane + far).start()

    def whole(self, block):
        piece = self.out.at[block, :, self.other]
        partner = (self.plane, self.place, 1 - self.core)
        remote(piece, piece, self.over.at[block], self.across.at[block], partner).wait_recv()

    def finish(self):
        plane = self.plane
        for block in range(PLANES):
            self.cross(block).wait_send()
            pl.when((plane < PLANES - 1) & (block <= plane))(lambda: self.rise(block).wait_send())
            pl.when((plane > 0) & (block >= plane))(lambda: self.fall(block).wait_send())

    def steps(self):
        self.start()
        yield
        for far in range(1, PLANES):
            self.pass_on(far)
            yield
        for block in range(PLANES):
            self.whole(block)
        self.finish()


def order_of_arrival(step):
    plane = lax.axis_index("z")
    nearest = [sorted(range(PLANES), key=lambda block: (abs(block - own), block)) for own in range(PLANES)]
    found = jnp.int32(0)
    for own in range(PLANES):
        for at in range(PLANES):
            found = jnp.where((plane == own) & (step == at), nearest[own][at], found)
    return found


def scatter_buffers(tokens, half):
    return [
        pltpu.VMEM((PLANES, tokens, half), BF16),
        pltpu.VMEM((PLANES + 1, tokens, half), BF16),
    ]


def scatter_sems():
    return [DMA((PLANES,)) for _ in range(6)]


def scatter_scratch(tokens, half):
    return scatter_buffers(tokens, half) + scatter_sems()


def column_scatter(part, scratch, total):
    twin, came, over_s, over_r, up_s, up_r, down_s, down_r = scratch
    plane, place, core = here()
    mine, other = halves(part.shape[2])

    def cross(block):
        return remote(
            part.at[block, :, other],
            twin.at[block],
            over_s.at[block],
            over_r.at[block],
            (plane, place, 1 - core),
        )

    def rise(block):
        return remote(
            came.at[block], came.at[block], up_s.at[block], up_r.at[block], (plane + 1, place, core)
        )

    def fall(block):
        last = jnp.where(block == plane - 1, PLANES, block)
        return remote(
            came.at[block], came.at[last], down_s.at[block], down_r.at[block], (plane - 1, place, core)
        )

    def own(block):
        return part[block, :, mine].astype(F32) + twin[block].astype(F32)

    def pass_on(block, link, first):
        cross(block).wait_recv()

        @pl.when(jnp.logical_not(first))
        def _():
            link(block).wait_recv()
            came[block] = (own(block) + came[block].astype(F32)).astype(BF16)

        @pl.when(first)
        def _():
            came[block] = own(block).astype(BF16)

        link(block).start()

    for far in range(PLANES - 1, 0, -1):
        pl.when(plane + far < PLANES)(lambda: cross(plane + far).start())
        pl.when(plane >= far)(lambda: cross(plane - far).start())
    cross(plane).start()
    yield
    for far in range(PLANES - 1, 0, -1):
        pl.when(plane + far < PLANES)(lambda: pass_on(plane + far, rise, plane == 0))
        pl.when(plane >= far)(lambda: pass_on(plane - far, fall, plane == PLANES - 1))
        yield
    cross(plane).wait_recv()
    total[...] = own(plane)

    @pl.when(plane > 0)
    def _():
        rise(plane).wait_recv()
        total[...] += came[plane].astype(F32)

    @pl.when(plane < PLANES - 1)
    def _():
        fall(plane).wait_recv()
        total[...] += came[PLANES].astype(F32)

    for block in range(PLANES):
        cross(block).wait_send()
        pl.when(block > plane)(lambda: rise(block).wait_send())
        pl.when(block < plane)(lambda: fall(block).wait_send())


def gathers(out, scratch):
    size = out.shape[1] // PARTS
    return [
        Gather(out.at[:, pl.ds(at * size, size)], scratch[5 * at : 5 * at + 5]).steps()
        for at in range(PARTS)
    ]


def scatters(part, scratch, total):
    size = part.shape[1] // PARTS
    return [
        column_scatter(
            part.at[:, pl.ds(at * size, size)],
            scratch[8 * at : 8 * at + 8],
            total.at[pl.ds(at * size, size)],
        )
        for at in range(PARTS)
    ]


def fold(values):
    return sum(values[:, at : at + LANES] for at in range(0, values.shape[1], LANES))


def both_cores(local, far, send, receive):
    plane, place, core = here()
    copy = remote(local, far, send, receive, (plane, place, 1 - core))
    copy.start()
    copy.wait()
    joined = local[...] + far[...]
    return [
        jnp.sum(joined[:, at : at + LANES], axis=1, keepdims=True)
        for at in range(0, joined.shape[1], LANES)
    ]


def turn_copies(blocks, spread, send, receive):
    plane, place, core = here()
    copies = []
    for step in range(1, PLANES):
        to = lax.rem(plane + step, PLANES)
        copies.append(
            remote(blocks.at[to], spread.at[plane], send.at[step], receive.at[step], (to, place, core))
        )
    return copies


def pack_units(weights, places, plane, padded):
    size = weights.shape[0] // PLANES
    chunk = size // places
    turned = weights[pl.ds(pl.multiple_of(plane * size, 16), size), :].astype(F32).T
    blank = jnp.zeros((turned.shape[0], padded - chunk), F32)
    pieces = []
    for place in range(places):
        pieces += [turned[:, place * chunk : (place + 1) * chunk], blank]
    return jnp.concatenate(pieces, axis=1)


def unpack_units(weights, places, padded, chunk):
    pieces = [weights[:, place * padded : place * padded + chunk] for place in range(places)]
    return jnp.concatenate(pieces, axis=1).T


def front_kernel(
    own,
    other,
    gain_one,
    gain_two,
    w_query,
    w_key,
    w_value,
    w_gate,
    w_up,
    w_output,
    lens,
    normed_one,
    weights,
    gains,
    att,
    norms,
    attended,
    seq,
    w_gu,
    w_out,
    normed,
    resid,
    inverse,
    whole_c,
    whole,
    normed_in,
    qkv,
    blocks,
    spread,
    tile,
    pair,
    twin,
    tiles,
    joined,
    turned,
    low,
    part,
    local,
    far_sums,
    sum_s,
    sum_r,
    stay,
    swap_s,
    swap_r,
    turn_s,
    turn_r,
    gain_s,
    gain_r,
    spread_s,
    spread_r,
    out_s,
    out_r,
    row_s,
    row_r,
    row_l,
    back_s,
    back_r,
    back_l,
    gu_s,
    gu_r,
    gu_l,
    pass_s,
    pass_r,
    pass_l,
    keep_n,
    *rest,
):
    plane, place, core = here()
    places = lax.axis_size("p")
    count = PLANES * places
    index = plane * places + place
    width = whole.shape[2]
    mine, _ = halves(width)
    rows = attended.shape[1]
    per_row = places // rows
    gather = Gather(whole, rest[:5])
    greeted = greet_same()

    keep = pltpu.make_async_copy(own, whole.at[plane, :, mine], stay.at[0])
    keep.start()
    keep_c = pltpu.make_async_copy(other, whole_c.at[plane, :, mine], stay.at[1])
    keep_c.start()
    own_gain = gain_one.shape[1]
    tile[...] = jnp.zeros_like(tile)
    tile[0:1, :own_gain] = gain_one[...].astype(F32)
    tile[1:2, :own_gain] = gain_two[...].astype(F32)
    tile[...] = pltpu.roll(tile[...], lax.rem((2 * index + core) * own_gain, LANES), 1)
    wide = w_value.shape[1] // PLANES
    slim = w_query.shape[1] // PLANES
    for to in range(PLANES):
        pieces = [
            w_value[:, to * wide : (to + 1) * wide],
            w_query[:, to * slim : (to + 1) * slim],
            w_key[:, to * slim : (to + 1) * slim],
        ]
        joint = jnp.concatenate([piece.astype(F32) for piece in pieces], axis=1)
        blocks[to] = joint.astype(BF16)
    keep.wait()
    greeted()

    swap = remote(tile, twin, swap_s, swap_r, (plane, place, 1 - core))
    swap.start()
    turns = turn_copies(blocks, spread, turn_s, turn_r)
    for copy in turns:
        copy.start()
    gather.start()
    own_block = pltpu.make_async_copy(blocks.at[plane], spread.at[plane], stay.at[2])
    own_block.start()
    swap.wait()
    pair[...] = tile[...] + twin[...]
    tiles[index] = pair[...]
    sends = []
    for step in range(1, count):
        sends.append(
            remote(pair, tiles.at[index], gain_s.at[step], gain_r.at[step], peer(step) + (core,))
        )
        sends[-1].start()
    own_block.wait()
    for copy in turns:
        copy.wait()
    around = [
        pltpu.make_async_copy(spread, weights.at[:, place], stay.at[3]),
        pltpu.make_async_copy(w_output, w_out.at[place], stay.at[4]),
    ]
    for step in range(1, places):
        to = (plane, lax.rem(place + step, places), core)
        around.append(
            remote(spread, weights.at[:, place], spread_s.at[step], spread_r.at[step], to)
        )
        around.append(remote(w_output, w_out.at[place], out_s.at[step], out_r.at[step], to))
    for copy in around:
        copy.start()

    units = joined.shape[2] // 2
    padded = units // places
    broad = units // LANES * LANES

    def lay_out(to):
        gate = pack_units(w_gate, places, to, padded)
        up = pack_units(w_up, places, to, padded)
        joined[to, :, :broad] = gate[:, :broad].astype(BF16)
        joined[to, :, broad : 2 * broad] = up[:, :broad].astype(BF16)
        if units > broad:
            joined[to, :, 2 * broad :] = jnp.concatenate(
                [gate[:, broad:], up[:, broad:]], axis=1
            ).astype(BF16)

    def passed(step):
        block = lax.rem(plane - step + PLANES, PLANES)
        source = joined.at[plane] if step == 0 else turned.at[block]
        target = w_gu.at[block, place]
        copies = [pltpu.make_async_copy(source, target, pass_l.at[step])]
        for side in range(1, places):
            to = (plane, lax.rem(place + side, places), core)
            copies.append(
                remote(source, target, pass_s.at[step, side], pass_r.at[step, side], to)
            )
        return copies

    lay_out(plane)
    for copy in passed(0):
        copy.start()
    for step in range(1, PLANES):
        lay_out(lax.rem(plane + step, PLANES))

    gu_turns = turn_copies(joined, turned, gu_s, gu_r)

    def inward(step):
        to = lax.rem(plane + step, PLANES)
        return (jnp.abs(to - plane) == 1) & (to > 0) & (to < PLANES - 1)

    for step in range(1, PLANES):
        pl.when(inward(step))(gu_turns[step - 1].start)
    gather.pass_on(1)
    for copy in sends + around:
        copy.wait()
    each = width // count
    for at in range(0, width, LANES):
        group = range(at // each, (at + LANES) // each)
        gains[:, at : at + LANES] = sum(tiles[source] for source in group)
    gain = gains[0:1, :]

    def row_copy(block, step):
        to = lax.rem(place + step, places)
        return remote(
            qkv.at[block, lax.div(to, per_row)],
            seq.at[block, place],
            row_s.at[block, step],
            row_r.at[block, step],
            (plane, to, core),
        )

    def own_row(block):
        return pltpu.make_async_copy(
            qkv.at[block, lax.div(place, per_row)], seq.at[block, place], row_l.at[block]
        )

    def project(block):
        gather.whole(block)
        values = whole[block].astype(F32)
        scale = lax.rsqrt(jnp.mean(values * values, axis=1, keepdims=True) + EPSILON)
        normed_in[block] = (values * scale * gain).astype(BF16)
        pltpu.make_async_copy(normed_in.at[block], normed_one.at[block], keep_n.at[block]).start()
        flat_weights = weights[...].reshape(width, qkv.shape[3])
        qkv[block] = dot(normed_in[block], flat_weights).astype(BF16).reshape(qkv.shape[1:])
        for step in range(1, places):
            row_copy(block, step).start()
        own_row(block).start()

    project(order_of_arrival(0))
    for far in range(2, PLANES):
        gather.pass_on(far)
        project(order_of_arrival(far - 1))

    for step in range(1, PLANES):
        pl.when(jnp.logical_not(inward(step)))(gu_turns[step - 1].start)
    project(order_of_arrival(PLANES - 1))
    gather.finish()

    alive = alive_of(lens, att.shape[0], rows).astype(BF16)
    for block in range(PLANES):
        for step in range(1, places):
            row_copy(block, step).wait()
        own_row(block).wait()
    attend(seq, alive, att, norms)
    low[...] = att[...].astype(BF16).reshape(low.shape)
    finish = start_back(low, attended, back_s, back_r, back_l)
    finish()
    tokens = whole.shape[1]
    flat_out = w_out[...].reshape(-1, width)
    for block in range(PLANES):
        rows_in = attended[block].reshape(tokens, flat_out.shape[0])
        part[block] = dot(rows_in, flat_out).astype(BF16)

    def gu_flow():
        for step in range(1, PLANES):
            gu_turns[step - 1].wait()
            for copy in passed(step):
                copy.start()
            yield

    keep_c.wait()
    two = 5 + 5 * PARTS
    in_turn(*scatters(part, rest[two:], resid), *gathers(whole_c, rest[5:two]), gu_flow())
    resid[...] += own[...].astype(F32)
    local[...] = fold(resid[...] * resid[...])
    (total,) = both_cores(local, far_sums, sum_s, sum_r)
    scale = lax.rsqrt(total / width + EPSILON)
    inverse[...] = jnp.broadcast_to(scale, inverse.shape)
    normed[...] = (resid[...] * scale * gains[1:2, mine]).astype(BF16)
    for step in range(PLANES):
        for copy in passed(step):
            copy.wait()
        pltpu.make_async_copy(normed_in.at[step], normed_one.at[step], keep_n.at[step]).wait()


def to_rows(values, seq, send, receive, local):
    plane, place, core = here()
    places = lax.axis_size("p")
    per_row = places // values.shape[1]
    copies = []
    for step in range(1, places):
        to = lax.rem(place + step, places)
        row = lax.div(to, per_row)
        copies.append(
            remote(
                values.at[:, row], seq.at[:, place], send.at[step], receive.at[step], (plane, to, core)
            )
        )
    copies.append(
        pltpu.make_async_copy(values.at[:, lax.div(place, per_row)], seq.at[:, place], local)
    )
    return copies


def start_back(seq, out, send, receive, local):
    plane, place, core = here()
    places = lax.axis_size("p")
    rows = out.shape[1]
    per_row = places // rows
    row = lax.div(place, per_row)
    speaks = lax.rem(place, per_row) == 0

    def copy(step):
        to = lax.rem(place + step, places)
        return remote(
            seq.at[:, to], out.at[:, row], send.at[step], receive.at[row], (plane, to, core)
        )

    def stay():
        return pltpu.make_async_copy(seq.at[:, place], out.at[:, row], local)

    @pl.when(speaks)
    def _():
        for step in range(1, places):
            copy(step).start()
        stay().start()

    def finish():
        @pl.when(speaks)
        def _():
            stay().wait()
            for step in range(1, places):
                copy(step).wait_send()

        for other in range(rows):

            @pl.when(other * per_row != place)
            def _():
                remote(
                    out.at[:, other],
                    out.at[:, other],
                    send.at[0],
                    receive.at[other],
                    (plane, lax.rem(place + 1, places), core),
                ).wait_recv()

    return finish


def flat(ref):
    block = ref[...]
    return block.reshape(-1, block.shape[-1])


def columns_of(seq, heads, head):
    wide = heads * HEAD_V
    slim = seq[:, wide : wide + 2 * heads * FEAT].astype(F32)
    queries = slim[:, head * FEAT : (head + 1) * FEAT].astype(BF16)
    keys = slim[:, (heads + head) * FEAT : (heads + head + 1) * FEAT].astype(BF16)
    return queries, keys, seq[:, head * HEAD_V : (head + 1) * HEAD_V]


def causal(start, stop, values):
    queries = start + lax.broadcasted_iota(jnp.int32, values.shape, 0)
    keys = lax.broadcasted_iota(jnp.int32, values.shape, 1)
    return jnp.where(queries >= keys, values, 0.0)


def alive_of(lens, length, rows):
    row = lax.div(lax.axis_index("p"), lax.axis_size("p") // rows)
    positions = lax.broadcasted_iota(jnp.int32, (length, LANES), 0)
    return jnp.where(positions < lens[pl.ds(row, 1), :], 1.0, 0.0).astype(F32)


def attend(seq, alive, att, norms):
    everything = flat(seq)
    length = everything.shape[0]
    heads = att.shape[1] // HEAD_V
    block = min(QUERY_BLOCK, length)
    for head in range(heads):
        queries, keys, values = columns_of(everything, heads, head)
        values = jnp.concatenate([values * alive, alive], axis=1)
        wide = slice(head * HEAD_V, (head + 1) * HEAD_V)
        for start in range(0, length, block):
            stop = start + block
            scores = dot(queries[start:stop], keys[:stop], ((1,), (1,)))
            half = 1.0 + 0.25 * scores
            taylor = causal(start, stop, 0.5 + 0.5 * (half * half)).astype(BF16)
            sums = dot(taylor, values[:stop])
            norm = sums[:, HEAD_V:]
            ratio = sums[:, :HEAD_V] / norm
            att[start:stop, wide] = ratio
            norms[start:stop, wide] = norm


def attend_back_kernel(
    grad_mix,
    w_out,
    attended,
    seq,
    lens,
    att,
    norms,
    blocks,
    out,
    spread,
    out_output,
    grad_att,
    rows,
    low,
    keep,
    *sems,
):
    row_s, row_r, local, back_s, back_r, back_l, turn_s, turn_r, stay_s = sems
    plane = lax.axis_index("z")
    greeted = greet_cross()
    for block in range(PLANES):
        product = dot(grad_mix[block], w_out[...], ((1,), (1,))).astype(BF16)
        grad_att[block] = product.reshape(grad_att.shape[1:])
    greeted()
    copies = to_rows(grad_att, rows, row_s, row_r, local)
    for copy in copies:
        copy.start()
    turns = turn_copies(blocks, spread, turn_s, turn_r)
    turns.append(pltpu.make_async_copy(blocks.at[plane], spread.at[plane], stay_s))
    for copy in turns:
        copy.start()
    alive = alive_of(lens, att.shape[0], grad_att.shape[1])
    for at in range(0, grad_mix.shape[2], TILE):
        cut = slice(at, at + TILE)
        product = sum(
            dot(attended[block], grad_mix[block, :, cut], ((0,), (0,))) for block in range(PLANES)
        )
        out_output[:, :, cut] = product.astype(BF16).reshape(out_output.shape[:2] + (TILE,))
    for copy in copies:
        copy.wait()
    everything = flat(seq)
    length = everything.shape[0]
    heads = att.shape[1] // HEAD_V
    block = min(QUERY_BLOCK, length)
    grads = flat(rows).astype(F32)
    grad_q, grad_k = [], []
    for head in range(heads):
        queries, keys, values = columns_of(everything, heads, head)
        live_keys = (keys.astype(F32) * alive[:, :FEAT]).astype(BF16)
        wide = slice(head * HEAD_V, (head + 1) * HEAD_V)
        grad = grads[:, wide]
        norm = norms[:, wide]
        grad_num = (grad / norm).astype(BF16)
        grad_norm = -jnp.sum(grad * att[:, wide] / norm, axis=1, keepdims=True)
        parts = []
        for start in range(0, length, block):
            stop = start + block
            scores = dot(queries[start:stop], keys[:stop], ((1,), (1,)))
            half = 1.0 + 0.25 * scores
            taylor = causal(start, stop, 0.5 + 0.5 * (half * half)).astype(BF16)
            inner = dot(grad_num[start:stop], values[:stop], ((1,), (1,))) + grad_norm[start:stop]
            slope = causal(start, stop, half * inner).astype(BF16)
            parts.append(dot(slope, live_keys[:stop]) * 0.25)
            from_values = dot(taylor, grad_num[start:stop], ((0,), (0,)))
            from_keys = dot(slope, queries[start:stop], ((0,), (0,)))
            if start:
                keep[:start, wide] += from_values[:start]
                keep[:start, heads * HEAD_V + head * FEAT : heads * HEAD_V + (head + 1) * FEAT] += (
                    from_keys[:start]
                )
            keep[start:stop, wide] = from_values[start:]
            keep[start:stop, heads * HEAD_V + head * FEAT : heads * HEAD_V + (head + 1) * FEAT] = (
                from_keys[start:]
            )
        grad_q.append(jnp.concatenate(parts, axis=0))
        keep[:, wide] *= alive
    wide = heads * HEAD_V
    keys = keep[:, wide : wide + heads * FEAT] * (0.25 * alive[:, : heads * FEAT])
    result = jnp.concatenate([keep[:, :wide]] + grad_q + [keys], axis=1)
    low[...] = result.astype(BF16).reshape(low.shape)
    finish = start_back(low, out, back_s, back_r, back_l)
    for copy in turns:
        copy.wait()
    finish()


def feed_kernel(
    own,
    w_gu,
    w_dn,
    grads,
    part,
    fed,
    out_gu,
    out_dn,
    normed,
    held_gu,
    held_dn,
    held_c,
    sum_gu,
    sum_dn,
    gate_up,
    grad_hidden,
    hidden,
    grad_gu,
    stage,
    load,
    keep,
    store,
    ending,
    *sems,
):
    plane = lax.axis_index("z")
    mine, _ = halves(normed.shape[2])
    places = lax.axis_size("p")
    units = hidden.shape[1]
    broad = units // LANES * LANES
    rest = units - broad
    rows = normed.shape[1]
    loads = [
        pltpu.make_async_copy(w_gu, held_gu, load.at[0]),
        pltpu.make_async_copy(w_dn, held_dn, load.at[1]),
        pltpu.make_async_copy(grads, held_c, load.at[2]),
    ]
    for copy in loads:
        copy.start()
    gather = Gather(normed, sems)
    greeted = greet_column()
    stay = pltpu.make_async_copy(own, normed.at[plane, :, mine], keep)
    stay.start()
    stay.wait()
    greeted()
    gather.start()
    sum_gu[...] = jnp.zeros_like(sum_gu)
    sum_dn[...] = jnp.zeros_like(sum_dn)
    for copy in loads:
        copy.wait()

    def tiles(width):
        return [slice(at, min(at + TILE, width)) for at in range(0, width, TILE)]

    def stores(block, slot):
        return (
            pltpu.make_async_copy(stage.at[0, slot], fed.at[block], store.at[0, slot]),
            pltpu.make_async_copy(stage.at[1, slot], part.at[block], store.at[1, slot]),
        )

    def middle(at):
        here_rows = pl.ds(pl.multiple_of(at * ROW_BLOCK, ROW_BLOCK), ROW_BLOCK)

        def parts(gate, up, above):
            sigmoid = jax.nn.sigmoid(gate)
            silu = gate * sigmoid
            slope = sigmoid * (1.0 + gate * (1.0 - sigmoid))
            return silu * up, above * up * slope, above * silu

        both = gate_up[here_rows, :]
        above = grad_hidden[here_rows, :]
        first, second, third = parts(
            both[:, :broad], both[:, broad : 2 * broad], above[:, :broad]
        )
        hidden[here_rows, :broad] = first.astype(BF16)
        grad_gu[here_rows, :broad] = second.astype(BF16)
        grad_gu[here_rows, broad : 2 * broad] = third.astype(BF16)
        if rest:
            last = both[:, 2 * broad :]
            turned = pltpu.roll(last, rest, 1)
            first, second, third = parts(last, turned, above[:, broad : broad + LANES])
            hidden[here_rows, broad:] = first[:, :rest].astype(BF16)
            lane = lax.broadcasted_iota(jnp.int32, last.shape, 1)
            joined = jnp.where(lane < rest, second, pltpu.roll(third, rest, 1))
            grad_gu[here_rows, 2 * broad :] = joined.astype(BF16)

    def through(step, carry):
        pl.when(step > 0)(lambda: gather.pass_on(step))
        block = order_of_arrival(step)
        slot = lax.rem(step, 2)
        gather.whole(block)
        for cut in tiles(2 * units):
            gate_up[:, cut] = dot(normed[block], held_gu[:, cut])
        grad_hidden[:, :units] = dot(held_c[block], held_dn[...], ((1,), (1,)))
        lax.fori_loop(0, rows // ROW_BLOCK, lambda at, none: (middle(at), none)[1], 0)

        @pl.when(step >= 2)
        def _():
            for copy in stores(order_of_arrival(step - 2), slot):
                copy.wait()

        for cut in tiles(normed.shape[2]):
            stage[0, slot, :, cut] = dot(hidden[...], held_dn[:, cut]).astype(BF16)
            stage[1, slot, :, cut] = dot(grad_gu[...], held_gu[cut, :], ((1,), (1,))).astype(BF16)
        for copy in stores(block, slot):
            copy.start()
        for cut in tiles(normed.shape[2]):
            sum_gu[cut, :] += dot(normed[block, :, cut], grad_gu[...], ((0,), (0,)))
            sum_dn[:, cut] += dot(hidden[...], held_c[block, :, cut], ((0,), (0,)))
        return carry

    lax.fori_loop(0, PLANES, through, 0)
    own_rows = out_gu.shape[2]
    ends = []
    for block in range(normed.shape[2] // own_rows):
        cut = pl.ds(block * own_rows, own_rows)
        held_gu[cut, :] = sum_gu[cut, :].astype(BF16)
        ends.append(
            pltpu.make_async_copy(
                held_gu.at[cut], out_gu.at[block % places, block // places], ending.at[block]
            )
        )
        ends[-1].start()
    held_dn[...] = sum_dn[...].astype(BF16)
    ends.append(pltpu.make_async_copy(held_dn, out_dn, load.at[1]))
    ends[-1].start()
    for step in (PLANES - 2, PLANES - 1):
        for copy in stores(order_of_arrival(step), step % 2):
            copy.wait()
    for copy in ends:
        copy.wait()
    gather.finish()


def back_kernel(
    far_part,
    resid,
    inverse,
    gains,
    cotangent,
    far_fed,
    low,
    grad,
    gain_sum,
    mixed,
    part,
    fed,
    local,
    far,
    send,
    receive,
    load,
    total_fed,
    *rest,
):
    plane = lax.axis_index("z")
    mine, _ = halves(part.shape[2])
    one, two = 5 * PARTS, 13 * PARTS
    greeted = greet_column()
    copies = [
        pltpu.make_async_copy(far_part, part, load.at[0]),
        pltpu.make_async_copy(far_fed, fed, load.at[1]),
    ]
    for copy in copies:
        copy.start()
    copies[0].wait()
    greeted()
    in_turn(*scatters(part, rest[one:two], grad))
    copies[1].wait()
    scale = inverse[:, :1]
    values, above = resid[...], grad[...]
    scaled = above * gains[1:2, mine]
    local[...] = fold(scaled * values)
    (total,) = both_cores(local, far, send, receive)
    mean = total / part.shape[2]
    grad[...] = cotangent[...].astype(F32) + scale * scaled - values * scale**3 * mean
    low[plane, :, mine] = grad[...].astype(BF16)
    in_turn(
        *gathers(low, rest[:one]),
        *scatters(fed, rest[two:], total_fed),
        keep_sum(gain_sum, above * values * scale),
    )
    mixed[...] = (total_fed[...] + resid[...]).astype(BF16)


def keep_sum(gain_sum, values):
    yield
    gain_sum[...] = jnp.sum(values, axis=0, keepdims=True)


def last_kernel(
    grad_qkv,
    w_qkv,
    normed,
    tokens,
    gains,
    resid_grad,
    parts_out,
    joined,
    gain_two,
    grad,
    sum_out,
    grad_query,
    grad_key,
    grad_value,
    grad_gate,
    grad_up,
    out_gains,
    part,
    parts_qkv,
    sums,
    came_gains,
    local,
    far,
    send,
    receive,
    came_out,
    came_qkv,
    blocks,
    spread,
    stay,
    out_s,
    out_r,
    qkv_s,
    qkv_r,
    turn_s,
    turn_r,
    own_s,
    own_r,
    *rest,
):
    plane, place, core = here()
    places = lax.axis_size("p")
    mine, _ = halves(part.shape[2])
    own_rows = parts_qkv.shape[2]
    greeted = greet_all()
    flat_weights = w_qkv[...].reshape(part.shape[2], grad_qkv.shape[2])
    for block in range(PLANES):
        part[block] = dot(grad_qkv[block], flat_weights, ((1,), (1,))).astype(BF16)
    greeted()
    outs, shares, moves = [], [], []
    for step in range(1, places):
        to = lax.rem(place + step, places)
        device = (plane, to, core)
        outs.append(
            remote(parts_out.at[to], came_out.at[place], out_s.at[step], out_r.at[step], device)
        )
        shares.append(
            remote(
                parts_qkv.at[:, to], came_qkv.at[place], qkv_s.at[step], qkv_r.at[step], device
            )
        )
    outs.append(pltpu.make_async_copy(parts_out.at[place], came_out.at[place], stay.at[0]))
    shares.append(pltpu.make_async_copy(parts_qkv.at[:, place], came_qkv.at[place], stay.at[1]))

    def lay_out(grads, first):
        units = joined.shape[2] // 2
        broad = units // LANES * LANES
        rest = units - broad
        size = grads.shape[0] // PLANES
        for to in range(PLANES):
            piece = joined[to].astype(F32)
            low = 2 * broad + (0 if first else rest)
            start = 0 if first else broad
            pieces = [piece[:, start : start + broad]]
            if rest:
                pieces.append(piece[:, low : low + rest])
            found = jnp.concatenate(pieces, axis=1)
            grads[to * size : (to + 1) * size, :] = unpack_units(
                found, places, units // places, size // places
            )

    def others():
        for copy in outs:
            copy.start()
        yield
        tokens_all = PLANES * normed.shape[1]
        grads = grad_qkv[...].reshape(tokens_all, grad_qkv.shape[2])
        for at in range(0, part.shape[2], TILE):
            left = normed[:, :, at : at + TILE].reshape(tokens_all, TILE)
            product = dot(left, grads, ((0,), (0,))).astype(BF16)
            for row in range(0, TILE, own_rows):
                owner = (at + row) // own_rows
                parts_qkv[owner // places, owner % places] = product[row : row + own_rows]
            if at + TILE == part.shape[2] // 2:
                yield
        for copy in shares:
            copy.start()
        yield
        lay_out(grad_gate, True)
        yield
        for copy in outs:
            copy.wait()
        sum_out[...] = sum(came_out[other].astype(F32) for other in range(places))
        for copy in shares:
            copy.wait()
        blocks[...] = sum(came_qkv[other].astype(F32) for other in range(places)).astype(BF16)
        moves.extend(turn_copies(blocks, spread, turn_s, turn_r))
        moves.append(pltpu.make_async_copy(blocks.at[plane], spread.at[plane], stay.at[2]))
        for copy in moves:
            copy.start()
        yield
        lay_out(grad_up, False)

    in_turn(*scatters(part, rest, grad), others())
    values, above = tokens[...].astype(F32), grad[...]
    scaled = above * gains[0:1, mine]
    local[:, :LANES] = fold(scaled * values)
    local[:, LANES:] = fold(values * values)
    total, square = both_cores(local, far, send, receive)
    scale = lax.rsqrt(square / part.shape[2] + EPSILON)
    sums[...] = jnp.zeros_like(sums)
    sums[0:1, :] = jnp.sum(above * values * scale, axis=0, keepdims=True)
    sums[1:2, :] = gain_two[...]
    finish = to_owners(sums, came_gains, own_s, own_r)
    mean = total / part.shape[2]
    grad[...] = resid_grad[...] + scale * scaled - values * scale**3 * mean
    for copy in moves:
        copy.wait()
    wide = grad_value.shape[1] // PLANES
    slim = grad_query.shape[1] // PLANES
    found = [spread[to].astype(F32) for to in range(PLANES)]
    for to in range(PLANES):
        grad_value[:, to * wide : (to + 1) * wide] = found[to][:, :wide]
    grad_query[...] = jnp.concatenate([one[:, wide : wide + slim] for one in found], axis=1)
    grad_key[...] = jnp.concatenate([one[:, wide + slim :] for one in found], axis=1)
    finish(out_gains)


def to_owners(sums, came, send, receive):
    plane, place, core = here()
    places = lax.axis_size("p")
    count = PLANES * places
    near = count // 2
    index = plane * places + place
    side = lax.div(index, near)
    width = sums.shape[1] // near

    def copy(step, target):
        at = step * width // LANES * LANES
        owner = core * near + step
        device = (lax.div(owner, places), lax.rem(owner, places), target)
        return remote(
            sums.at[:, pl.ds(at, LANES)],
            came.at[index],
            send.at[2 * step + target],
            receive.at[index],
            device,
        )

    def to_self(step, target):
        return (core * near + step == index) & (core == target)

    for step in range(near):
        for target in range(2):
            local = to_self(step, target)
            pl.when(jnp.logical_not(local))(lambda: copy(step, target).start())

            @pl.when(local)
            def _():
                at = step * width // LANES * LANES
                came[index] = sums[:, at : at + LANES]

    def finish(out):
        for step in range(count):
            source = lax.rem(index + step, count)

            @pl.when((step > 0) | (side != core))
            def _():
                remote(
                    came.at[source],
                    came.at[source],
                    send.at[0],
                    receive.at[source],
                    (plane, place, 1 - core),
                ).wait_recv()

        out[...] = sum(came[step] for step in range(count))
        for step in range(near):
            for target in range(2):
                local = to_self(step, target)
                pl.when(jnp.logical_not(local))(lambda: copy(step, target).wait_send())

    return finish


def call(kernel, identity, micros, outs, scratch, args, far_args=(), far_outs=()):
    def spec(far):
        return pl.BlockSpec(memory_space=pl.ANY if far else pltpu.VMEM)

    return pl.pallas_call(
        kernel,
        out_shape=outs,
        in_specs=[spec(at in far_args) for at in range(len(args))],
        out_specs=[spec(at in far_outs) for at in range(len(outs))],
        scratch_shapes=scratch,
        cost_estimate=pl.CostEstimate(
            flops=micros * 10**9, bytes_accessed=micros * 10**6, transcendentals=0
        ),
        compiler_params=pltpu.CompilerParams(
            collective_id=identity, has_side_effects=True, vmem_limit_bytes=VMEM_LIMIT
        ),
    )(*args)


def shape(dims, dtype):
    return jax.ShapeDtypeStruct(dims, dtype)


def front(x_half, c_half, gain_one, gain_two, w_query, w_key, w_value, w_gate, w_up, w_output, lens, units, identity):
    tokens, half = x_half.shape
    places = lax.axis_size("p")
    count = PLANES * places
    rows = lens.shape[0]
    positions = tokens // rows
    length = PLANES * places * positions
    own_rows = w_query.shape[0]
    wide = w_value.shape[1] // PLANES
    width = wide + 2 * (w_query.shape[1] // PLANES)
    whole = (PLANES, tokens, 2 * half)
    blocks = (PLANES, own_rows, width)
    gu = (PLANES, own_rows, 2 * units)
    return call(
        front_kernel,
        identity,
        150,
        [
            shape(whole, BF16),
            shape((PLANES, places, own_rows, width), BF16),
            shape((8, 2 * half), F32),
            shape((length, wide), F32),
            shape((length, wide), F32),
            shape((PLANES, rows, positions, wide), BF16),
            shape((PLANES, places, positions, width), BF16),
            shape((PLANES, places, own_rows, 2 * units), BF16),
            shape((places,) + w_output.shape, BF16),
            shape((tokens, half), BF16),
            shape((tokens, half), F32),
            shape((tokens, LANES), F32),
            shape(whole, BF16),
        ],
        [
            pltpu.VMEM(whole, BF16),
            pltpu.VMEM(whole, BF16),
            pltpu.VMEM((PLANES, rows, positions, width), BF16),
            pltpu.VMEM(blocks, BF16),
            pltpu.VMEM(blocks, BF16),
            pltpu.VMEM((8, LANES), F32),
            pltpu.VMEM((8, LANES), F32),
            pltpu.VMEM((8, LANES), F32),
            pltpu.VMEM((count, 8, LANES), F32),
            pltpu.VMEM(gu, BF16),
            pltpu.VMEM(gu, BF16),
            pltpu.VMEM((PLANES, places, positions, wide), BF16),
            pltpu.VMEM(whole, BF16),
        ]
        + sums_scratch(tokens, 1)
        + [DMA((5,)), DMA, DMA]
        + [DMA((PLANES,)), DMA((PLANES,)), DMA((count,)), DMA((count,))]
        + [DMA((places,)) for _ in range(4)]
        + [DMA((PLANES, places)), DMA((PLANES, places)), DMA((PLANES,))]
        + [DMA((places,)), DMA((rows,)), DMA]
        + [DMA((PLANES,)), DMA((PLANES,)), DMA]
        + [DMA((PLANES, places)), DMA((PLANES, places)), DMA((PLANES,)), DMA((PLANES,))]
        + gather_scratch() * (1 + PARTS)
        + scatter_scratch(tokens // PARTS, half) * PARTS,
        [
            x_half,
            c_half,
            gain_one,
            gain_two,
            w_query,
            w_key,
            w_value,
            w_gate,
            w_up,
            w_output,
            lens,
        ],
        (1,),
        (0, 7, 12),
    )


def row_sems(rows):
    places = lax.axis_size("p")
    sems = [DMA((places,)), DMA((places,)), DMA, DMA((places,)), DMA((rows,)), DMA]
    return sems + [DMA((PLANES,)), DMA((PLANES,)), DMA]


def attend_back(grad_mix, w_out, attended, seq, lens, att, norms, blocks, rows, identity):
    places = lax.axis_size("p")
    positions = grad_mix.shape[1] // rows
    wide = w_out.shape[0]
    width = seq.shape[-1]
    return call(
        attend_back_kernel,
        identity,
        35,
        [
            shape((PLANES, rows, positions, width), BF16),
            shape(blocks.shape, BF16),
            shape((places, wide // places, grad_mix.shape[2]), BF16),
        ],
        [
            pltpu.VMEM((PLANES, rows, positions, wide), BF16),
            pltpu.VMEM(seq.shape[:-1] + (wide,), BF16),
            pltpu.VMEM(seq.shape, BF16),
            pltpu.VMEM((att.shape[0], wide + LANES), F32),
        ]
        + row_sems(rows),
        [grad_mix, w_out, attended, seq, lens, att, norms, blocks],
        (7,),
        (1,),
    )


def sums_scratch(tokens, count):
    return [pltpu.VMEM((tokens, count * LANES), F32) for _ in range(2)] + [DMA, DMA]


def feed(own, w_gu, w_dn, grads, identity):
    tokens, half = own.shape
    units, width = w_dn.shape
    places = lax.axis_size("p")
    whole = (PLANES, tokens, width)
    return call(
        feed_kernel,
        identity,
        55,
        [
            shape(whole, BF16),
            shape(whole, BF16),
            shape((places, PLANES, width // (PLANES * places), 2 * units), BF16),
            shape(w_dn.shape, BF16),
        ],
        [
            pltpu.VMEM(whole, BF16),
            pltpu.VMEM(w_gu.shape, BF16),
            pltpu.VMEM(w_dn.shape, BF16),
            pltpu.VMEM(whole, BF16),
            pltpu.VMEM(w_gu.shape, F32),
            pltpu.VMEM(w_dn.shape, F32),
            pltpu.VMEM((tokens, 2 * units), F32),
            pltpu.VMEM((tokens, -(-units // LANES) * LANES), F32),
            pltpu.VMEM((tokens, units), BF16),
            pltpu.VMEM((tokens, 2 * units), BF16),
            pltpu.VMEM((2, 2, tokens, width), BF16),
            DMA((3,)),
            DMA,
            DMA((2, 2)),
            DMA((PLANES * places,)),
        ]
        + gather_scratch(),
        [own, w_gu, w_dn, grads],
        (1, 2, 3),
        (0, 1, 2, 3),
    )


def mix_back(part, resid, inverse, gains, cotangent, fed, identity):
    tokens, half = resid.shape
    whole = (PLANES, tokens, 2 * half)
    return call(
        back_kernel,
        identity,
        95,
        [
            shape(whole, BF16),
            shape((tokens, half), F32),
            shape((1, half), F32),
            shape((tokens, half), BF16),
        ],
        [pltpu.VMEM(whole, BF16), pltpu.VMEM(whole, BF16)]
        + sums_scratch(tokens, 1)
        + [DMA((2,)), pltpu.VMEM((tokens, half), F32)]
        + gather_scratch() * PARTS
        + scatter_scratch(tokens // PARTS, half) * 2 * PARTS,
        [part, resid, inverse, gains, cotangent, fed],
        (0, 5),
    )


def last_back(grad_qkv, w_qkv, normed, tokens, gains, resid_grad, parts_out, joined, gain_two, units, identity):
    size, half = tokens.shape
    places = lax.axis_size("p")
    count = PLANES * places
    own_rows, width = w_qkv.shape[2:]
    slim = (width - parts_out.shape[0] * parts_out.shape[1]) // 2
    blocks = (PLANES, own_rows, width)
    outs = [
        (size, half),
        parts_out.shape[1:],
        (own_rows, PLANES * slim),
        (own_rows, PLANES * slim),
        (own_rows, PLANES * (width - 2 * slim)),
        (units, own_rows),
        (units, own_rows),
        (8, LANES),
    ]
    return call(
        last_kernel,
        identity,
        60,
        [shape(dims, F32) for dims in outs],
        [
            pltpu.VMEM((PLANES, size, 2 * half), BF16),
            pltpu.VMEM((PLANES, places, own_rows, width), BF16),
            pltpu.VMEM((8, half), F32),
            pltpu.VMEM((count, 8, LANES), F32),
        ]
        + sums_scratch(size, 2)
        + [
            pltpu.VMEM(parts_out.shape, BF16),
            pltpu.VMEM((places,) + blocks, BF16),
            pltpu.VMEM(blocks, BF16),
            pltpu.VMEM(blocks, BF16),
            DMA((3,)),
        ]
        + [DMA((places,)) for _ in range(4)]
        + [DMA((PLANES,)) for _ in range(2)]
        + [DMA((count,)) for _ in range(2)]
        + scatter_scratch(size // PARTS, half) * PARTS,
        [grad_qkv, w_qkv, normed, tokens, gains, resid_grad, parts_out, joined, gain_two],
    )


def dot(left, right, dims=((1,), (0,))):
    return lax.dot_general(left, right, (dims, ((), ())), preferred_element_type=F32)


def pad_units(weights, axis, chunk, padded):
    shape = weights.shape
    weights = weights.reshape(shape[:axis] + (-1, chunk) + shape[axis + 1 :])
    pads = [(0, 0)] * weights.ndim
    pads[axis + 1] = (0, padded - chunk)
    return jnp.pad(weights, pads).reshape(shape[:axis] + (-1,) + shape[axis + 1 :])


def on_device(
    tokens,
    lengths,
    attn_gain,
    w_query,
    w_key,
    w_value,
    w_output,
    ffn_gain,
    w_gate,
    w_up,
    w_down,
    cotangent,
):
    plane, place, core = (lax.axis_index(name) for name in ("z", "p", "core"))
    count = lax.axis_size("p")
    batches, per_batch, own_len, half = tokens.shape
    rows = batches * per_batch
    own_rows = w_query.shape[0]
    heads = w_query.shape[1] // FEAT // PLANES
    chunk = w_down.shape[0]
    padded = -(-chunk // 16) * 16
    units = count * padded
    slim, broad = heads * FEAT, heads * HEAD_V

    own_gain = attn_gain.shape[0]
    index = plane * count + place
    x_half = tokens.reshape(rows * own_len, half)
    c_half = cotangent.reshape(rows * own_len, half)
    lens = jnp.broadcast_to(lengths.reshape(-1)[:, None], (rows, LANES))
    w_dn = lax.all_gather(pad_units(w_down, 0, chunk, padded), "p", axis=0, tiled=True)
    (
        normed_one,
        w_qkv,
        gains,
        att,
        norms,
        attended,
        seq,
        w_gu,
        w_out,
        normed_two,
        resid,
        inv_two,
        c_all,
    ) = front(
        x_half,
        c_half,
        attn_gain[None],
        ffn_gain[None],
        w_query,
        w_key,
        w_value,
        w_gate.T,
        w_up.T,
        w_output,
        lens,
        units,
        0,
    )
    attended = attended.reshape(PLANES, -1, broad)
    w_gu = w_gu.reshape(-1, 2 * units)
    w_out = w_out.reshape(broad, -1)
    part, fed, out_gu, out_down = feed(normed_two, w_gu, w_dn, c_all, 1)
    out_gu = lax.psum_scatter(out_gu, "p", scatter_dimension=0, tiled=False)
    out_gu, out_down = lax.optimization_barrier((out_gu, out_down))
    out_down = lax.psum_scatter(out_down, "p", scatter_dimension=0, tiled=True)
    grad_mix, grad_resid, gain_two, mixed = mix_back(
        part, resid, inv_two, gains, c_half, fed, 4
    )
    grad_qkv, out_gu, out_output = attend_back(
        grad_mix, w_out, attended, seq, lens, att, norms, out_gu, rows, 5
    )
    grad_tokens, out_output, out_query, out_key, out_value, out_gate, out_up, out_gains = last_back(
        grad_qkv.reshape(PLANES, -1, 2 * slim + broad),
        w_qkv,
        normed_one,
        x_half,
        gains,
        grad_resid,
        out_output,
        out_gu,
        gain_two,
        w_gate.shape[1],
        6,
    )
    at = (index * 2 + core) * own_gain
    out_gains = lax.dynamic_slice_in_dim(out_gains, lax.rem(at, LANES), own_gain, axis=1)
    return (
        mixed.reshape(tokens.shape),
        grad_tokens.reshape(tokens.shape),
        out_gains[0],
        out_query,
        out_key,
        out_value,
        out_output,
        out_gains[1],
        out_gate.T,
        out_up.T,
        out_down[:chunk].astype(F32),
    )


def solution(mesh):
    split = Mesh(mesh.devices.reshape(PLANES, -1, 2), ("z", "p", "core"))
    seq = ("z", "p")
    both = ("z", "p", "core")
    rows, columns = P(seq, "core"), P(("core", "z", "p"), None)
    tokens = P(None, None, seq, "core")
    return jax.shard_map(
        on_device,
        mesh=split,
        in_specs=(
            tokens,
            P(),
            P(both),
            rows,
            rows,
            rows,
            columns,
            P(both),
            rows,
            rows,
            columns,
            tokens,
        ),
        out_specs=(
            tokens,
            tokens,
            P(both),
            rows,
            rows,
            rows,
            columns,
            P(both),
            rows,
            rows,
            columns,
        ),
        check_vma=False,
    )
```

```python
import jax
import jax.numpy as jnp
from jax import lax
from jax.experimental import pallas as pl
from jax.experimental.pallas import tpu as pltpu
from jax.sharding import Mesh
from jax.sharding import PartitionSpec as P

FEAT = 16
HEAD_V = 128
PLANES = 4
LANES = 128
EPSILON = 1e-05
F32 = jnp.float32
BF16 = jnp.bfloat16
MESH = pl.DeviceIdType.MESH
DMA = pltpu.SemaphoreType.DMA
VMEM_LIMIT = 60 << 20
QUERY_BLOCK = 256
MERGED_LENGTH = 1024
PARTS = 2
TILE = 256
ROW_BLOCK = 32


def remote(source, target, send, receive, device):
    return pltpu.make_async_remote_copy(
        src_ref=source,
        dst_ref=target,
        send_sem=send,
        recv_sem=receive,
        device_id=device,
        device_id_type=MESH,
    )


def here():
    return tuple(lax.axis_index(name) for name in ("z", "p", "core"))


def signal(semaphore, device):
    pl.semaphore_signal(semaphore, inc=1, device_id=device, device_id_type=MESH)


def greet_column():
    plane, place, core = here()
    barrier = pltpu.get_barrier_semaphore()
    signal(barrier, (plane, place, 1 - core))
    pl.when(plane > 0)(lambda: signal(barrier, (plane - 1, place, core)))
    pl.when(plane < PLANES - 1)(lambda: signal(barrier, (plane + 1, place, core)))
    inner = (plane > 0).astype(jnp.int32) + (plane < PLANES - 1).astype(jnp.int32)
    return lambda: pl.semaphore_wait(barrier, 1 + inner)


def greet_same():
    plane, place, core = here()
    places = lax.axis_size("p")
    barrier = pltpu.get_barrier_semaphore()
    signal(barrier, (plane, place, 1 - core))
    for step in range(1, PLANES * places):
        signal(barrier, peer(step) + (core,))
    return lambda: pl.semaphore_wait(barrier, PLANES * places)


def greet_all():
    plane, place, core = here()
    count = PLANES * lax.axis_size("p")
    barrier = pltpu.get_barrier_semaphore()
    signal(barrier, (plane, place, 1 - core))
    for step in range(1, count):
        signal(barrier, peer(step) + (core,))
        signal(barrier, peer(step) + (1 - core,))
    return lambda: pl.semaphore_wait(barrier, 2 * count - 1)


def greet_cross():
    plane, place, core = here()
    places = lax.axis_size("p")
    barrier = pltpu.get_barrier_semaphore()
    for step in range(1, places):
        signal(barrier, (plane, lax.rem(place + step, places), core))
    for step in range(1, PLANES):
        signal(barrier, (lax.rem(plane + step, PLANES), place, core))
    return lambda: pl.semaphore_wait(barrier, places + PLANES - 2)


def peer(step):
    plane, place, _ = here()
    places = lax.axis_size("p")
    index = lax.rem(plane * places + place + step, PLANES * places)
    return lax.div(index, places), lax.rem(index, places)


def halves(width):
    core = lax.axis_index("core")
    half = width // 2
    return (
        pl.ds(pl.multiple_of(core * half, LANES), half),
        pl.ds(pl.multiple_of((1 - core) * half, LANES), half),
    )


def in_turn(*steps):
    steps = list(steps)
    while steps:
        steps = [one for one in steps if next(one, steps) is not steps]


def gather_scratch():
    return [DMA((PLANES,)) for _ in range(5)]


class Gather:
    def __init__(self, out, sems):
        self.out = out
        self.arrive, self.across, self.up, self.down, self.over = sems
        self.plane, self.place, self.core = here()
        self.mine, self.other = halves(out.shape[2])

    def send(self, block, sems, receive, device):
        piece = self.out.at[block, :, self.mine]
        return remote(piece, piece, sems.at[block], receive.at[block], device)

    def rise(self, block):
        return self.send(block, self.up, self.arrive, (self.plane + 1, self.place, self.core))

    def fall(self, block):
        return self.send(block, self.down, self.arrive, (self.plane - 1, self.place, self.core))

    def cross(self, block):
        return self.send(block, self.over, self.across, (self.plane, self.place, 1 - self.core))

    def start(self):
        plane = self.plane
        pl.when(plane < PLANES - 1)(lambda: self.rise(plane).start())
        pl.when(plane > 0)(lambda: self.fall(plane).start())
        self.cross(plane).start()

    def landed(self, block):
        partner = (self.plane, self.place, 1 - self.core)
        self.send(block, self.over, self.arrive, partner).wait_recv()

    def pass_on(self, far):
        plane = self.plane

        @pl.when(plane >= far)
        def _():
            self.landed(plane - far)
            pl.when(plane < PLANES - 1)(lambda: self.rise(plane - far).start())
            self.cross(plane - far).start()

        @pl.when(plane + far < PLANES)
        def _():
            self.landed(plane + far)
            pl.when(plane > 0)(lambda: self.fall(plane + far).start())
            self.cross(plane + far).start()

    def whole(self, block):
        piece = self.out.at[block, :, self.other]
        partner = (self.plane, self.place, 1 - self.core)
        remote(piece, piece, self.over.at[block], self.across.at[block], partner).wait_recv()

    def finish(self):
        plane = self.plane
        for block in range(PLANES):
            self.cross(block).wait_send()
            pl.when((plane < PLANES - 1) & (block <= plane))(lambda: self.rise(block).wait_send())
            pl.when((plane > 0) & (block >= plane))(lambda: self.fall(block).wait_send())

    def steps(self):
        self.start()
        yield
        for far in range(1, PLANES):
            self.pass_on(far)
            yield
        for block in range(PLANES):
            self.whole(block)
        self.finish()


def order_of_arrival(step):
    plane = lax.axis_index("z")
    nearest = [sorted(range(PLANES), key=lambda block: (abs(block - own), block)) for own in range(PLANES)]
    found = jnp.int32(0)
    for own in range(PLANES):
        for at in range(PLANES):
            found = jnp.where((plane == own) & (step == at), nearest[own][at], found)
    return found


def scatter_buffers(tokens, half):
    return [
        pltpu.VMEM((PLANES, tokens, half), BF16),
        pltpu.VMEM((PLANES + 1, tokens, half), BF16),
    ]


def scatter_sems():
    return [DMA((PLANES,)) for _ in range(6)]


def scatter_scratch(tokens, half):
    return scatter_buffers(tokens, half) + scatter_sems()


def column_scatter(part, scratch, total):
    twin, came, over_s, over_r, up_s, up_r, down_s, down_r = scratch
    plane, place, core = here()
    mine, other = halves(part.shape[2])

    def cross(block):
        return remote(
            part.at[block, :, other],
            twin.at[block],
            over_s.at[block],
            over_r.at[block],
            (plane, place, 1 - core),
        )

    def rise(block):
        return remote(
            came.at[block], came.at[block], up_s.at[block], up_r.at[block], (plane + 1, place, core)
        )

    def fall(block):
        last = jnp.where(block == plane - 1, PLANES, block)
        return remote(
            came.at[block], came.at[last], down_s.at[block], down_r.at[block], (plane - 1, place, core)
        )

    def own(block):
        return part[block, :, mine].astype(F32) + twin[block].astype(F32)

    def pass_on(block, link, first):
        cross(block).wait_recv()

        @pl.when(jnp.logical_not(first))
        def _():
            link(block).wait_recv()
            came[block] = (own(block) + came[block].astype(F32)).astype(BF16)

        @pl.when(first)
        def _():
            came[block] = own(block).astype(BF16)

        link(block).start()

    for far in range(PLANES - 1, 0, -1):
        pl.when(plane + far < PLANES)(lambda: cross(plane + far).start())
        pl.when(plane >= far)(lambda: cross(plane - far).start())
    cross(plane).start()
    yield
    for far in range(PLANES - 1, 0, -1):
        pl.when(plane + far < PLANES)(lambda: pass_on(plane + far, rise, plane == 0))
        pl.when(plane >= far)(lambda: pass_on(plane - far, fall, plane == PLANES - 1))
        yield
    cross(plane).wait_recv()
    total[...] = own(plane)

    @pl.when(plane > 0)
    def _():
        rise(plane).wait_recv()
        total[...] += came[plane].astype(F32)

    @pl.when(plane < PLANES - 1)
    def _():
        fall(plane).wait_recv()
        total[...] += came[PLANES].astype(F32)

    for block in range(PLANES):
        cross(block).wait_send()
        pl.when(block > plane)(lambda: rise(block).wait_send())
        pl.when(block < plane)(lambda: fall(block).wait_send())


def gathers(out, scratch):
    size = out.shape[1] // PARTS
    return [
        Gather(out.at[:, pl.ds(at * size, size)], scratch[5 * at : 5 * at + 5]).steps()
        for at in range(PARTS)
    ]


def scatters(part, scratch, total):
    size = part.shape[1] // PARTS
    return [
        column_scatter(
            part.at[:, pl.ds(at * size, size)],
            scratch[8 * at : 8 * at + 8],
            total.at[pl.ds(at * size, size)],
        )
        for at in range(PARTS)
    ]


def fold(values):
    return sum(values[:, at : at + LANES] for at in range(0, values.shape[1], LANES))


def both_cores(local, far, send, receive):
    plane, place, core = here()
    copy = remote(local, far, send, receive, (plane, place, 1 - core))
    copy.start()
    copy.wait()
    joined = local[...] + far[...]
    return [
        jnp.sum(joined[:, at : at + LANES], axis=1, keepdims=True)
        for at in range(0, joined.shape[1], LANES)
    ]


def turn_copies(blocks, spread, send, receive):
    plane, place, core = here()
    copies = []
    for step in range(1, PLANES):
        to = lax.rem(plane + step, PLANES)
        copies.append(
            remote(blocks.at[to], spread.at[plane], send.at[step], receive.at[step], (to, place, core))
        )
    return copies


def pack_units(weights, places, plane, padded):
    size = weights.shape[0] // PLANES
    chunk = size // places
    turned = weights[pl.ds(pl.multiple_of(plane * size, 16), size), :].astype(F32).T
    blank = jnp.zeros((turned.shape[0], padded - chunk), F32)
    pieces = []
    for place in range(places):
        pieces += [turned[:, place * chunk : (place + 1) * chunk], blank]
    return jnp.concatenate(pieces, axis=1)


def unpack_units(weights, places, padded, chunk):
    pieces = [weights[:, place * padded : place * padded + chunk] for place in range(places)]
    return jnp.concatenate(pieces, axis=1).T


def front_kernel(
    own,
    other,
    gain_one,
    gain_two,
    w_query,
    w_key,
    w_value,
    w_gate,
    w_up,
    w_output,
    lens,
    normed_one,
    weights,
    gains,
    att,
    norms,
    attended,
    seq,
    w_gu,
    w_out,
    normed,
    resid,
    inverse,
    whole_c,
    whole,
    normed_in,
    qkv,
    blocks,
    spread,
    tile,
    pair,
    twin,
    tiles,
    joined,
    turned,
    low,
    part,
    local,
    far_sums,
    sum_s,
    sum_r,
    stay,
    swap_s,
    swap_r,
    turn_s,
    turn_r,
    gain_s,
    gain_r,
    spread_s,
    spread_r,
    out_s,
    out_r,
    row_s,
    row_r,
    row_l,
    back_s,
    back_r,
    back_l,
    gu_s,
    gu_r,
    gu_l,
    pass_s,
    pass_r,
    pass_l,
    keep_n,
    *rest,
):
    plane, place, core = here()
    places = lax.axis_size("p")
    count = PLANES * places
    index = plane * places + place
    width = whole.shape[2]
    mine, _ = halves(width)
    rows = attended.shape[1]
    per_row = places // rows
    gather = Gather(whole, rest[:5])
    greeted = greet_same()

    keep = pltpu.make_async_copy(own, whole.at[plane, :, mine], stay.at[0])
    keep.start()
    keep_c = pltpu.make_async_copy(other, whole_c.at[plane, :, mine], stay.at[1])
    keep_c.start()
    own_gain = gain_one.shape[1]
    tile[...] = jnp.zeros_like(tile)
    tile[0:1, :own_gain] = gain_one[...].astype(F32)
    tile[1:2, :own_gain] = gain_two[...].astype(F32)
    tile[...] = pltpu.roll(tile[...], lax.rem((2 * index + core) * own_gain, LANES), 1)
    wide = w_value.shape[1] // PLANES
    slim = w_query.shape[1] // PLANES
    for to in range(PLANES):
        pieces = [
            w_value[:, to * wide : (to + 1) * wide],
            w_query[:, to * slim : (to + 1) * slim],
            w_key[:, to * slim : (to + 1) * slim],
        ]
        joint = jnp.concatenate([piece.astype(F32) for piece in pieces], axis=1)
        blocks[to] = joint.astype(BF16)
    keep.wait()
    greeted()

    swap = remote(tile, twin, swap_s, swap_r, (plane, place, 1 - core))
    swap.start()
    turns = turn_copies(blocks, spread, turn_s, turn_r)
    for copy in turns:
        copy.start()
    gather.start()
    own_block = pltpu.make_async_copy(blocks.at[plane], spread.at[plane], stay.at[2])
    own_block.start()
    swap.wait()
    pair[...] = tile[...] + twin[...]
    tiles[index] = pair[...]
    sends = []
    for step in range(1, count):
        sends.append(
            remote(pair, tiles.at[index], gain_s.at[step], gain_r.at[step], peer(step) + (core,))
        )
        sends[-1].start()
    own_block.wait()
    for copy in turns:
        copy.wait()
    around = [
        pltpu.make_async_copy(spread, weights.at[:, place], stay.at[3]),
        pltpu.make_async_copy(w_output, w_out.at[place], stay.at[4]),
    ]
    for step in range(1, places):
        to = (plane, lax.rem(place + step, places), core)
        around.append(
            remote(spread, weights.at[:, place], spread_s.at[step], spread_r.at[step], to)
        )
        around.append(remote(w_output, w_out.at[place], out_s.at[step], out_r.at[step], to))
    for copy in around:
        copy.start()

    units = joined.shape[2] // 2
    padded = units // places
    broad = units // LANES * LANES

    def lay_out(to):
        gate = pack_units(w_gate, places, to, padded)
        up = pack_units(w_up, places, to, padded)
        joined[to, :, :broad] = gate[:, :broad].astype(BF16)
        joined[to, :, broad : 2 * broad] = up[:, :broad].astype(BF16)
        if units > broad:
            joined[to, :, 2 * broad :] = jnp.concatenate(
                [gate[:, broad:], up[:, broad:]], axis=1
            ).astype(BF16)

    def passed(step):
        block = lax.rem(plane - step + PLANES, PLANES)
        source = joined.at[plane] if step == 0 else turned.at[block]
        target = w_gu.at[block, place]
        copies = [pltpu.make_async_copy(source, target, pass_l.at[step])]
        for side in range(1, places):
            to = (plane, lax.rem(place + side, places), core)
            copies.append(
                remote(source, target, pass_s.at[step, side], pass_r.at[step, side], to)
            )
        return copies

    lay_out(plane)
    for copy in passed(0):
        copy.start()
    for step in range(1, PLANES):
        lay_out(lax.rem(plane + step, PLANES))

    gu_turns = turn_copies(joined, turned, gu_s, gu_r)

    def inward(step):
        to = lax.rem(plane + step, PLANES)
        return (jnp.abs(to - plane) == 1) & (to > 0) & (to < PLANES - 1)

    for step in range(1, PLANES):
        pl.when(inward(step))(gu_turns[step - 1].start)
    gather.pass_on(1)
    for copy in sends + around:
        copy.wait()
    each = width // count
    for at in range(0, width, LANES):
        group = range(at // each, (at + LANES) // each)
        gains[:, at : at + LANES] = sum(tiles[source] for source in group)
    gain = gains[0:1, :]

    def row_copy(block, step):
        to = lax.rem(place + step, places)
        return remote(
            qkv.at[block, lax.div(to, per_row)],
            seq.at[block, place],
            row_s.at[block, step],
            row_r.at[block, step],
            (plane, to, core),
        )

    def own_row(block):
        return pltpu.make_async_copy(
            qkv.at[block, lax.div(place, per_row)], seq.at[block, place], row_l.at[block]
        )

    def project(block):
        gather.whole(block)
        values = whole[block].astype(F32)
        scale = lax.rsqrt(jnp.mean(values * values, axis=1, keepdims=True) + EPSILON)
        normed_in[block] = (values * scale * gain).astype(BF16)
        pltpu.make_async_copy(normed_in.at[block], normed_one.at[block], keep_n.at[block]).start()
        flat_weights = weights[...].reshape(width, qkv.shape[3])
        qkv[block] = dot(normed_in[block], flat_weights).astype(BF16).reshape(qkv.shape[1:])
        for step in range(1, places):
            row_copy(block, step).start()
        own_row(block).start()

    project(order_of_arrival(0))
    for far in range(2, PLANES):
        gather.pass_on(far)
        project(order_of_arrival(far - 1))

    for step in range(1, PLANES):
        pl.when(jnp.logical_not(inward(step)))(gu_turns[step - 1].start)
    project(order_of_arrival(PLANES - 1))
    gather.finish()

    alive = alive_of(lens, att.shape[0], rows).astype(BF16)
    for block in range(PLANES):
        for step in range(1, places):
            row_copy(block, step).wait()
        own_row(block).wait()
    attend(seq, alive, att, norms)
    low[...] = att[...].astype(BF16).reshape(low.shape)
    finish = start_back(low, attended, back_s, back_r, back_l)
    finish()
    tokens = whole.shape[1]
    flat_out = w_out[...].reshape(-1, width)
    for block in range(PLANES):
        rows_in = attended[block].reshape(tokens, flat_out.shape[0])
        part[block] = dot(rows_in, flat_out).astype(BF16)

    def gu_flow():
        for step in range(1, PLANES):
            gu_turns[step - 1].wait()
            for copy in passed(step):
                copy.start()
            yield

    keep_c.wait()
    two = 5 + 5 * PARTS
    in_turn(*scatters(part, rest[two:], resid), *gathers(whole_c, rest[5:two]), gu_flow())
    resid[...] += own[...].astype(F32)
    local[...] = fold(resid[...] * resid[...])
    (total,) = both_cores(local, far_sums, sum_s, sum_r)
    scale = lax.rsqrt(total / width + EPSILON)
    inverse[...] = jnp.broadcast_to(scale, inverse.shape)
    normed[...] = (resid[...] * scale * gains[1:2, mine]).astype(BF16)
    for step in range(PLANES):
        for copy in passed(step):
            copy.wait()
        pltpu.make_async_copy(normed_in.at[step], normed_one.at[step], keep_n.at[step]).wait()


def start_back(seq, out, send, receive, local):
    plane, place, core = here()
    places = lax.axis_size("p")
    rows = out.shape[1]
    per_row = places // rows
    row = lax.div(place, per_row)
    speaks = lax.rem(place, per_row) == 0

    def copy(step):
        to = lax.rem(place + step, places)
        return remote(
            seq.at[:, to], out.at[:, row], send.at[step], receive.at[row], (plane, to, core)
        )

    def stay():
        return pltpu.make_async_copy(seq.at[:, place], out.at[:, row], local)

    @pl.when(speaks)
    def _():
        for step in range(1, places):
            copy(step).start()
        stay().start()

    def finish():
        @pl.when(speaks)
        def _():
            stay().wait()
            for step in range(1, places):
                copy(step).wait_send()

        for other in range(rows):

            @pl.when(other * per_row != place)
            def _():
                remote(
                    out.at[:, other],
                    out.at[:, other],
                    send.at[0],
                    receive.at[other],
                    (plane, lax.rem(place + 1, places), core),
                ).wait_recv()

    return finish


def flat(ref):
    block = ref[...]
    return block.reshape(-1, block.shape[-1])


def columns_of(seq, heads, head):
    wide = heads * HEAD_V
    slim = seq[:, wide : wide + 2 * heads * FEAT].astype(F32)
    queries = slim[:, head * FEAT : (head + 1) * FEAT].astype(BF16)
    keys = slim[:, (heads + head) * FEAT : (heads + head + 1) * FEAT].astype(BF16)
    return queries, keys, seq[:, head * HEAD_V : (head + 1) * HEAD_V]


def causal(start, stop, values):
    queries = start + lax.broadcasted_iota(jnp.int32, values.shape, 0)
    keys = lax.broadcasted_iota(jnp.int32, values.shape, 1)
    return jnp.where(queries >= keys, values, 0.0)


def alive_of(lens, length, rows):
    row = lax.div(lax.axis_index("p"), lax.axis_size("p") // rows)
    positions = lax.broadcasted_iota(jnp.int32, (length, LANES), 0)
    return jnp.where(positions < lens[pl.ds(row, 1), :], 1.0, 0.0).astype(F32)


def attend(seq, alive, att, norms):
    everything = flat(seq)
    length = everything.shape[0]
    heads = att.shape[1] // HEAD_V
    block = min(QUERY_BLOCK, length)
    for head in range(heads):
        queries, keys, values = columns_of(everything, heads, head)
        values = jnp.concatenate([values * alive, alive], axis=1)
        wide = slice(head * HEAD_V, (head + 1) * HEAD_V)
        for start in range(0, length, block):
            stop = start + block
            scores = dot(queries[start:stop], keys[:stop], ((1,), (1,)))
            half = 1.0 + 0.25 * scores
            taylor = causal(start, stop, 0.5 + 0.5 * (half * half)).astype(BF16)
            sums = dot(taylor, values[:stop])
            norm = sums[:, HEAD_V:]
            ratio = sums[:, :HEAD_V] / norm
            att[start:stop, wide] = ratio
            norms[start:stop, wide] = norm


def attend_back(seq, alive, att, norms, rows, keep, low):
    everything = flat(seq)
    length = everything.shape[0]
    heads = att.shape[1] // HEAD_V
    block = min(QUERY_BLOCK, length)
    grads = flat(rows).astype(F32)
    grad_q, grad_k = [], []
    for head in range(heads):
        queries, keys, values = columns_of(everything, heads, head)
        live_keys = (keys.astype(F32) * alive[:, :FEAT]).astype(BF16)
        wide = slice(head * HEAD_V, (head + 1) * HEAD_V)
        grad = grads[:, wide]
        norm = norms[:, wide]
        grad_num = (grad / norm).astype(BF16)
        grad_norm = -jnp.sum(grad * att[:, wide] / norm, axis=1, keepdims=True)
        parts = []
        for start in range(0, length, block):
            stop = start + block
            scores = dot(queries[start:stop], keys[:stop], ((1,), (1,)))
            half = 1.0 + 0.25 * scores
            taylor = causal(start, stop, 0.5 + 0.5 * (half * half)).astype(BF16)
            inner = dot(grad_num[start:stop], values[:stop], ((1,), (1,))) + grad_norm[start:stop]
            slope = causal(start, stop, half * inner).astype(BF16)
            parts.append(dot(slope, live_keys[:stop]) * 0.25)
            from_values = dot(taylor, grad_num[start:stop], ((0,), (0,)))
            from_keys = dot(slope, queries[start:stop], ((0,), (0,)))
            if start:
                keep[:start, wide] += from_values[:start]
                keep[:start, heads * HEAD_V + head * FEAT : heads * HEAD_V + (head + 1) * FEAT] += (
                    from_keys[:start]
                )
            keep[start:stop, wide] = from_values[start:]
            keep[start:stop, heads * HEAD_V + head * FEAT : heads * HEAD_V + (head + 1) * FEAT] = (
                from_keys[start:]
            )
        grad_q.append(jnp.concatenate(parts, axis=0))
        keep[:, wide] *= alive
    wide = heads * HEAD_V
    keys = keep[:, wide : wide + heads * FEAT] * (0.25 * alive[:, : heads * FEAT])
    result = jnp.concatenate([keep[:, :wide]] + grad_q + [keys], axis=1)
    low[...] = result.astype(BF16).reshape(low.shape)


def feed_kernel(
    own,
    w_gu,
    w_dn,
    grads,
    part,
    fed,
    out_gu,
    out_dn,
    normed,
    held_gu,
    held_dn,
    held_c,
    sum_gu,
    sum_dn,
    gate_up,
    grad_hidden,
    hidden,
    grad_gu,
    stage,
    load,
    keep,
    store,
    ending,
    *sems,
):
    plane = lax.axis_index("z")
    mine, _ = halves(normed.shape[2])
    places = lax.axis_size("p")
    units = hidden.shape[1]
    broad = units // LANES * LANES
    rest = units - broad
    rows = normed.shape[1]
    loads = [
        pltpu.make_async_copy(w_gu, held_gu, load.at[0]),
        pltpu.make_async_copy(w_dn, held_dn, load.at[1]),
        pltpu.make_async_copy(grads, held_c, load.at[2]),
    ]
    for copy in loads:
        copy.start()
    gather = Gather(normed, sems)
    greeted = greet_column()
    stay = pltpu.make_async_copy(own, normed.at[plane, :, mine], keep)
    stay.start()
    stay.wait()
    greeted()
    gather.start()
    sum_gu[...] = jnp.zeros_like(sum_gu)
    sum_dn[...] = jnp.zeros_like(sum_dn)
    for copy in loads:
        copy.wait()

    def tiles(width):
        return [slice(at, min(at + TILE, width)) for at in range(0, width, TILE)]

    def stores(block, slot):
        return (
            pltpu.make_async_copy(stage.at[0, slot], fed.at[block], store.at[0, slot]),
            pltpu.make_async_copy(stage.at[1, slot], part.at[block], store.at[1, slot]),
        )

    def middle(at):
        here_rows = pl.ds(pl.multiple_of(at * ROW_BLOCK, ROW_BLOCK), ROW_BLOCK)

        def parts(gate, up, above):
            sigmoid = jax.nn.sigmoid(gate)
            silu = gate * sigmoid
            slope = sigmoid * (1.0 + gate * (1.0 - sigmoid))
            return silu * up, above * up * slope, above * silu

        both = gate_up[here_rows, :]
        above = grad_hidden[here_rows, :]
        first, second, third = parts(
            both[:, :broad], both[:, broad : 2 * broad], above[:, :broad]
        )
        hidden[here_rows, :broad] = first.astype(BF16)
        grad_gu[here_rows, :broad] = second.astype(BF16)
        grad_gu[here_rows, broad : 2 * broad] = third.astype(BF16)
        if rest:
            last = both[:, 2 * broad :]
            turned = pltpu.roll(last, rest, 1)
            first, second, third = parts(last, turned, above[:, broad : broad + LANES])
            hidden[here_rows, broad:] = first[:, :rest].astype(BF16)
            lane = lax.broadcasted_iota(jnp.int32, last.shape, 1)
            joined = jnp.where(lane < rest, second, pltpu.roll(third, rest, 1))
            grad_gu[here_rows, 2 * broad :] = joined.astype(BF16)

    def through(step, carry):
        pl.when(step > 0)(lambda: gather.pass_on(step))
        block = order_of_arrival(step)
        slot = lax.rem(step, 2)
        gather.whole(block)
        for cut in tiles(2 * units):
            gate_up[:, cut] = dot(normed[block], held_gu[:, cut])
        grad_hidden[:, :units] = dot(held_c[block], held_dn[...], ((1,), (1,)))
        lax.fori_loop(0, rows // ROW_BLOCK, lambda at, none: (middle(at), none)[1], 0)

        @pl.when(step >= 2)
        def _():
            for copy in stores(order_of_arrival(step - 2), slot):
                copy.wait()

        for cut in tiles(normed.shape[2]):
            stage[0, slot, :, cut] = dot(hidden[...], held_dn[:, cut]).astype(BF16)
            stage[1, slot, :, cut] = dot(grad_gu[...], held_gu[cut, :], ((1,), (1,))).astype(BF16)
        for copy in stores(block, slot):
            copy.start()
        for cut in tiles(normed.shape[2]):
            sum_gu[cut, :] += dot(normed[block, :, cut], grad_gu[...], ((0,), (0,)))
            sum_dn[:, cut] += dot(hidden[...], held_c[block, :, cut], ((0,), (0,)))
        return carry

    lax.fori_loop(0, PLANES, through, 0)
    own_rows = out_gu.shape[2]
    ends = []
    for block in range(normed.shape[2] // own_rows):
        cut = pl.ds(block * own_rows, own_rows)
        held_gu[cut, :] = sum_gu[cut, :].astype(BF16)
        ends.append(
            pltpu.make_async_copy(
                held_gu.at[cut], out_gu.at[block % places, block // places], ending.at[block]
            )
        )
        ends[-1].start()
    held_dn[...] = sum_dn[...].astype(BF16)
    ends.append(pltpu.make_async_copy(held_dn, out_dn, load.at[1]))
    ends[-1].start()
    for step in (PLANES - 2, PLANES - 1):
        for copy in stores(order_of_arrival(step), step % 2):
            copy.wait()
    for copy in ends:
        copy.wait()
    gather.finish()


def to_rows(values, seq, send, receive, local):
    plane, place, core = here()
    places = lax.axis_size("p")
    per_row = places // values.shape[1]
    copies = []
    for step in range(1, places):
        to = lax.rem(place + step, places)
        row = lax.div(to, per_row)
        copies.append(
            remote(
                values.at[:, row], seq.at[:, place], send.at[step], receive.at[step], (plane, to, core)
            )
        )
    copies.append(
        pltpu.make_async_copy(values.at[:, lax.div(place, per_row)], seq.at[:, place], local)
    )
    return copies


def attend_back_kernel(
    grad_mix,
    w_out,
    attended,
    seq,
    lens,
    att,
    norms,
    blocks,
    out,
    spread,
    out_output,
    grad_att,
    rows,
    low,
    keep,
    *sems,
):
    row_s, row_r, local, back_s, back_r, back_l, turn_s, turn_r, stay_s = sems
    plane = lax.axis_index("z")
    greeted = greet_cross()
    for block in range(PLANES):
        product = dot(grad_mix[block], w_out[...], ((1,), (1,))).astype(BF16)
        grad_att[block] = product.reshape(grad_att.shape[1:])
    greeted()
    copies = to_rows(grad_att, rows, row_s, row_r, local)
    for copy in copies:
        copy.start()
    turns = turn_copies(blocks, spread, turn_s, turn_r)
    turns.append(pltpu.make_async_copy(blocks.at[plane], spread.at[plane], stay_s))
    for copy in turns:
        copy.start()
    alive = alive_of(lens, att.shape[0], grad_att.shape[1])
    for at in range(0, grad_mix.shape[2], TILE):
        cut = slice(at, at + TILE)
        product = sum(
            dot(attended[block], grad_mix[block, :, cut], ((0,), (0,))) for block in range(PLANES)
        )
        out_output[:, :, cut] = product.astype(BF16).reshape(out_output.shape[:2] + (TILE,))
    for copy in copies:
        copy.wait()
    attend_back(seq, alive, att, norms, rows, keep, low)
    finish = start_back(low, out, back_s, back_r, back_l)
    for copy in turns:
        copy.wait()
    finish()


def back_kernel(
    far_part,
    resid,
    inverse,
    gains,
    cotangent,
    far_fed,
    low,
    grad,
    gain_sum,
    mixed,
    part,
    fed,
    local,
    far,
    send,
    receive,
    load,
    total_fed,
    *rest,
):
    plane = lax.axis_index("z")
    mine, _ = halves(part.shape[2])
    one, two = 5 * PARTS, 13 * PARTS
    greeted = greet_column()
    copies = [
        pltpu.make_async_copy(far_part, part, load.at[0]),
        pltpu.make_async_copy(far_fed, fed, load.at[1]),
    ]
    for copy in copies:
        copy.start()
    copies[0].wait()
    greeted()
    in_turn(*scatters(part, rest[one:two], grad))
    copies[1].wait()
    scale = inverse[:, :1]
    values, above = resid[...], grad[...]
    scaled = above * gains[1:2, mine]
    local[...] = fold(scaled * values)
    (total,) = both_cores(local, far, send, receive)
    mean = total / part.shape[2]
    grad[...] = cotangent[...].astype(F32) + scale * scaled - values * scale**3 * mean
    low[plane, :, mine] = grad[...].astype(BF16)
    in_turn(
        *gathers(low, rest[:one]),
        *scatters(fed, rest[two:], total_fed),
        keep_sum(gain_sum, above * values * scale),
    )
    mixed[...] = (total_fed[...] + resid[...]).astype(BF16)


def keep_sum(gain_sum, values):
    yield
    gain_sum[...] = jnp.sum(values, axis=0, keepdims=True)


def last_kernel(
    grad_qkv,
    w_qkv,
    normed,
    tokens,
    gains,
    resid_grad,
    parts_out,
    joined,
    gain_two,
    grad,
    sum_out,
    grad_query,
    grad_key,
    grad_value,
    grad_gate,
    grad_up,
    out_gains,
    part,
    parts_qkv,
    sums,
    came_gains,
    local,
    far,
    send,
    receive,
    came_out,
    came_qkv,
    blocks,
    spread,
    stay,
    out_s,
    out_r,
    qkv_s,
    qkv_r,
    turn_s,
    turn_r,
    own_s,
    own_r,
    *rest,
):
    plane, place, core = here()
    places = lax.axis_size("p")
    mine, _ = halves(part.shape[2])
    own_rows = parts_qkv.shape[2]
    greeted = greet_all()
    flat_weights = w_qkv[...].reshape(part.shape[2], grad_qkv.shape[2])
    for block in range(PLANES):
        part[block] = dot(grad_qkv[block], flat_weights, ((1,), (1,))).astype(BF16)
    greeted()
    outs, shares, moves = [], [], []
    for step in range(1, places):
        to = lax.rem(place + step, places)
        device = (plane, to, core)
        outs.append(
            remote(parts_out.at[to], came_out.at[place], out_s.at[step], out_r.at[step], device)
        )
        shares.append(
            remote(
                parts_qkv.at[:, to], came_qkv.at[place], qkv_s.at[step], qkv_r.at[step], device
            )
        )
    outs.append(pltpu.make_async_copy(parts_out.at[place], came_out.at[place], stay.at[0]))
    shares.append(pltpu.make_async_copy(parts_qkv.at[:, place], came_qkv.at[place], stay.at[1]))

    def lay_out(grads, first):
        units = joined.shape[2] // 2
        broad = units // LANES * LANES
        rest = units - broad
        size = grads.shape[0] // PLANES
        for to in range(PLANES):
            piece = joined[to].astype(F32)
            low = 2 * broad + (0 if first else rest)
            start = 0 if first else broad
            pieces = [piece[:, start : start + broad]]
            if rest:
                pieces.append(piece[:, low : low + rest])
            found = jnp.concatenate(pieces, axis=1)
            grads[to * size : (to + 1) * size, :] = unpack_units(
                found, places, units // places, size // places
            )

    def others():
        for copy in outs:
            copy.start()
        yield
        tokens_all = PLANES * normed.shape[1]
        grads = grad_qkv[...].reshape(tokens_all, grad_qkv.shape[2])
        for at in range(0, part.shape[2], TILE):
            left = normed[:, :, at : at + TILE].reshape(tokens_all, TILE)
            product = dot(left, grads, ((0,), (0,))).astype(BF16)
            for row in range(0, TILE, own_rows):
                owner = (at + row) // own_rows
                parts_qkv[owner // places, owner % places] = product[row : row + own_rows]
            if at + TILE == part.shape[2] // 2:
                yield
        for copy in shares:
            copy.start()
        yield
        lay_out(grad_gate, True)
        yield
        for copy in outs:
            copy.wait()
        sum_out[...] = sum(came_out[other].astype(F32) for other in range(places))
        for copy in shares:
            copy.wait()
        blocks[...] = sum(came_qkv[other].astype(F32) for other in range(places)).astype(BF16)
        moves.extend(turn_copies(blocks, spread, turn_s, turn_r))
        moves.append(pltpu.make_async_copy(blocks.at[plane], spread.at[plane], stay.at[2]))
        for copy in moves:
            copy.start()
        yield
        lay_out(grad_up, False)

    in_turn(*scatters(part, rest, grad), others())
    values, above = tokens[...].astype(F32), grad[...]
    scaled = above * gains[0:1, mine]
    local[:, :LANES] = fold(scaled * values)
    local[:, LANES:] = fold(values * values)
    total, square = both_cores(local, far, send, receive)
    scale = lax.rsqrt(square / part.shape[2] + EPSILON)
    sums[...] = jnp.zeros_like(sums)
    sums[0:1, :] = jnp.sum(above * values * scale, axis=0, keepdims=True)
    sums[1:2, :] = gain_two[...]
    finish = to_owners(sums, came_gains, own_s, own_r)
    mean = total / part.shape[2]
    grad[...] = resid_grad[...] + scale * scaled - values * scale**3 * mean
    for copy in moves:
        copy.wait()
    wide = grad_value.shape[1] // PLANES
    slim = grad_query.shape[1] // PLANES
    found = [spread[to].astype(F32) for to in range(PLANES)]
    for to in range(PLANES):
        grad_value[:, to * wide : (to + 1) * wide] = found[to][:, :wide]
    grad_query[...] = jnp.concatenate([one[:, wide : wide + slim] for one in found], axis=1)
    grad_key[...] = jnp.concatenate([one[:, wide + slim :] for one in found], axis=1)
    finish(out_gains)


def end_kernel(
    far_part,
    far_fed,
    parts_gu,
    far_normed,
    resid,
    inverse,
    gains,
    cotangent,
    tokens,
    w_out,
    attended,
    seq,
    lens,
    att,
    norms,
    w_qkv,
    mixed,
    grad,
    sum_out,
    grad_query,
    grad_key,
    grad_value,
    grad_gate,
    grad_up,
    out_gains,
    part,
    fed,
    low,
    resid_grad,
    total_fed,
    came_gu,
    blocks_gu,
    joined,
    grad_att,
    rows_in,
    rows_out,
    keep,
    grad_qkv,
    parts_out,
    came_out,
    parts_qkv,
    came_qkv,
    blocks,
    spread,
    sums,
    came_gains,
    local,
    far,
    local_two,
    far_two,
    sum_s,
    sum_r,
    load,
    gu_s,
    gu_r,
    gu_l,
    turn_gu_s,
    turn_gu_r,
    row_s,
    row_r,
    row_l,
    back_s,
    back_r,
    back_l,
    out_s,
    out_r,
    qkv_s,
    qkv_r,
    turn_s,
    turn_r,
    own_s,
    own_r,
    stay,
    *rest,
):
    plane, place, core = here()
    places = lax.axis_size("p")
    mine, _ = halves(part.shape[2])
    width = part.shape[2]
    own_rows = parts_qkv.shape[2]
    rows = grad_att.shape[1]
    per_row = places // rows
    size = part.shape[1] // PARTS
    cuts = [pl.ds(at * size, size) for at in range(PARTS)]
    gather_at, first_at, fed_at, last_at = (PARTS * n for n in (0, 5, 13, 21))
    buffers = [rest[first_at + 8 * at : first_at + 8 * at + 2] for at in range(PARTS)]
    last_sems = [rest[last_at + 6 * at : last_at + 6 * at + 6] for at in range(PARTS)]
    greeted = greet_all()
    loads = [
        pltpu.make_async_copy(far_part, part, load.at[0]),
        pltpu.make_async_copy(far_fed, fed, load.at[1]),
    ]
    for copy in loads:
        copy.start()
    plane_gu = [pltpu.make_async_copy(parts_gu.at[place], came_gu.at[place], gu_l)]
    for step in range(1, places):
        to = lax.rem(place + step, places)
        plane_gu.append(
            remote(
                parts_gu.at[to], came_gu.at[place], gu_s.at[step], gu_r.at[step], (plane, to, core)
            )
        )
    loads[0].wait()
    greeted()
    for copy in plane_gu:
        copy.start()

    in_turn(*scatters(part, rest[first_at:fed_at], resid_grad))
    loads[1].wait()
    scale = inverse[:, :1]
    values, above = resid[...], resid_grad[...]
    scaled = above * gains[1:2, mine]
    local[...] = fold(scaled * values)
    (total,) = both_cores(local, far, sum_s.at[0], sum_r.at[0])
    mean = total / width
    resid_grad[...] = cotangent[...].astype(F32) + scale * scaled - values * scale**3 * mean
    low[plane, :, mine] = resid_grad[...].astype(BF16)
    sums[...] = jnp.zeros_like(sums)

    def row_copy(block, step):
        to = lax.rem(place + step, places)
        return remote(
            grad_att.at[block, lax.div(to, per_row)],
            rows_in.at[block, place],
            row_s.at[block, step],
            row_r.at[block, step],
            (plane, to, core),
        )

    def own_row(block):
        return pltpu.make_async_copy(
            grad_att.at[block, lax.div(place, per_row)], rows_in.at[block, place], row_l.at[block]
        )

    all_lows = [
        Gather(low.at[:, cut], rest[gather_at + 5 * at : gather_at + 5 * at + 5])
        for at, cut in enumerate(cuts)
    ]

    def to_rows(block):
        for gather in all_lows:
            gather.whole(block)
        product = dot(low[block], w_out[...], ((1,), (1,))).astype(BF16)
        grad_att[block] = product.reshape(grad_att.shape[1:])
        for step in range(1, places):
            row_copy(block, step).start()
        own_row(block).start()

    def lows():
        for gather in all_lows:
            gather.start()
        yield
        sums[1:2, :] = jnp.sum(above * values * scale, axis=0, keepdims=True)
        for step in range(1, PLANES):
            for gather in all_lows:
                gather.pass_on(step)
            to_rows(order_of_arrival(step - 1))
            yield
        to_rows(order_of_arrival(PLANES - 1))
        for gather in all_lows:
            gather.finish()

    in_turn(lows(), *scatters(fed, rest[fed_at:last_at], total_fed))
    mixed[...] = (total_fed[...] + resid[...]).astype(BF16)
    normed_load = pltpu.make_async_copy(far_normed, fed, load.at[2])
    normed_load.start()
    for copy in plane_gu:
        copy.wait()
    for to in range(PLANES):
        total_gu = sum(came_gu[other, to].astype(F32) for other in range(places))
        blocks_gu[to] = total_gu.astype(BF16)
    gu_turns = turn_copies(blocks_gu, joined, turn_gu_s, turn_gu_r)
    gu_turns.append(pltpu.make_async_copy(blocks_gu.at[plane], joined.at[plane], stay.at[3]))
    for copy in gu_turns:
        copy.start()

    alive = alive_of(lens, att.shape[0], rows)
    for block in range(PLANES):
        for step in range(1, places):
            row_copy(block, step).wait()
        own_row(block).wait()
    attend_back(seq, alive, att, norms, rows_in, keep, rows_out)
    finish = start_back(rows_out, grad_qkv, back_s, back_r, back_l)
    for at in range(0, width, TILE):
        cut = slice(at, at + TILE)
        product = sum(
            dot(attended[block], low[block, :, cut], ((0,), (0,))) for block in range(PLANES)
        )
        parts_out[:, :, cut] = product.astype(BF16).reshape(parts_out.shape[:2] + (TILE,))
    finish()

    flat_weights = w_qkv[...].reshape(width, grad_qkv.shape[3])
    count = part.shape[1]
    for block in range(PLANES):
        rows_of = grad_qkv[block].reshape(count, grad_qkv.shape[3])
        part[block] = dot(rows_of, flat_weights, ((1,), (1,))).astype(BF16)
    outs, shares, moves = [], [], []
    for step in range(1, places):
        to = lax.rem(place + step, places)
        device = (plane, to, core)
        outs.append(
            remote(parts_out.at[to], came_out.at[place], out_s.at[step], out_r.at[step], device)
        )
        shares.append(
            remote(
                parts_qkv.at[:, to], came_qkv.at[place], qkv_s.at[step], qkv_r.at[step], device
            )
        )
    outs.append(pltpu.make_async_copy(parts_out.at[place], came_out.at[place], stay.at[0]))
    shares.append(pltpu.make_async_copy(parts_qkv.at[:, place], came_qkv.at[place], stay.at[1]))

    def lay_out(grads, first):
        units = joined.shape[2] // 2
        broad = units // LANES * LANES
        left = units - broad
        extent = grads.shape[0] // PLANES
        for to in range(PLANES):
            piece = joined[to].astype(F32)
            low_at = 2 * broad + (0 if first else left)
            start = 0 if first else broad
            pieces = [piece[:, start : start + broad]]
            if left:
                pieces.append(piece[:, low_at : low_at + left])
            found = jnp.concatenate(pieces, axis=1)
            grads[to * extent : (to + 1) * extent, :] = unpack_units(
                found, places, units // places, extent // places
            )

    def others():
        yield
        normed_load.wait()
        tokens_all = PLANES * count
        grads = grad_qkv[...].reshape(tokens_all, grad_qkv.shape[3])
        for at in range(0, width, TILE):
            left = fed[:, :, at : at + TILE].reshape(tokens_all, TILE)
            product = dot(left, grads, ((0,), (0,))).astype(BF16)
            for row in range(0, TILE, own_rows):
                owner = (at + row) // own_rows
                parts_qkv[owner // places, owner % places] = product[row : row + own_rows]
            if at + TILE == width // 2:
                yield
        for copy in shares + outs:
            copy.start()
        yield
        for copy in gu_turns:
            copy.wait()
        lay_out(grad_gate, True)
        yield
        for copy in shares:
            copy.wait()
        blocks[...] = sum(came_qkv[other].astype(F32) for other in range(places)).astype(BF16)
        moves.extend(turn_copies(blocks, spread, turn_s, turn_r))
        moves.append(pltpu.make_async_copy(blocks.at[plane], spread.at[plane], stay.at[2]))
        for copy in moves:
            copy.start()
        yield
        for copy in outs:
            copy.wait()
        sum_out[...] = sum(came_out[other].astype(F32) for other in range(places))
        lay_out(grad_up, False)

    lasts = [
        column_scatter(part.at[:, cut], (*buffers[at], *last_sems[at]), grad.at[cut])
        for at, cut in enumerate(cuts)
    ]
    in_turn(*lasts, others())
    values, above = tokens[...].astype(F32), grad[...]
    scaled = above * gains[0:1, mine]
    local_two[:, :LANES] = fold(scaled * values)
    local_two[:, LANES:] = fold(values * values)
    total, square = both_cores(local_two, far_two, sum_s.at[1], sum_r.at[1])
    scale = lax.rsqrt(square / width + EPSILON)
    sums[0:1, :] = jnp.sum(above * values * scale, axis=0, keepdims=True)
    finish = to_owners(sums, came_gains, own_s, own_r)
    mean = total / width
    grad[...] = resid_grad[...] + scale * scaled - values * scale**3 * mean
    for copy in moves:
        copy.wait()
    wide = grad_value.shape[1] // PLANES
    slim = grad_query.shape[1] // PLANES
    found = [spread[to].astype(F32) for to in range(PLANES)]
    for to in range(PLANES):
        grad_value[:, to * wide : (to + 1) * wide] = found[to][:, :wide]
    grad_query[...] = jnp.concatenate([one[:, wide : wide + slim] for one in found], axis=1)
    grad_key[...] = jnp.concatenate([one[:, wide + slim :] for one in found], axis=1)
    finish(out_gains)


def to_owners(sums, came, send, receive):
    plane, place, core = here()
    places = lax.axis_size("p")
    count = PLANES * places
    near = count // 2
    index = plane * places + place
    side = lax.div(index, near)
    width = sums.shape[1] // near

    def copy(step, target):
        at = step * width // LANES * LANES
        owner = core * near + step
        device = (lax.div(owner, places), lax.rem(owner, places), target)
        return remote(
            sums.at[:, pl.ds(at, LANES)],
            came.at[index],
            send.at[2 * step + target],
            receive.at[index],
            device,
        )

    def to_self(step, target):
        return (core * near + step == index) & (core == target)

    for step in range(near):
        for target in range(2):
            local = to_self(step, target)
            pl.when(jnp.logical_not(local))(lambda: copy(step, target).start())

            @pl.when(local)
            def _():
                at = step * width // LANES * LANES
                came[index] = sums[:, at : at + LANES]

    def finish(out):
        for step in range(count):
            source = lax.rem(index + step, count)

            @pl.when((step > 0) | (side != core))
            def _():
                remote(
                    came.at[source],
                    came.at[source],
                    send.at[0],
                    receive.at[source],
                    (plane, place, 1 - core),
                ).wait_recv()

        out[...] = sum(came[step] for step in range(count))
        for step in range(near):
            for target in range(2):
                local = to_self(step, target)
                pl.when(jnp.logical_not(local))(lambda: copy(step, target).wait_send())

    return finish


def call(kernel, identity, micros, outs, scratch, args, far_args=(), far_outs=()):
    def spec(far):
        return pl.BlockSpec(memory_space=pl.ANY if far else pltpu.VMEM)

    return pl.pallas_call(
        kernel,
        out_shape=outs,
        in_specs=[spec(at in far_args) for at in range(len(args))],
        out_specs=[spec(at in far_outs) for at in range(len(outs))],
        scratch_shapes=scratch,
        cost_estimate=pl.CostEstimate(
            flops=micros * 10**9, bytes_accessed=micros * 10**6, transcendentals=0
        ),
        compiler_params=pltpu.CompilerParams(
            collective_id=identity, has_side_effects=True, vmem_limit_bytes=VMEM_LIMIT
        ),
    )(*args)


def shape(dims, dtype):
    return jax.ShapeDtypeStruct(dims, dtype)


def front(x_half, c_half, gain_one, gain_two, w_query, w_key, w_value, w_gate, w_up, w_output, lens, units, identity):
    tokens, half = x_half.shape
    places = lax.axis_size("p")
    count = PLANES * places
    rows = lens.shape[0]
    positions = tokens // rows
    length = PLANES * places * positions
    own_rows = w_query.shape[0]
    wide = w_value.shape[1] // PLANES
    width = wide + 2 * (w_query.shape[1] // PLANES)
    whole = (PLANES, tokens, 2 * half)
    blocks = (PLANES, own_rows, width)
    gu = (PLANES, own_rows, 2 * units)
    return call(
        front_kernel,
        identity,
        150,
        [
            shape(whole, BF16),
            shape((PLANES, places, own_rows, width), BF16),
            shape((8, 2 * half), F32),
            shape((length, wide), F32),
            shape((length, wide), F32),
            shape((PLANES, rows, positions, wide), BF16),
            shape((PLANES, places, positions, width), BF16),
            shape((PLANES, places, own_rows, 2 * units), BF16),
            shape((places,) + w_output.shape, BF16),
            shape((tokens, half), BF16),
            shape((tokens, half), F32),
            shape((tokens, LANES), F32),
            shape(whole, BF16),
        ],
        [
            pltpu.VMEM(whole, BF16),
            pltpu.VMEM(whole, BF16),
            pltpu.VMEM((PLANES, rows, positions, width), BF16),
            pltpu.VMEM(blocks, BF16),
            pltpu.VMEM(blocks, BF16),
            pltpu.VMEM((8, LANES), F32),
            pltpu.VMEM((8, LANES), F32),
            pltpu.VMEM((8, LANES), F32),
            pltpu.VMEM((count, 8, LANES), F32),
            pltpu.VMEM(gu, BF16),
            pltpu.VMEM(gu, BF16),
            pltpu.VMEM((PLANES, places, positions, wide), BF16),
            pltpu.VMEM(whole, BF16),
        ]
        + sums_scratch(tokens, 1)
        + [DMA((5,)), DMA, DMA]
        + [DMA((PLANES,)), DMA((PLANES,)), DMA((count,)), DMA((count,))]
        + [DMA((places,)) for _ in range(4)]
        + [DMA((PLANES, places)), DMA((PLANES, places)), DMA((PLANES,))]
        + [DMA((places,)), DMA((rows,)), DMA]
        + [DMA((PLANES,)), DMA((PLANES,)), DMA]
        + [DMA((PLANES, places)), DMA((PLANES, places)), DMA((PLANES,)), DMA((PLANES,))]
        + gather_scratch() * (1 + PARTS)
        + scatter_scratch(tokens // PARTS, half) * PARTS,
        [
            x_half,
            c_half,
            gain_one,
            gain_two,
            w_query,
            w_key,
            w_value,
            w_gate,
            w_up,
            w_output,
            lens,
        ],
        (1,),
        (0, 7, 12),
    )


def sums_scratch(tokens, count):
    return [pltpu.VMEM((tokens, count * LANES), F32) for _ in range(2)] + [DMA, DMA]


def feed(own, w_gu, w_dn, grads, identity):
    tokens, half = own.shape
    units, width = w_dn.shape
    places = lax.axis_size("p")
    whole = (PLANES, tokens, width)
    return call(
        feed_kernel,
        identity,
        55,
        [
            shape(whole, BF16),
            shape(whole, BF16),
            shape((places, PLANES, width // (PLANES * places), 2 * units), BF16),
            shape(w_dn.shape, BF16),
        ],
        [
            pltpu.VMEM(whole, BF16),
            pltpu.VMEM(w_gu.shape, BF16),
            pltpu.VMEM(w_dn.shape, BF16),
            pltpu.VMEM(whole, BF16),
            pltpu.VMEM(w_gu.shape, F32),
            pltpu.VMEM(w_dn.shape, F32),
            pltpu.VMEM((tokens, 2 * units), F32),
            pltpu.VMEM((tokens, -(-units // LANES) * LANES), F32),
            pltpu.VMEM((tokens, units), BF16),
            pltpu.VMEM((tokens, 2 * units), BF16),
            pltpu.VMEM((2, 2, tokens, width), BF16),
            DMA((3,)),
            DMA,
            DMA((2, 2)),
            DMA((PLANES * places,)),
        ]
        + gather_scratch(),
        [own, w_gu, w_dn, grads],
        (1, 2, 3),
        (0, 1, 2, 3),
    )


def row_sems(rows):
    places = lax.axis_size("p")
    sems = [DMA((places,)), DMA((places,)), DMA, DMA((places,)), DMA((rows,)), DMA]
    return sems + [DMA((PLANES,)), DMA((PLANES,)), DMA]


def attend_back_alone(grad_mix, w_out, attended, seq, lens, att, norms, blocks, rows, identity):
    places = lax.axis_size("p")
    positions = grad_mix.shape[1] // rows
    wide = w_out.shape[0]
    width = seq.shape[-1]
    return call(
        attend_back_kernel,
        identity,
        35,
        [
            shape((PLANES, rows, positions, width), BF16),
            shape(blocks.shape, BF16),
            shape((places, wide // places, grad_mix.shape[2]), BF16),
        ],
        [
            pltpu.VMEM((PLANES, rows, positions, wide), BF16),
            pltpu.VMEM(seq.shape[:-1] + (wide,), BF16),
            pltpu.VMEM(seq.shape, BF16),
            pltpu.VMEM((att.shape[0], wide + LANES), F32),
        ]
        + row_sems(rows),
        [grad_mix, w_out, attended, seq, lens, att, norms, blocks],
        (7,),
        (1,),
    )


def mix_back(part, resid, inverse, gains, cotangent, fed, identity):
    tokens, half = resid.shape
    whole = (PLANES, tokens, 2 * half)
    return call(
        back_kernel,
        identity,
        95,
        [
            shape(whole, BF16),
            shape((tokens, half), F32),
            shape((1, half), F32),
            shape((tokens, half), BF16),
        ],
        [pltpu.VMEM(whole, BF16), pltpu.VMEM(whole, BF16)]
        + sums_scratch(tokens, 1)
        + [DMA((2,)), pltpu.VMEM((tokens, half), F32)]
        + gather_scratch() * PARTS
        + scatter_scratch(tokens // PARTS, half) * 2 * PARTS,
        [part, resid, inverse, gains, cotangent, fed],
        (0, 5),
    )


def last_back(grad_qkv, w_qkv, normed, tokens, gains, resid_grad, parts_out, joined, gain_two, units, identity):
    size, half = tokens.shape
    places = lax.axis_size("p")
    count = PLANES * places
    own_rows, width = w_qkv.shape[2:]
    slim = (width - parts_out.shape[0] * parts_out.shape[1]) // 2
    blocks = (PLANES, own_rows, width)
    outs = [
        (size, half),
        parts_out.shape[1:],
        (own_rows, PLANES * slim),
        (own_rows, PLANES * slim),
        (own_rows, PLANES * (width - 2 * slim)),
        (units, own_rows),
        (units, own_rows),
        (8, LANES),
    ]
    return call(
        last_kernel,
        identity,
        60,
        [shape(dims, F32) for dims in outs],
        [
            pltpu.VMEM((PLANES, size, 2 * half), BF16),
            pltpu.VMEM((PLANES, places, own_rows, width), BF16),
            pltpu.VMEM((8, half), F32),
            pltpu.VMEM((count, 8, LANES), F32),
        ]
        + sums_scratch(size, 2)
        + [
            pltpu.VMEM(parts_out.shape, BF16),
            pltpu.VMEM((places,) + blocks, BF16),
            pltpu.VMEM(blocks, BF16),
            pltpu.VMEM(blocks, BF16),
            DMA((3,)),
        ]
        + [DMA((places,)) for _ in range(4)]
        + [DMA((PLANES,)) for _ in range(2)]
        + [DMA((count,)) for _ in range(2)]
        + scatter_scratch(size // PARTS, half) * PARTS,
        [grad_qkv, w_qkv, normed, tokens, gains, resid_grad, parts_out, joined, gain_two],
    )


def end(far, near, units, identity):
    resid, seq, att, w_qkv = near[0], near[7], near[9], near[11]
    tokens, half = resid.shape
    places = lax.axis_size("p")
    count = PLANES * places
    rows = near[8].shape[0]
    positions = tokens // rows
    own_rows, width = w_qkv.shape[2:]
    wide = att.shape[1]
    slim = (width - wide) // 2
    whole = (PLANES, tokens, 2 * half)
    blocks = (PLANES, own_rows, width)
    gu = far[2].shape
    outs = [
        ((tokens, half), BF16),
        ((tokens, half), F32),
        ((wide // places, 2 * half), F32),
        ((own_rows, PLANES * slim), F32),
        ((own_rows, PLANES * slim), F32),
        ((own_rows, PLANES * wide), F32),
        ((units, own_rows), F32),
        ((units, own_rows), F32),
        ((8, LANES), F32),
    ]
    parts_out = (places, wide // places, 2 * half)
    scratch = [
        (whole, BF16),
        (whole, BF16),
        (whole, BF16),
        ((tokens, half), F32),
        ((tokens, half), F32),
        (gu, BF16),
        (gu[1:], BF16),
        (gu[1:], BF16),
        ((PLANES, rows, positions, wide), BF16),
        ((PLANES, places, positions, wide), BF16),
        (seq.shape, BF16),
        ((att.shape[0], wide + LANES), F32),
        ((PLANES, rows, positions, width), BF16),
        (parts_out, BF16),
        (parts_out, BF16),
        ((PLANES, places, own_rows, width), BF16),
        ((places,) + blocks, BF16),
        (blocks, BF16),
        (blocks, BF16),
        ((8, half), F32),
        ((count, 8, LANES), F32),
        ((tokens, LANES), F32),
        ((tokens, LANES), F32),
        ((tokens, 2 * LANES), F32),
        ((tokens, 2 * LANES), F32),
    ]
    sems = [(2,), (2,), (3,), (places,), (places,), (), (PLANES,), (PLANES,)]
    sems += [(PLANES, places), (PLANES, places), (PLANES,), (places,), (rows,), ()]
    sems += [(places,)] * 4 + [(PLANES,)] * 2 + [(count,)] * 2 + [(4,)]
    return call(
        end_kernel,
        identity,
        190,
        [shape(dims, kind) for dims, kind in outs],
        [pltpu.VMEM(dims, kind) for dims, kind in scratch]
        + [DMA(dims) if dims else DMA for dims in sems]
        + gather_scratch() * PARTS
        + scatter_scratch(tokens // PARTS, half) * 2 * PARTS
        + scatter_sems() * PARTS,
        [*far, *near],
        (0, 1, 2, 3),
    )


def end_in_parts(far, near, units, identities):
    part, fed, parts_gu, normed_one = far
    resid, inverse, gains, cotangent, tokens, w_out, attended, seq, lens, att, norms, w_qkv = near
    rows = lens.shape[0]
    blocks_gu = lax.psum_scatter(parts_gu, "p", scatter_dimension=0, tiled=False)
    grad_mix, grad_resid, gain_two, mixed = mix_back(
        part, resid, inverse, gains, cotangent, fed, identities[0]
    )
    grad_qkv, blocks_gu, out_output = attend_back_alone(
        grad_mix, w_out, attended, seq, lens, att, norms, blocks_gu, rows, identities[1]
    )
    grad_qkv = grad_qkv.reshape(PLANES, -1, grad_qkv.shape[-1])
    rest = last_back(
        grad_qkv,
        w_qkv,
        normed_one,
        tokens,
        gains,
        grad_resid,
        out_output,
        blocks_gu,
        gain_two,
        units,
        identities[2],
    )
    return (mixed, *rest)


def dot(left, right, dims=((1,), (0,))):
    return lax.dot_general(left, right, (dims, ((), ())), preferred_element_type=F32)


def pad_units(weights, axis, chunk, padded):
    shape = weights.shape
    weights = weights.reshape(shape[:axis] + (-1, chunk) + shape[axis + 1 :])
    pads = [(0, 0)] * weights.ndim
    pads[axis + 1] = (0, padded - chunk)
    return jnp.pad(weights, pads).reshape(shape[:axis] + (-1,) + shape[axis + 1 :])


def on_device(
    tokens,
    lengths,
    attn_gain,
    w_query,
    w_key,
    w_value,
    w_output,
    ffn_gain,
    w_gate,
    w_up,
    w_down,
    cotangent,
):
    plane, place, core = (lax.axis_index(name) for name in ("z", "p", "core"))
    count = lax.axis_size("p")
    batches, per_batch, own_len, half = tokens.shape
    rows = batches * per_batch
    own_rows = w_query.shape[0]
    heads = w_query.shape[1] // FEAT // PLANES
    chunk = w_down.shape[0]
    padded = -(-chunk // 16) * 16
    units = count * padded
    slim, broad = heads * FEAT, heads * HEAD_V

    own_gain = attn_gain.shape[0]
    index = plane * count + place
    x_half = tokens.reshape(rows * own_len, half)
    c_half = cotangent.reshape(rows * own_len, half)
    lens = jnp.broadcast_to(lengths.reshape(-1)[:, None], (rows, LANES))
    w_dn = lax.all_gather(pad_units(w_down, 0, chunk, padded), "p", axis=0, tiled=True)
    (
        normed_one,
        w_qkv,
        gains,
        att,
        norms,
        attended,
        seq,
        w_gu,
        w_out,
        normed_two,
        resid,
        inv_two,
        c_all,
    ) = front(
        x_half,
        c_half,
        attn_gain[None],
        ffn_gain[None],
        w_query,
        w_key,
        w_value,
        w_gate.T,
        w_up.T,
        w_output,
        lens,
        units,
        0,
    )
    attended = attended.reshape(PLANES, -1, broad)
    w_gu = w_gu.reshape(-1, 2 * units)
    w_out = w_out.reshape(broad, -1)
    part, fed, out_gu, out_down = feed(normed_two, w_gu, w_dn, c_all, 1)
    out_down = lax.psum_scatter(out_down, "p", scatter_dimension=0, tiled=True)
    names = (resid, inv_two, gains, c_half, x_half, w_out, attended, seq, lens, att, norms, w_qkv)
    if PLANES * count * own_len <= MERGED_LENGTH:
        ends = end((part, fed, out_gu, normed_one), names, w_gate.shape[1], 2)
    else:
        ends = end_in_parts((part, fed, out_gu, normed_one), names, w_gate.shape[1], (4, 5, 6))
    mixed, grad_tokens, out_output, out_query, out_key, out_value, out_gate, out_up, out_gains = ends
    at = (index * 2 + core) * own_gain
    out_gains = lax.dynamic_slice_in_dim(out_gains, lax.rem(at, LANES), own_gain, axis=1)
    return (
        mixed.reshape(tokens.shape),
        grad_tokens.reshape(tokens.shape),
        out_gains[0],
        out_query,
        out_key,
        out_value,
        out_output,
        out_gains[1],
        out_gate.T,
        out_up.T,
        out_down[:chunk].astype(F32),
    )


def solution(mesh):
    split = Mesh(mesh.devices.reshape(PLANES, -1, 2), ("z", "p", "core"))
    seq = ("z", "p")
    both = ("z", "p", "core")
    rows, columns = P(seq, "core"), P(("core", "z", "p"), None)
    tokens = P(None, None, seq, "core")
    return jax.shard_map(
        on_device,
        mesh=split,
        in_specs=(
            tokens,
            P(),
            P(both),
            rows,
            rows,
            rows,
            columns,
            P(both),
            rows,
            rows,
            columns,
            tokens,
        ),
        out_specs=(
            tokens,
            tokens,
            P(both),
            rows,
            rows,
            rows,
            columns,
            P(both),
            rows,
            rows,
            columns,
        ),
        check_vma=False,
    )
```

```python
import jax
import jax.numpy as jnp
from jax import lax
from jax.experimental import pallas as pl
from jax.experimental.pallas import tpu as pltpu
from jax.sharding import Mesh
from jax.sharding import PartitionSpec as P

FEAT = 16
HEAD_V = 128
PLANES = 4
LANES = 128
EPSILON = 1e-05
F32 = jnp.float32
BF16 = jnp.bfloat16
MESH = pl.DeviceIdType.MESH
DMA = pltpu.SemaphoreType.DMA
VMEM_LIMIT = 60 << 20
QUERY_BLOCK = 256
MERGED_LENGTH = 1024
PARTS = 2
TILE = 256
ROW_BLOCK = 32


def remote(source, target, send, receive, device):
    return pltpu.make_async_remote_copy(
        src_ref=source,
        dst_ref=target,
        send_sem=send,
        recv_sem=receive,
        device_id=device,
        device_id_type=MESH,
    )


def here():
    return tuple(lax.axis_index(name) for name in ("z", "p", "core"))


def signal(semaphore, device):
    pl.semaphore_signal(semaphore, inc=1, device_id=device, device_id_type=MESH)


def greet_column():
    plane, place, core = here()
    barrier = pltpu.get_barrier_semaphore()
    signal(barrier, (plane, place, 1 - core))
    pl.when(plane > 0)(lambda: signal(barrier, (plane - 1, place, core)))
    pl.when(plane < PLANES - 1)(lambda: signal(barrier, (plane + 1, place, core)))
    inner = (plane > 0).astype(jnp.int32) + (plane < PLANES - 1).astype(jnp.int32)
    return lambda: pl.semaphore_wait(barrier, 1 + inner)


def greet_same():
    plane, place, core = here()
    places = lax.axis_size("p")
    barrier = pltpu.get_barrier_semaphore()
    signal(barrier, (plane, place, 1 - core))
    for step in range(1, PLANES * places):
        signal(barrier, peer(step) + (core,))
    return lambda: pl.semaphore_wait(barrier, PLANES * places)


def greet_all():
    plane, place, core = here()
    count = PLANES * lax.axis_size("p")
    barrier = pltpu.get_barrier_semaphore()
    signal(barrier, (plane, place, 1 - core))
    for step in range(1, count):
        signal(barrier, peer(step) + (core,))
        signal(barrier, peer(step) + (1 - core,))
    return lambda: pl.semaphore_wait(barrier, 2 * count - 1)


def greet_cross():
    plane, place, core = here()
    places = lax.axis_size("p")
    barrier = pltpu.get_barrier_semaphore()
    for step in range(1, places):
        signal(barrier, (plane, lax.rem(place + step, places), core))
    for step in range(1, PLANES):
        signal(barrier, (lax.rem(plane + step, PLANES), place, core))
    return lambda: pl.semaphore_wait(barrier, places + PLANES - 2)


def peer(step):
    plane, place, _ = here()
    places = lax.axis_size("p")
    index = lax.rem(plane * places + place + step, PLANES * places)
    return lax.div(index, places), lax.rem(index, places)


def halves(width):
    core = lax.axis_index("core")
    half = width // 2
    return (
        pl.ds(pl.multiple_of(core * half, LANES), half),
        pl.ds(pl.multiple_of((1 - core) * half, LANES), half),
    )


def in_turn(*steps):
    steps = list(steps)
    while steps:
        steps = [one for one in steps if next(one, steps) is not steps]


def gather_scratch():
    return [DMA((PLANES,)) for _ in range(5)]


class Gather:
    def __init__(self, out, sems):
        self.out = out
        self.arrive, self.across, self.up, self.down, self.over = sems
        self.plane, self.place, self.core = here()
        self.mine, self.other = halves(out.shape[2])

    def send(self, block, sems, receive, device):
        piece = self.out.at[block, :, self.mine]
        return remote(piece, piece, sems.at[block], receive.at[block], device)

    def rise(self, block):
        return self.send(block, self.up, self.arrive, (self.plane + 1, self.place, self.core))

    def fall(self, block):
        return self.send(block, self.down, self.arrive, (self.plane - 1, self.place, self.core))

    def cross(self, block):
        return self.send(block, self.over, self.across, (self.plane, self.place, 1 - self.core))

    def start(self):
        plane = self.plane
        pl.when(plane < PLANES - 1)(lambda: self.rise(plane).start())
        pl.when(plane > 0)(lambda: self.fall(plane).start())
        self.cross(plane).start()

    def landed(self, block):
        partner = (self.plane, self.place, 1 - self.core)
        self.send(block, self.over, self.arrive, partner).wait_recv()

    def pass_on(self, far):
        plane = self.plane

        @pl.when(plane >= far)
        def _():
            self.landed(plane - far)
            pl.when(plane < PLANES - 1)(lambda: self.rise(plane - far).start())
            self.cross(plane - far).start()

        @pl.when(plane + far < PLANES)
        def _():
            self.landed(plane + far)
            pl.when(plane > 0)(lambda: self.fall(plane + far).start())
            self.cross(plane + far).start()

    def whole(self, block):
        piece = self.out.at[block, :, self.other]
        partner = (self.plane, self.place, 1 - self.core)
        remote(piece, piece, self.over.at[block], self.across.at[block], partner).wait_recv()

    def finish(self):
        plane = self.plane
        for block in range(PLANES):
            self.cross(block).wait_send()
            pl.when((plane < PLANES - 1) & (block <= plane))(lambda: self.rise(block).wait_send())
            pl.when((plane > 0) & (block >= plane))(lambda: self.fall(block).wait_send())

    def steps(self):
        self.start()
        yield
        for far in range(1, PLANES):
            self.pass_on(far)
            yield
        for block in range(PLANES):
            self.whole(block)
        self.finish()


def order_of_arrival(step):
    plane = lax.axis_index("z")
    nearest = [sorted(range(PLANES), key=lambda block: (abs(block - own), block)) for own in range(PLANES)]
    found = jnp.int32(0)
    for own in range(PLANES):
        for at in range(PLANES):
            found = jnp.where((plane == own) & (step == at), nearest[own][at], found)
    return found


def scatter_buffers(tokens, half):
    return [
        pltpu.VMEM((PLANES, tokens, half), BF16),
        pltpu.VMEM((PLANES + 1, tokens, half), BF16),
    ]


def scatter_sems():
    return [DMA((PLANES,)) for _ in range(6)]


def scatter_scratch(tokens, half):
    return scatter_buffers(tokens, half) + scatter_sems()


def column_scatter(part, scratch, total):
    twin, came, over_s, over_r, up_s, up_r, down_s, down_r = scratch
    plane, place, core = here()
    mine, other = halves(part.shape[2])

    def cross(block):
        return remote(
            part.at[block, :, other],
            twin.at[block],
            over_s.at[block],
            over_r.at[block],
            (plane, place, 1 - core),
        )

    def rise(block):
        return remote(
            came.at[block], came.at[block], up_s.at[block], up_r.at[block], (plane + 1, place, core)
        )

    def fall(block):
        last = jnp.where(block == plane - 1, PLANES, block)
        return remote(
            came.at[block], came.at[last], down_s.at[block], down_r.at[block], (plane - 1, place, core)
        )

    def own(block):
        return part[block, :, mine].astype(F32) + twin[block].astype(F32)

    def pass_on(block, link, first):
        cross(block).wait_recv()

        @pl.when(jnp.logical_not(first))
        def _():
            link(block).wait_recv()
            came[block] = (own(block) + came[block].astype(F32)).astype(BF16)

        @pl.when(first)
        def _():
            came[block] = own(block).astype(BF16)

        link(block).start()

    for far in range(PLANES - 1, 0, -1):
        pl.when(plane + far < PLANES)(lambda: cross(plane + far).start())
        pl.when(plane >= far)(lambda: cross(plane - far).start())
    cross(plane).start()
    yield
    for far in range(PLANES - 1, 0, -1):
        pl.when(plane + far < PLANES)(lambda: pass_on(plane + far, rise, plane == 0))
        pl.when(plane >= far)(lambda: pass_on(plane - far, fall, plane == PLANES - 1))
        yield
    cross(plane).wait_recv()
    total[...] = own(plane)

    @pl.when(plane > 0)
    def _():
        rise(plane).wait_recv()
        total[...] += came[plane].astype(F32)

    @pl.when(plane < PLANES - 1)
    def _():
        fall(plane).wait_recv()
        total[...] += came[PLANES].astype(F32)

    for block in range(PLANES):
        cross(block).wait_send()
        pl.when(block > plane)(lambda: rise(block).wait_send())
        pl.when(block < plane)(lambda: fall(block).wait_send())


def gathers(out, scratch):
    size = out.shape[1] // PARTS
    return [
        Gather(out.at[:, pl.ds(at * size, size)], scratch[5 * at : 5 * at + 5]).steps()
        for at in range(PARTS)
    ]


def scatters(part, scratch, total):
    size = part.shape[1] // PARTS
    return [
        column_scatter(
            part.at[:, pl.ds(at * size, size)],
            scratch[8 * at : 8 * at + 8],
            total.at[pl.ds(at * size, size)],
        )
        for at in range(PARTS)
    ]


def fold(values):
    return sum(values[:, at : at + LANES] for at in range(0, values.shape[1], LANES))


def both_cores(local, far, send, receive):
    plane, place, core = here()
    copy = remote(local, far, send, receive, (plane, place, 1 - core))
    copy.start()
    copy.wait()
    joined = local[...] + far[...]
    return [
        jnp.sum(joined[:, at : at + LANES], axis=1, keepdims=True)
        for at in range(0, joined.shape[1], LANES)
    ]


def turn_copies(blocks, spread, send, receive):
    plane, place, core = here()
    copies = []
    for step in range(1, PLANES):
        to = lax.rem(plane + step, PLANES)
        copies.append(
            remote(blocks.at[to], spread.at[plane], send.at[step], receive.at[step], (to, place, core))
        )
    return copies


def pack_units(weights, places, plane, padded):
    size = weights.shape[0] // PLANES
    chunk = size // places
    turned = weights[pl.ds(pl.multiple_of(plane * size, 16), size), :].astype(F32).T
    blank = jnp.zeros((turned.shape[0], padded - chunk), F32)
    pieces = []
    for place in range(places):
        pieces += [turned[:, place * chunk : (place + 1) * chunk], blank]
    return jnp.concatenate(pieces, axis=1)


def unpack_units(weights, places, padded, chunk):
    pieces = [weights[:, place * padded : place * padded + chunk] for place in range(places)]
    return jnp.concatenate(pieces, axis=1).T


def front_kernel(
    own,
    other,
    gain_one,
    gain_two,
    w_query,
    w_key,
    w_value,
    w_gate,
    w_up,
    w_output,
    lens,
    normed_one,
    far_weights,
    gains,
    far_att,
    far_norms,
    attended,
    far_seq,
    w_gu,
    far_out,
    normed,
    resid,
    inverse,
    whole_c,
    weights,
    att,
    norms,
    seq,
    w_out,
    whole,
    normed_in,
    qkv,
    blocks,
    spread,
    tile,
    pair,
    twin,
    tiles,
    joined,
    turned,
    low,
    part,
    local,
    far_sums,
    sum_s,
    sum_r,
    stay,
    swap_s,
    swap_r,
    turn_s,
    turn_r,
    gain_s,
    gain_r,
    spread_s,
    spread_r,
    out_s,
    out_r,
    row_s,
    row_r,
    row_l,
    back_s,
    back_r,
    back_l,
    gu_s,
    gu_r,
    gu_l,
    pass_s,
    pass_r,
    pass_l,
    keep_n,
    write,
    *rest,
):
    plane, place, core = here()
    places = lax.axis_size("p")
    count = PLANES * places
    index = plane * places + place
    width = whole.shape[2]
    mine, _ = halves(width)
    rows = attended.shape[1]
    per_row = places // rows
    gather = Gather(whole, rest[:5])
    greeted = greet_same()

    keep = pltpu.make_async_copy(own, whole.at[plane, :, mine], stay.at[0])
    keep.start()
    keep_c = pltpu.make_async_copy(other, whole_c.at[plane, :, mine], stay.at[1])
    keep_c.start()
    own_gain = gain_one.shape[1]
    tile[...] = jnp.zeros_like(tile)
    tile[0:1, :own_gain] = gain_one[...].astype(F32)
    tile[1:2, :own_gain] = gain_two[...].astype(F32)
    tile[...] = pltpu.roll(tile[...], lax.rem((2 * index + core) * own_gain, LANES), 1)
    wide = w_value.shape[1] // PLANES
    slim = w_query.shape[1] // PLANES
    for to in range(PLANES):
        pieces = [
            w_value[:, to * wide : (to + 1) * wide],
            w_query[:, to * slim : (to + 1) * slim],
            w_key[:, to * slim : (to + 1) * slim],
        ]
        joint = jnp.concatenate([piece.astype(F32) for piece in pieces], axis=1)
        blocks[to] = joint.astype(BF16)
    keep.wait()
    greeted()

    swap = remote(tile, twin, swap_s, swap_r, (plane, place, 1 - core))
    swap.start()
    turns = turn_copies(blocks, spread, turn_s, turn_r)
    for copy in turns:
        copy.start()
    gather.start()
    own_block = pltpu.make_async_copy(blocks.at[plane], spread.at[plane], stay.at[2])
    own_block.start()
    swap.wait()
    pair[...] = tile[...] + twin[...]
    tiles[index] = pair[...]
    sends = []
    for step in range(1, count):
        sends.append(
            remote(pair, tiles.at[index], gain_s.at[step], gain_r.at[step], peer(step) + (core,))
        )
        sends[-1].start()
    own_block.wait()
    for copy in turns:
        copy.wait()
    around = [
        pltpu.make_async_copy(spread, weights.at[:, place], stay.at[3]),
        pltpu.make_async_copy(w_output, w_out.at[place], stay.at[4]),
    ]
    for step in range(1, places):
        to = (plane, lax.rem(place + step, places), core)
        around.append(
            remote(spread, weights.at[:, place], spread_s.at[step], spread_r.at[step], to)
        )
        around.append(remote(w_output, w_out.at[place], out_s.at[step], out_r.at[step], to))
    for copy in around:
        copy.start()

    units = joined.shape[2] // 2
    padded = units // places
    broad = units // LANES * LANES

    def lay_out(to):
        gate = pack_units(w_gate, places, to, padded)
        up = pack_units(w_up, places, to, padded)
        joined[to, :, :broad] = gate[:, :broad].astype(BF16)
        joined[to, :, broad : 2 * broad] = up[:, :broad].astype(BF16)
        if units > broad:
            joined[to, :, 2 * broad :] = jnp.concatenate(
                [gate[:, broad:], up[:, broad:]], axis=1
            ).astype(BF16)

    def passed(step):
        block = lax.rem(plane - step + PLANES, PLANES)
        source = joined.at[plane] if step == 0 else turned.at[block]
        target = w_gu.at[block, place]
        copies = [pltpu.make_async_copy(source, target, pass_l.at[step])]
        for side in range(1, places):
            to = (plane, lax.rem(place + side, places), core)
            copies.append(
                remote(source, target, pass_s.at[step, side], pass_r.at[step, side], to)
            )
        return copies

    lay_out(plane)
    for copy in passed(0):
        copy.start()
    for step in range(1, PLANES):
        lay_out(lax.rem(plane + step, PLANES))

    gu_turns = turn_copies(joined, turned, gu_s, gu_r)

    def inward(step):
        to = lax.rem(plane + step, PLANES)
        return (jnp.abs(to - plane) == 1) & (to > 0) & (to < PLANES - 1)

    for step in range(1, PLANES):
        pl.when(inward(step))(gu_turns[step - 1].start)
    gather.pass_on(1)
    for copy in sends + around:
        copy.wait()
    each = width // count
    for at in range(0, width, LANES):
        group = range(at // each, (at + LANES) // each)
        gains[:, at : at + LANES] = sum(tiles[source] for source in group)
    gain = gains[0:1, :]

    def row_copy(block, step):
        to = lax.rem(place + step, places)
        return remote(
            qkv.at[block, lax.div(to, per_row)],
            seq.at[block, place],
            row_s.at[block, step],
            row_r.at[block, step],
            (plane, to, core),
        )

    def own_row(block):
        return pltpu.make_async_copy(
            qkv.at[block, lax.div(place, per_row)], seq.at[block, place], row_l.at[block]
        )

    def project(block):
        gather.whole(block)
        values = whole[block].astype(F32)
        scale = lax.rsqrt(jnp.mean(values * values, axis=1, keepdims=True) + EPSILON)
        normed_in[block] = (values * scale * gain).astype(BF16)
        pltpu.make_async_copy(normed_in.at[block], normed_one.at[block], keep_n.at[block]).start()
        flat_weights = weights[...].reshape(width, qkv.shape[3])
        qkv[block] = dot(normed_in[block], flat_weights).astype(BF16).reshape(qkv.shape[1:])
        for step in range(1, places):
            row_copy(block, step).start()
        own_row(block).start()

    project(order_of_arrival(0))
    for far in range(2, PLANES):
        gather.pass_on(far)
        project(order_of_arrival(far - 1))

    for step in range(1, PLANES):
        pl.when(jnp.logical_not(inward(step)))(gu_turns[step - 1].start)
    project(order_of_arrival(PLANES - 1))
    gather.finish()

    alive = alive_of(lens, att.shape[0], rows).astype(BF16)
    for block in range(PLANES):
        for step in range(1, places):
            row_copy(block, step).wait()
        own_row(block).wait()
    attend(seq, alive, att, norms)
    low[...] = att[...].astype(BF16).reshape(low.shape)
    finish = start_back(low, attended, back_s, back_r, back_l)
    finish()
    pairs = [
        (weights, far_weights),
        (att, far_att),
        (norms, far_norms),
        (seq, far_seq),
        (w_out, far_out),
    ]
    writes = [
        pltpu.make_async_copy(source, target, write.at[at])
        for at, (source, target) in enumerate(pairs)
    ]
    for copy in writes:
        copy.start()
    tokens = whole.shape[1]
    flat_out = w_out[...].reshape(-1, width)
    for block in range(PLANES):
        rows_in = attended[block].reshape(tokens, flat_out.shape[0])
        part[block] = dot(rows_in, flat_out).astype(BF16)

    def gu_flow():
        for step in range(1, PLANES):
            gu_turns[step - 1].wait()
            for copy in passed(step):
                copy.start()
            yield

    keep_c.wait()
    two = 5 + 5 * PARTS
    in_turn(*scatters(part, rest[two:], resid), *gathers(whole_c, rest[5:two]), gu_flow())
    resid[...] += own[...].astype(F32)
    local[...] = fold(resid[...] * resid[...])
    (total,) = both_cores(local, far_sums, sum_s, sum_r)
    scale = lax.rsqrt(total / width + EPSILON)
    inverse[...] = jnp.broadcast_to(scale, inverse.shape)
    normed[...] = (resid[...] * scale * gains[1:2, mine]).astype(BF16)
    for step in range(PLANES):
        for copy in passed(step):
            copy.wait()
        pltpu.make_async_copy(normed_in.at[step], normed_one.at[step], keep_n.at[step]).wait()
    for copy in writes:
        copy.wait()


def start_back(seq, out, send, receive, local):
    plane, place, core = here()
    places = lax.axis_size("p")
    rows = out.shape[1]
    per_row = places // rows
    row = lax.div(place, per_row)
    speaks = lax.rem(place, per_row) == 0

    def copy(step):
        to = lax.rem(place + step, places)
        return remote(
            seq.at[:, to], out.at[:, row], send.at[step], receive.at[row], (plane, to, core)
        )

    def stay():
        return pltpu.make_async_copy(seq.at[:, place], out.at[:, row], local)

    @pl.when(speaks)
    def _():
        for step in range(1, places):
            copy(step).start()
        stay().start()

    def finish():
        @pl.when(speaks)
        def _():
            stay().wait()
            for step in range(1, places):
                copy(step).wait_send()

        for other in range(rows):

            @pl.when(other * per_row != place)
            def _():
                remote(
                    out.at[:, other],
                    out.at[:, other],
                    send.at[0],
                    receive.at[other],
                    (plane, lax.rem(place + 1, places), core),
                ).wait_recv()

    return finish


def flat(ref):
    block = ref[...]
    return block.reshape(-1, block.shape[-1])


def columns_of(seq, heads, head):
    wide = heads * HEAD_V
    slim = seq[:, wide : wide + 2 * heads * FEAT].astype(F32)
    queries = slim[:, head * FEAT : (head + 1) * FEAT].astype(BF16)
    keys = slim[:, (heads + head) * FEAT : (heads + head + 1) * FEAT].astype(BF16)
    return queries, keys, seq[:, head * HEAD_V : (head + 1) * HEAD_V]


def causal(start, stop, values):
    queries = start + lax.broadcasted_iota(jnp.int32, values.shape, 0)
    keys = lax.broadcasted_iota(jnp.int32, values.shape, 1)
    return jnp.where(queries >= keys, values, 0.0)


def alive_of(lens, length, rows):
    row = lax.div(lax.axis_index("p"), lax.axis_size("p") // rows)
    per_batch = lens.shape[1]
    found = lens[pl.ds(lax.div(row, per_batch), 1), :].astype(F32)
    column = lax.broadcasted_iota(jnp.int32, found.shape, 1)
    limit = jnp.sum(jnp.where(column == lax.rem(row, per_batch), found, 0.0), axis=1, keepdims=True)
    positions = lax.broadcasted_iota(jnp.int32, (length, LANES), 0).astype(F32)
    return jnp.where(positions < limit, 1.0, 0.0).astype(F32)


def attend(seq, alive, att, norms):
    everything = flat(seq)
    length = everything.shape[0]
    heads = att.shape[1] // HEAD_V
    block = min(QUERY_BLOCK, length)
    for head in range(heads):
        queries, keys, values = columns_of(everything, heads, head)
        values = jnp.concatenate([values * alive, alive], axis=1)
        wide = slice(head * HEAD_V, (head + 1) * HEAD_V)
        for start in range(0, length, block):
            stop = start + block
            scores = dot(queries[start:stop], keys[:stop], ((1,), (1,)))
            half = 1.0 + 0.25 * scores
            taylor = causal(start, stop, 0.5 + 0.5 * (half * half)).astype(BF16)
            sums = dot(taylor, values[:stop])
            norm = sums[:, HEAD_V:]
            ratio = sums[:, :HEAD_V] / norm
            att[start:stop, wide] = ratio
            norms[start:stop, wide] = norm


def attend_back(seq, alive, att, norms, rows, keep, low):
    everything = flat(seq)
    length = everything.shape[0]
    heads = att.shape[1] // HEAD_V
    block = min(QUERY_BLOCK, length)
    grads = flat(rows).astype(F32)
    grad_q, grad_k = [], []
    for head in range(heads):
        queries, keys, values = columns_of(everything, heads, head)
        live_keys = (keys.astype(F32) * alive[:, :FEAT]).astype(BF16)
        wide = slice(head * HEAD_V, (head + 1) * HEAD_V)
        grad = grads[:, wide]
        norm = norms[:, wide]
        grad_num = (grad / norm).astype(BF16)
        grad_norm = -jnp.sum(grad * att[:, wide] / norm, axis=1, keepdims=True)
        parts = []
        for start in range(0, length, block):
            stop = start + block
            scores = dot(queries[start:stop], keys[:stop], ((1,), (1,)))
            half = 1.0 + 0.25 * scores
            taylor = causal(start, stop, 0.5 + 0.5 * (half * half)).astype(BF16)
            inner = dot(grad_num[start:stop], values[:stop], ((1,), (1,))) + grad_norm[start:stop]
            slope = causal(start, stop, half * inner).astype(BF16)
            parts.append(dot(slope, live_keys[:stop]) * 0.25)
            from_values = dot(taylor, grad_num[start:stop], ((0,), (0,)))
            from_keys = dot(slope, queries[start:stop], ((0,), (0,)))
            if start:
                keep[:start, wide] += from_values[:start]
                keep[:start, heads * HEAD_V + head * FEAT : heads * HEAD_V + (head + 1) * FEAT] += (
                    from_keys[:start]
                )
            keep[start:stop, wide] = from_values[start:]
            keep[start:stop, heads * HEAD_V + head * FEAT : heads * HEAD_V + (head + 1) * FEAT] = (
                from_keys[start:]
            )
        grad_q.append(jnp.concatenate(parts, axis=0))
        keep[:, wide] *= alive
    wide = heads * HEAD_V
    keys = keep[:, wide : wide + heads * FEAT] * (0.25 * alive[:, : heads * FEAT])
    result = jnp.concatenate([keep[:, :wide]] + grad_q + [keys], axis=1)
    low[...] = result.astype(BF16).reshape(low.shape)


def feed_kernel(
    own,
    w_gu,
    w_dn,
    grads,
    part,
    fed,
    out_gu,
    out_dn,
    normed,
    held_gu,
    held_dn,
    held_c,
    sum_gu,
    sum_dn,
    gate_up,
    grad_hidden,
    hidden,
    grad_gu,
    stage,
    load,
    keep,
    store,
    ending,
    *sems,
):
    plane = lax.axis_index("z")
    mine, _ = halves(normed.shape[2])
    places = lax.axis_size("p")
    units = hidden.shape[1]
    broad = units // LANES * LANES
    rest = units - broad
    rows = normed.shape[1]
    loads = [
        pltpu.make_async_copy(w_gu, held_gu, load.at[0]),
        pltpu.make_async_copy(w_dn, held_dn, load.at[1]),
        pltpu.make_async_copy(grads, held_c, load.at[2]),
    ]
    for copy in loads:
        copy.start()
    gather = Gather(normed, sems)
    greeted = greet_column()
    stay = pltpu.make_async_copy(own, normed.at[plane, :, mine], keep)
    stay.start()
    stay.wait()
    greeted()
    gather.start()
    sum_gu[...] = jnp.zeros_like(sum_gu)
    sum_dn[...] = jnp.zeros_like(sum_dn)
    for copy in loads:
        copy.wait()

    def tiles(width):
        return [slice(at, min(at + TILE, width)) for at in range(0, width, TILE)]

    def stores(block, slot):
        return (
            pltpu.make_async_copy(stage.at[0, slot], fed.at[block], store.at[0, slot]),
            pltpu.make_async_copy(stage.at[1, slot], part.at[block], store.at[1, slot]),
        )

    def middle(at):
        here_rows = pl.ds(pl.multiple_of(at * ROW_BLOCK, ROW_BLOCK), ROW_BLOCK)

        def parts(gate, up, above):
            sigmoid = jax.nn.sigmoid(gate)
            silu = gate * sigmoid
            slope = sigmoid * (1.0 + gate * (1.0 - sigmoid))
            return silu * up, above * up * slope, above * silu

        both = gate_up[here_rows, :]
        above = grad_hidden[here_rows, :]
        first, second, third = parts(
            both[:, :broad], both[:, broad : 2 * broad], above[:, :broad]
        )
        hidden[here_rows, :broad] = first.astype(BF16)
        grad_gu[here_rows, :broad] = second.astype(BF16)
        grad_gu[here_rows, broad : 2 * broad] = third.astype(BF16)
        if rest:
            last = both[:, 2 * broad :]
            turned = pltpu.roll(last, rest, 1)
            first, second, third = parts(last, turned, above[:, broad : broad + LANES])
            hidden[here_rows, broad:] = first[:, :rest].astype(BF16)
            lane = lax.broadcasted_iota(jnp.int32, last.shape, 1)
            joined = jnp.where(lane < rest, second, pltpu.roll(third, rest, 1))
            grad_gu[here_rows, 2 * broad :] = joined.astype(BF16)

    def through(step, carry):
        pl.when(step > 0)(lambda: gather.pass_on(step))
        block = order_of_arrival(step)
        slot = lax.rem(step, 2)
        gather.whole(block)
        for cut in tiles(2 * units):
            gate_up[:, cut] = dot(normed[block], held_gu[:, cut])
        grad_hidden[:, :units] = dot(held_c[block], held_dn[...], ((1,), (1,)))
        lax.fori_loop(0, rows // ROW_BLOCK, lambda at, none: (middle(at), none)[1], 0)

        @pl.when(step >= 2)
        def _():
            for copy in stores(order_of_arrival(step - 2), slot):
                copy.wait()

        for cut in tiles(normed.shape[2]):
            stage[0, slot, :, cut] = dot(hidden[...], held_dn[:, cut]).astype(BF16)
            stage[1, slot, :, cut] = dot(grad_gu[...], held_gu[cut, :], ((1,), (1,))).astype(BF16)
        for copy in stores(block, slot):
            copy.start()
        for cut in tiles(normed.shape[2]):
            sum_gu[cut, :] += dot(normed[block, :, cut], grad_gu[...], ((0,), (0,)))
            sum_dn[:, cut] += dot(hidden[...], held_c[block, :, cut], ((0,), (0,)))
        return carry

    lax.fori_loop(0, PLANES, through, 0)
    own_rows = out_gu.shape[2]
    ends = []
    for block in range(normed.shape[2] // own_rows):
        cut = pl.ds(block * own_rows, own_rows)
        held_gu[cut, :] = sum_gu[cut, :].astype(BF16)
        ends.append(
            pltpu.make_async_copy(
                held_gu.at[cut], out_gu.at[block % places, block // places], ending.at[block]
            )
        )
        ends[-1].start()
    held_dn[...] = sum_dn[...].astype(BF16)
    ends.append(pltpu.make_async_copy(held_dn, out_dn, load.at[1]))
    ends[-1].start()
    for step in (PLANES - 2, PLANES - 1):
        for copy in stores(order_of_arrival(step), step % 2):
            copy.wait()
    for copy in ends:
        copy.wait()
    gather.finish()


def to_rows(values, seq, send, receive, local):
    plane, place, core = here()
    places = lax.axis_size("p")
    per_row = places // values.shape[1]
    copies = []
    for step in range(1, places):
        to = lax.rem(place + step, places)
        row = lax.div(to, per_row)
        copies.append(
            remote(
                values.at[:, row], seq.at[:, place], send.at[step], receive.at[step], (plane, to, core)
            )
        )
    copies.append(
        pltpu.make_async_copy(values.at[:, lax.div(place, per_row)], seq.at[:, place], local)
    )
    return copies


def attend_back_kernel(
    grad_mix,
    w_out,
    attended,
    seq,
    lens,
    att,
    norms,
    blocks,
    out,
    spread,
    out_output,
    grad_att,
    rows,
    low,
    keep,
    *sems,
):
    row_s, row_r, local, back_s, back_r, back_l, turn_s, turn_r, stay_s = sems
    plane = lax.axis_index("z")
    greeted = greet_cross()
    for block in range(PLANES):
        product = dot(grad_mix[block], w_out[...], ((1,), (1,))).astype(BF16)
        grad_att[block] = product.reshape(grad_att.shape[1:])
    greeted()
    copies = to_rows(grad_att, rows, row_s, row_r, local)
    for copy in copies:
        copy.start()
    turns = turn_copies(blocks, spread, turn_s, turn_r)
    turns.append(pltpu.make_async_copy(blocks.at[plane], spread.at[plane], stay_s))
    for copy in turns:
        copy.start()
    alive = alive_of(lens, att.shape[0], grad_att.shape[1])
    for at in range(0, grad_mix.shape[2], TILE):
        cut = slice(at, at + TILE)
        product = sum(
            dot(attended[block], grad_mix[block, :, cut], ((0,), (0,))) for block in range(PLANES)
        )
        out_output[:, :, cut] = product.astype(BF16).reshape(out_output.shape[:2] + (TILE,))
    for copy in copies:
        copy.wait()
    attend_back(seq, alive, att, norms, rows, keep, low)
    finish = start_back(low, out, back_s, back_r, back_l)
    for copy in turns:
        copy.wait()
    finish()


def back_kernel(
    far_part,
    resid,
    inverse,
    gains,
    cotangent,
    far_fed,
    low,
    grad,
    gain_sum,
    mixed,
    part,
    fed,
    local,
    far,
    send,
    receive,
    load,
    total_fed,
    *rest,
):
    plane = lax.axis_index("z")
    mine, _ = halves(part.shape[2])
    one, two = 5 * PARTS, 13 * PARTS
    greeted = greet_column()
    copies = [
        pltpu.make_async_copy(far_part, part, load.at[0]),
        pltpu.make_async_copy(far_fed, fed, load.at[1]),
    ]
    for copy in copies:
        copy.start()
    copies[0].wait()
    greeted()
    in_turn(*scatters(part, rest[one:two], grad))
    copies[1].wait()
    scale = inverse[:, :1]
    values, above = resid[...], grad[...]
    scaled = above * gains[1:2, mine]
    local[...] = fold(scaled * values)
    (total,) = both_cores(local, far, send, receive)
    mean = total / part.shape[2]
    grad[...] = cotangent[...].astype(F32) + scale * scaled - values * scale**3 * mean
    low[plane, :, mine] = grad[...].astype(BF16)
    in_turn(
        *gathers(low, rest[:one]),
        *scatters(fed, rest[two:], total_fed),
        keep_sum(gain_sum, above * values * scale),
    )
    mixed[...] = (total_fed[...] + resid[...]).astype(BF16)


def keep_sum(gain_sum, values):
    yield
    gain_sum[...] = jnp.sum(values, axis=0, keepdims=True)


def last_kernel(
    grad_qkv,
    w_qkv,
    normed,
    tokens,
    gains,
    resid_grad,
    parts_out,
    joined,
    gain_two,
    grad,
    sum_out,
    grad_query,
    grad_key,
    grad_value,
    grad_gate,
    grad_up,
    out_gains,
    part,
    parts_qkv,
    sums,
    came_gains,
    local,
    far,
    send,
    receive,
    came_out,
    came_qkv,
    blocks,
    spread,
    stay,
    out_s,
    out_r,
    qkv_s,
    qkv_r,
    turn_s,
    turn_r,
    own_s,
    own_r,
    *rest,
):
    plane, place, core = here()
    places = lax.axis_size("p")
    mine, _ = halves(part.shape[2])
    own_rows = parts_qkv.shape[2]
    greeted = greet_all()
    flat_weights = w_qkv[...].reshape(part.shape[2], grad_qkv.shape[2])
    for block in range(PLANES):
        part[block] = dot(grad_qkv[block], flat_weights, ((1,), (1,))).astype(BF16)
    greeted()
    outs, shares, moves = [], [], []
    for step in range(1, places):
        to = lax.rem(place + step, places)
        device = (plane, to, core)
        outs.append(
            remote(parts_out.at[to], came_out.at[place], out_s.at[step], out_r.at[step], device)
        )
        shares.append(
            remote(
                parts_qkv.at[:, to], came_qkv.at[place], qkv_s.at[step], qkv_r.at[step], device
            )
        )
    outs.append(pltpu.make_async_copy(parts_out.at[place], came_out.at[place], stay.at[0]))
    shares.append(pltpu.make_async_copy(parts_qkv.at[:, place], came_qkv.at[place], stay.at[1]))

    def lay_out(grads, first):
        units = joined.shape[2] // 2
        broad = units // LANES * LANES
        rest = units - broad
        size = grads.shape[0] // PLANES
        for to in range(PLANES):
            piece = joined[to].astype(F32)
            low = 2 * broad + (0 if first else rest)
            start = 0 if first else broad
            pieces = [piece[:, start : start + broad]]
            if rest:
                pieces.append(piece[:, low : low + rest])
            found = jnp.concatenate(pieces, axis=1)
            grads[to * size : (to + 1) * size, :] = unpack_units(
                found, places, units // places, size // places
            )

    def others():
        for copy in outs:
            copy.start()
        yield
        tokens_all = PLANES * normed.shape[1]
        grads = grad_qkv[...].reshape(tokens_all, grad_qkv.shape[2])
        for at in range(0, part.shape[2], TILE):
            left = normed[:, :, at : at + TILE].reshape(tokens_all, TILE)
            product = dot(left, grads, ((0,), (0,))).astype(BF16)
            for row in range(0, TILE, own_rows):
                owner = (at + row) // own_rows
                parts_qkv[owner // places, owner % places] = product[row : row + own_rows]
            if at + TILE == part.shape[2] // 2:
                yield
        for copy in shares:
            copy.start()
        yield
        lay_out(grad_gate, True)
        yield
        for copy in outs:
            copy.wait()
        sum_out[...] = sum(came_out[other].astype(F32) for other in range(places))
        for copy in shares:
            copy.wait()
        blocks[...] = sum(came_qkv[other].astype(F32) for other in range(places)).astype(BF16)
        moves.extend(turn_copies(blocks, spread, turn_s, turn_r))
        moves.append(pltpu.make_async_copy(blocks.at[plane], spread.at[plane], stay.at[2]))
        for copy in moves:
            copy.start()
        yield
        lay_out(grad_up, False)

    in_turn(*scatters(part, rest, grad), others())
    values, above = tokens[...].astype(F32), grad[...]
    scaled = above * gains[0:1, mine]
    local[:, :LANES] = fold(scaled * values)
    local[:, LANES:] = fold(values * values)
    total, square = both_cores(local, far, send, receive)
    scale = lax.rsqrt(square / part.shape[2] + EPSILON)
    sums[...] = jnp.zeros_like(sums)
    sums[0:1, :] = jnp.sum(above * values * scale, axis=0, keepdims=True)
    sums[1:2, :] = gain_two[...]
    finish = to_owners(sums, came_gains, own_s, own_r)
    mean = total / part.shape[2]
    grad[...] = resid_grad[...] + scale * scaled - values * scale**3 * mean
    for copy in moves:
        copy.wait()
    wide = grad_value.shape[1] // PLANES
    slim = grad_query.shape[1] // PLANES
    found = [spread[to].astype(F32) for to in range(PLANES)]
    for to in range(PLANES):
        grad_value[:, to * wide : (to + 1) * wide] = found[to][:, :wide]
    grad_query[...] = jnp.concatenate([one[:, wide : wide + slim] for one in found], axis=1)
    grad_key[...] = jnp.concatenate([one[:, wide + slim :] for one in found], axis=1)
    finish(out_gains)


def end_kernel(
    far_part,
    far_fed,
    parts_gu,
    far_normed,
    resid,
    inverse,
    gains,
    cotangent,
    tokens,
    far_out,
    far_attended,
    far_seq,
    lens,
    far_att,
    far_norms,
    far_qkv,
    mixed,
    grad,
    sum_out,
    grad_query,
    grad_key,
    grad_value,
    grad_gate,
    grad_up,
    out_gains,
    part,
    fed,
    low,
    resid_grad,
    total_fed,
    came_gu,
    blocks_gu,
    joined,
    grad_att,
    rows_in,
    rows_out,
    keep,
    grad_qkv,
    parts_out,
    came_out,
    parts_qkv,
    came_qkv,
    blocks,
    spread,
    sums,
    came_gains,
    w_out,
    attended,
    seq,
    att,
    norms,
    w_qkv,
    local,
    far,
    local_two,
    far_two,
    sum_s,
    sum_r,
    load,
    gu_s,
    gu_r,
    gu_l,
    turn_gu_s,
    turn_gu_r,
    row_s,
    row_r,
    row_l,
    back_s,
    back_r,
    back_l,
    out_s,
    out_r,
    qkv_s,
    qkv_r,
    turn_s,
    turn_r,
    own_s,
    own_r,
    stay,
    hold,
    *rest,
):
    plane, place, core = here()
    places = lax.axis_size("p")
    mine, _ = halves(part.shape[2])
    width = part.shape[2]
    own_rows = parts_qkv.shape[2]
    rows = grad_att.shape[1]
    per_row = places // rows
    size = part.shape[1] // PARTS
    cuts = [pl.ds(at * size, size) for at in range(PARTS)]
    gather_at, first_at, fed_at, last_at = (PARTS * n for n in (0, 5, 13, 21))
    buffers = [rest[first_at + 8 * at : first_at + 8 * at + 2] for at in range(PARTS)]
    last_sems = [rest[last_at + 6 * at : last_at + 6 * at + 6] for at in range(PARTS)]
    greeted = greet_all()
    loads = [
        pltpu.make_async_copy(far_part, part, load.at[0]),
        pltpu.make_async_copy(far_fed, fed, load.at[1]),
    ]
    pairs = [
        (far_out, w_out),
        (far_attended, attended),
        (far_seq, seq),
        (far_att, att),
        (far_norms, norms),
        (far_qkv, w_qkv),
    ]
    holds = [
        pltpu.make_async_copy(source, target, hold.at[at])
        for at, (source, target) in enumerate(pairs)
    ]
    for copy in loads + holds:
        copy.start()
    plane_gu = [pltpu.make_async_copy(parts_gu.at[place], came_gu.at[place], gu_l)]
    for step in range(1, places):
        to = lax.rem(place + step, places)
        plane_gu.append(
            remote(
                parts_gu.at[to], came_gu.at[place], gu_s.at[step], gu_r.at[step], (plane, to, core)
            )
        )
    loads[0].wait()
    greeted()
    for copy in plane_gu:
        copy.start()

    in_turn(*scatters(part, rest[first_at:fed_at], resid_grad))
    loads[1].wait()
    for copy in holds:
        copy.wait()
    scale = inverse[:, :1]
    values, above = resid[...], resid_grad[...]
    scaled = above * gains[1:2, mine]
    local[...] = fold(scaled * values)
    (total,) = both_cores(local, far, sum_s.at[0], sum_r.at[0])
    mean = total / width
    resid_grad[...] = cotangent[...].astype(F32) + scale * scaled - values * scale**3 * mean
    low[plane, :, mine] = resid_grad[...].astype(BF16)
    sums[...] = jnp.zeros_like(sums)

    def row_copy(block, step):
        to = lax.rem(place + step, places)
        return remote(
            grad_att.at[block, lax.div(to, per_row)],
            rows_in.at[block, place],
            row_s.at[block, step],
            row_r.at[block, step],
            (plane, to, core),
        )

    def own_row(block):
        return pltpu.make_async_copy(
            grad_att.at[block, lax.div(place, per_row)], rows_in.at[block, place], row_l.at[block]
        )

    all_lows = [
        Gather(low.at[:, cut], rest[gather_at + 5 * at : gather_at + 5 * at + 5])
        for at, cut in enumerate(cuts)
    ]

    def to_rows(block):
        for gather in all_lows:
            gather.whole(block)
        product = dot(low[block], w_out[...], ((1,), (1,))).astype(BF16)
        grad_att[block] = product.reshape(grad_att.shape[1:])
        for step in range(1, places):
            row_copy(block, step).start()
        own_row(block).start()

    def lows():
        for gather in all_lows:
            gather.start()
        yield
        sums[1:2, :] = jnp.sum(above * values * scale, axis=0, keepdims=True)
        for step in range(1, PLANES):
            for gather in all_lows:
                gather.pass_on(step)
            to_rows(order_of_arrival(step - 1))
            yield
        to_rows(order_of_arrival(PLANES - 1))
        for gather in all_lows:
            gather.finish()

    in_turn(lows(), *scatters(fed, rest[fed_at:last_at], total_fed))
    mixed[...] = (total_fed[...] + resid[...]).astype(BF16)
    normed_load = pltpu.make_async_copy(far_normed, fed, load.at[2])
    normed_load.start()
    for copy in plane_gu:
        copy.wait()
    for to in range(PLANES):
        total_gu = sum(came_gu[other, to].astype(F32) for other in range(places))
        blocks_gu[to] = total_gu.astype(BF16)
    gu_turns = turn_copies(blocks_gu, joined, turn_gu_s, turn_gu_r)
    gu_turns.append(pltpu.make_async_copy(blocks_gu.at[plane], joined.at[plane], stay.at[3]))
    for copy in gu_turns:
        copy.start()

    alive = alive_of(lens, att.shape[0], rows)
    for block in range(PLANES):
        for step in range(1, places):
            row_copy(block, step).wait()
        own_row(block).wait()
    attend_back(seq, alive, att, norms, rows_in, keep, rows_out)
    finish = start_back(rows_out, grad_qkv, back_s, back_r, back_l)
    for at in range(0, width, TILE):
        cut = slice(at, at + TILE)
        product = sum(
            dot(attended[block], low[block, :, cut], ((0,), (0,))) for block in range(PLANES)
        )
        parts_out[:, :, cut] = product.astype(BF16).reshape(parts_out.shape[:2] + (TILE,))
    outs = [pltpu.make_async_copy(parts_out.at[place], came_out.at[place], stay.at[0])]
    shares = [pltpu.make_async_copy(parts_qkv.at[:, place], came_qkv.at[place], stay.at[1])]
    moves = []
    for step in range(1, places):
        to = lax.rem(place + step, places)
        device = (plane, to, core)
        outs.append(
            remote(parts_out.at[to], came_out.at[place], out_s.at[step], out_r.at[step], device)
        )
        shares.append(
            remote(
                parts_qkv.at[:, to], came_qkv.at[place], qkv_s.at[step], qkv_r.at[step], device
            )
        )
    finish()
    normed_load.wait()

    flat_weights = w_qkv[...].reshape(width, grad_qkv.shape[3])
    count = part.shape[1]
    for block in range(PLANES):
        rows_of = grad_qkv[block].reshape(count, grad_qkv.shape[3])
        part[block] = dot(rows_of, flat_weights, ((1,), (1,))).astype(BF16)
    def lay_out(grads, first):
        units = joined.shape[2] // 2
        broad = units // LANES * LANES
        left = units - broad
        extent = grads.shape[0] // PLANES
        for to in range(PLANES):
            piece = joined[to].astype(F32)
            low_at = 2 * broad + (0 if first else left)
            start = 0 if first else broad
            pieces = [piece[:, start : start + broad]]
            if left:
                pieces.append(piece[:, low_at : low_at + left])
            found = jnp.concatenate(pieces, axis=1)
            grads[to * extent : (to + 1) * extent, :] = unpack_units(
                found, places, units // places, extent // places
            )

    def others():
        tokens_all = PLANES * count
        grads = grad_qkv[...].reshape(tokens_all, grad_qkv.shape[3])
        for at in range(0, width, TILE):
            left = fed[:, :, at : at + TILE].reshape(tokens_all, TILE)
            product = dot(left, grads, ((0,), (0,))).astype(BF16)
            for row in range(0, TILE, own_rows):
                owner = (at + row) // own_rows
                parts_qkv[owner // places, owner % places] = product[row : row + own_rows]
        for copy in shares + outs:
            copy.start()
        yield
        for copy in gu_turns:
            copy.wait()
        lay_out(grad_gate, True)
        yield
        for copy in shares:
            copy.wait()
        blocks[...] = sum(came_qkv[other].astype(F32) for other in range(places)).astype(BF16)
        moves.extend(turn_copies(blocks, spread, turn_s, turn_r))
        moves.append(pltpu.make_async_copy(blocks.at[plane], spread.at[plane], stay.at[2]))
        for copy in moves:
            copy.start()
        yield
        lay_out(grad_up, False)
        for copy in outs:
            copy.wait()
        sum_out[...] = sum(came_out[other].astype(F32) for other in range(places))

    lasts = [
        column_scatter(part.at[:, cut], (*buffers[at], *last_sems[at]), grad.at[cut])
        for at, cut in enumerate(cuts)
    ]
    in_turn(*lasts, others())
    values, above = tokens[...].astype(F32), grad[...]
    scaled = above * gains[0:1, mine]
    local_two[:, :LANES] = fold(scaled * values)
    local_two[:, LANES:] = fold(values * values)
    total, square = both_cores(local_two, far_two, sum_s.at[1], sum_r.at[1])
    scale = lax.rsqrt(square / width + EPSILON)
    sums[0:1, :] = jnp.sum(above * values * scale, axis=0, keepdims=True)
    finish = to_owners(sums, came_gains, own_s, own_r)
    mean = total / width
    grad[...] = resid_grad[...] + scale * scaled - values * scale**3 * mean
    for copy in moves:
        copy.wait()
    wide = grad_value.shape[1] // PLANES
    slim = grad_query.shape[1] // PLANES
    found = [spread[to].astype(F32) for to in range(PLANES)]
    for to in range(PLANES):
        grad_value[:, to * wide : (to + 1) * wide] = found[to][:, :wide]
    grad_query[...] = jnp.concatenate([one[:, wide : wide + slim] for one in found], axis=1)
    grad_key[...] = jnp.concatenate([one[:, wide + slim :] for one in found], axis=1)
    finish(out_gains)


def to_owners(sums, came, send, receive):
    plane, place, core = here()
    places = lax.axis_size("p")
    count = PLANES * places
    near = count // 2
    index = plane * places + place
    side = lax.div(index, near)
    width = sums.shape[1] // near

    def copy(step, target):
        at = step * width // LANES * LANES
        owner = core * near + step
        device = (lax.div(owner, places), lax.rem(owner, places), target)
        return remote(
            sums.at[:, pl.ds(at, LANES)],
            came.at[index],
            send.at[2 * step + target],
            receive.at[index],
            device,
        )

    def to_self(step, target):
        return (core * near + step == index) & (core == target)

    for step in range(near):
        for target in range(2):
            local = to_self(step, target)
            pl.when(jnp.logical_not(local))(lambda: copy(step, target).start())

            @pl.when(local)
            def _():
                at = step * width // LANES * LANES
                came[index] = sums[:, at : at + LANES]

    def finish(out):
        for step in range(count):
            source = lax.rem(index + step, count)

            @pl.when((step > 0) | (side != core))
            def _():
                remote(
                    came.at[source],
                    came.at[source],
                    send.at[0],
                    receive.at[source],
                    (plane, place, 1 - core),
                ).wait_recv()

        out[...] = sum(came[step] for step in range(count))
        for step in range(near):
            for target in range(2):
                local = to_self(step, target)
                pl.when(jnp.logical_not(local))(lambda: copy(step, target).wait_send())

    return finish


def call(kernel, identity, micros, outs, scratch, args, far_args=(), far_outs=()):
    def spec(far):
        return pl.BlockSpec(memory_space=pl.ANY if far else pltpu.VMEM)

    return pl.pallas_call(
        kernel,
        out_shape=outs,
        in_specs=[spec(at in far_args) for at in range(len(args))],
        out_specs=[spec(at in far_outs) for at in range(len(outs))],
        scratch_shapes=scratch,
        cost_estimate=pl.CostEstimate(
            flops=micros * 10**9, bytes_accessed=micros * 10**6, transcendentals=0
        ),
        compiler_params=pltpu.CompilerParams(
            collective_id=identity, has_side_effects=True, vmem_limit_bytes=VMEM_LIMIT
        ),
    )(*args)


def shape(dims, dtype):
    return jax.ShapeDtypeStruct(dims, dtype)


def front(x_half, c_half, gain_one, gain_two, w_query, w_key, w_value, w_gate, w_up, w_output, lens, units, identity):
    tokens, half = x_half.shape
    places = lax.axis_size("p")
    count = PLANES * places
    rows = lens.size
    positions = tokens // rows
    length = PLANES * places * positions
    own_rows = w_query.shape[0]
    wide = w_value.shape[1] // PLANES
    width = wide + 2 * (w_query.shape[1] // PLANES)
    whole = (PLANES, tokens, 2 * half)
    blocks = (PLANES, own_rows, width)
    gu = (PLANES, own_rows, 2 * units)
    return call(
        front_kernel,
        identity,
        150,
        [
            shape(whole, BF16),
            shape((PLANES, places, own_rows, width), BF16),
            shape((8, 2 * half), F32),
            shape((length, wide), F32),
            shape((length, wide), F32),
            shape((PLANES, rows, positions, wide), BF16),
            shape((PLANES, places, positions, width), BF16),
            shape((PLANES, places, own_rows, 2 * units), BF16),
            shape((places,) + w_output.shape, BF16),
            shape((tokens, half), BF16),
            shape((tokens, half), F32),
            shape((tokens, LANES), F32),
            shape(whole, BF16),
        ],
        [
            pltpu.VMEM((PLANES, places, own_rows, width), BF16),
            pltpu.VMEM((length, wide), F32),
            pltpu.VMEM((length, wide), F32),
            pltpu.VMEM((PLANES, places, positions, width), BF16),
            pltpu.VMEM((places,) + w_output.shape, BF16),
            pltpu.VMEM(whole, BF16),
            pltpu.VMEM(whole, BF16),
            pltpu.VMEM((PLANES, rows, positions, width), BF16),
            pltpu.VMEM(blocks, BF16),
            pltpu.VMEM(blocks, BF16),
            pltpu.VMEM((8, LANES), F32),
            pltpu.VMEM((8, LANES), F32),
            pltpu.VMEM((8, LANES), F32),
            pltpu.VMEM((count, 8, LANES), F32),
            pltpu.VMEM(gu, BF16),
            pltpu.VMEM(gu, BF16),
            pltpu.VMEM((PLANES, places, positions, wide), BF16),
            pltpu.VMEM(whole, BF16),
        ]
        + sums_scratch(tokens, 1)
        + [DMA((5,)), DMA, DMA]
        + [DMA((PLANES,)), DMA((PLANES,)), DMA((count,)), DMA((count,))]
        + [DMA((places,)) for _ in range(4)]
        + [DMA((PLANES, places)), DMA((PLANES, places)), DMA((PLANES,))]
        + [DMA((places,)), DMA((rows,)), DMA]
        + [DMA((PLANES,)), DMA((PLANES,)), DMA]
        + [DMA((PLANES, places)), DMA((PLANES, places)), DMA((PLANES,)), DMA((PLANES,)), DMA((5,))]
        + gather_scratch() * (1 + PARTS)
        + scatter_scratch(tokens // PARTS, half) * PARTS,
        [
            x_half,
            c_half,
            gain_one,
            gain_two,
            w_query,
            w_key,
            w_value,
            w_gate,
            w_up,
            w_output,
            lens,
        ],
        (1,),
        (0, 1, 3, 4, 6, 7, 8, 12),
    )


def sums_scratch(tokens, count):
    return [pltpu.VMEM((tokens, count * LANES), F32) for _ in range(2)] + [DMA, DMA]


def feed(own, w_gu, w_dn, grads, identity):
    tokens, half = own.shape
    units, width = w_dn.shape
    places = lax.axis_size("p")
    whole = (PLANES, tokens, width)
    return call(
        feed_kernel,
        identity,
        55,
        [
            shape(whole, BF16),
            shape(whole, BF16),
            shape((places, PLANES, width // (PLANES * places), 2 * units), BF16),
            shape(w_dn.shape, BF16),
        ],
        [
            pltpu.VMEM(whole, BF16),
            pltpu.VMEM(w_gu.shape, BF16),
            pltpu.VMEM(w_dn.shape, BF16),
            pltpu.VMEM(whole, BF16),
            pltpu.VMEM(w_gu.shape, F32),
            pltpu.VMEM(w_dn.shape, F32),
            pltpu.VMEM((tokens, 2 * units), F32),
            pltpu.VMEM((tokens, -(-units // LANES) * LANES), F32),
            pltpu.VMEM((tokens, units), BF16),
            pltpu.VMEM((tokens, 2 * units), BF16),
            pltpu.VMEM((2, 2, tokens, width), BF16),
            DMA((3,)),
            DMA,
            DMA((2, 2)),
            DMA((PLANES * places,)),
        ]
        + gather_scratch(),
        [own, w_gu, w_dn, grads],
        (1, 2, 3),
        (0, 1, 2, 3),
    )


def row_sems(rows):
    places = lax.axis_size("p")
    sems = [DMA((places,)), DMA((places,)), DMA, DMA((places,)), DMA((rows,)), DMA]
    return sems + [DMA((PLANES,)), DMA((PLANES,)), DMA]


def attend_back_alone(grad_mix, w_out, attended, seq, lens, att, norms, blocks, rows, identity):
    places = lax.axis_size("p")
    positions = grad_mix.shape[1] // rows
    wide = w_out.shape[0]
    width = seq.shape[-1]
    return call(
        attend_back_kernel,
        identity,
        35,
        [
            shape((PLANES, rows, positions, width), BF16),
            shape(blocks.shape, BF16),
            shape((places, wide // places, grad_mix.shape[2]), BF16),
        ],
        [
            pltpu.VMEM((PLANES, rows, positions, wide), BF16),
            pltpu.VMEM(seq.shape[:-1] + (wide,), BF16),
            pltpu.VMEM(seq.shape, BF16),
            pltpu.VMEM((att.shape[0], wide + LANES), F32),
        ]
        + row_sems(rows),
        [grad_mix, w_out, attended, seq, lens, att, norms, blocks],
        (7,),
        (1,),
    )


def mix_back(part, resid, inverse, gains, cotangent, fed, identity):
    tokens, half = resid.shape
    whole = (PLANES, tokens, 2 * half)
    return call(
        back_kernel,
        identity,
        95,
        [
            shape(whole, BF16),
            shape((tokens, half), F32),
            shape((1, half), F32),
            shape((tokens, half), BF16),
        ],
        [pltpu.VMEM(whole, BF16), pltpu.VMEM(whole, BF16)]
        + sums_scratch(tokens, 1)
        + [DMA((2,)), pltpu.VMEM((tokens, half), F32)]
        + gather_scratch() * PARTS
        + scatter_scratch(tokens // PARTS, half) * 2 * PARTS,
        [part, resid, inverse, gains, cotangent, fed],
        (0, 5),
    )


def last_back(grad_qkv, w_qkv, normed, tokens, gains, resid_grad, parts_out, joined, gain_two, units, identity):
    size, half = tokens.shape
    places = lax.axis_size("p")
    count = PLANES * places
    own_rows, width = w_qkv.shape[2:]
    slim = (width - parts_out.shape[0] * parts_out.shape[1]) // 2
    blocks = (PLANES, own_rows, width)
    outs = [
        (size, half),
        parts_out.shape[1:],
        (own_rows, PLANES * slim),
        (own_rows, PLANES * slim),
        (own_rows, PLANES * (width - 2 * slim)),
        (units, own_rows),
        (units, own_rows),
        (8, LANES),
    ]
    return call(
        last_kernel,
        identity,
        60,
        [shape(dims, F32) for dims in outs],
        [
            pltpu.VMEM((PLANES, size, 2 * half), BF16),
            pltpu.VMEM((PLANES, places, own_rows, width), BF16),
            pltpu.VMEM((8, half), F32),
            pltpu.VMEM((count, 8, LANES), F32),
        ]
        + sums_scratch(size, 2)
        + [
            pltpu.VMEM(parts_out.shape, BF16),
            pltpu.VMEM((places,) + blocks, BF16),
            pltpu.VMEM(blocks, BF16),
            pltpu.VMEM(blocks, BF16),
            DMA((3,)),
        ]
        + [DMA((places,)) for _ in range(4)]
        + [DMA((PLANES,)) for _ in range(2)]
        + [DMA((count,)) for _ in range(2)]
        + scatter_scratch(size // PARTS, half) * PARTS,
        [grad_qkv, w_qkv, normed, tokens, gains, resid_grad, parts_out, joined, gain_two],
    )


def end(far, near, units, identity):
    resid, seq, att, w_qkv = near[0], near[7], near[9], near[11]
    tokens, half = resid.shape
    places = lax.axis_size("p")
    count = PLANES * places
    rows = near[8].size
    positions = tokens // rows
    own_rows, width = w_qkv.shape[2:]
    wide = att.shape[1]
    slim = (width - wide) // 2
    whole = (PLANES, tokens, 2 * half)
    blocks = (PLANES, own_rows, width)
    gu = far[2].shape
    outs = [
        ((tokens, half), BF16),
        ((tokens, half), F32),
        ((wide // places, 2 * half), F32),
        ((own_rows, PLANES * slim), F32),
        ((own_rows, PLANES * slim), F32),
        ((own_rows, PLANES * wide), F32),
        ((units, own_rows), F32),
        ((units, own_rows), F32),
        ((8, LANES), F32),
    ]
    parts_out = (places, wide // places, 2 * half)
    scratch = [
        (whole, BF16),
        (whole, BF16),
        (whole, BF16),
        ((tokens, half), F32),
        ((tokens, half), F32),
        (gu, BF16),
        (gu[1:], BF16),
        (gu[1:], BF16),
        ((PLANES, rows, positions, wide), BF16),
        ((PLANES, places, positions, wide), BF16),
        (seq.shape, BF16),
        ((att.shape[0], wide + LANES), F32),
        ((PLANES, rows, positions, width), BF16),
        (parts_out, BF16),
        (parts_out, BF16),
        ((PLANES, places, own_rows, width), BF16),
        ((places,) + blocks, BF16),
        (blocks, BF16),
        (blocks, BF16),
        ((8, half), F32),
        ((count, 8, LANES), F32),
        *[(near[at].shape, near[at].dtype) for at in (5, 6, 7, 9, 10, 11)],
        ((tokens, LANES), F32),
        ((tokens, LANES), F32),
        ((tokens, 2 * LANES), F32),
        ((tokens, 2 * LANES), F32),
    ]
    sems = [(2,), (2,), (3,), (places,), (places,), (), (PLANES,), (PLANES,)]
    sems += [(PLANES, places), (PLANES, places), (PLANES,), (places,), (rows,), ()]
    sems += [(places,)] * 4 + [(PLANES,)] * 2 + [(count,)] * 2 + [(4,), (6,)]
    return call(
        end_kernel,
        identity,
        190,
        [shape(dims, kind) for dims, kind in outs],
        [pltpu.VMEM(dims, kind) for dims, kind in scratch]
        + [DMA(dims) if dims else DMA for dims in sems]
        + gather_scratch() * PARTS
        + scatter_scratch(tokens // PARTS, half) * 2 * PARTS
        + scatter_sems() * PARTS,
        [*far, *near],
        (0, 1, 2, 3, 9, 10, 11, 13, 14, 15),
    )


def end_in_parts(far, near, units, identities):
    part, fed, parts_gu, normed_one = far
    resid, inverse, gains, cotangent, tokens, w_out, attended, seq, lens, att, norms, w_qkv = near
    rows = lens.size
    blocks_gu = lax.psum_scatter(parts_gu, "p", scatter_dimension=0, tiled=False)
    grad_mix, grad_resid, gain_two, mixed = mix_back(
        part, resid, inverse, gains, cotangent, fed, identities[0]
    )
    grad_qkv, blocks_gu, out_output = attend_back_alone(
        grad_mix, w_out, attended, seq, lens, att, norms, blocks_gu, rows, identities[1]
    )
    grad_qkv = grad_qkv.reshape(PLANES, -1, grad_qkv.shape[-1])
    rest = last_back(
        grad_qkv,
        w_qkv,
        normed_one,
        tokens,
        gains,
        grad_resid,
        out_output,
        blocks_gu,
        gain_two,
        units,
        identities[2],
    )
    return (mixed, *rest)


def deliver_kernel(padded, gains, *rest):
    count = (len(rest) - 5) // 3
    ready = rest[:count]
    down, one, two = rest[count : count + 3]
    places = rest[count + 3 : 2 * count + 3]
    held = rest[2 * count + 3 : -2]
    load, store = rest[-2:]
    loads = [
        pltpu.make_async_copy(source, target, load.at[at])
        for at, (source, target) in enumerate(zip(ready, held))
    ]
    stores = [
        pltpu.make_async_copy(source, target, store.at[at])
        for at, (source, target) in enumerate(zip(held, places))
    ]
    for copy in loads:
        copy.start()
    plane, place, core = here()
    index = plane * lax.axis_size("p") + place
    size = one.shape[1]
    at = lax.rem((2 * index + core) * size, LANES)
    turned = pltpu.roll(gains[...], lax.rem(LANES - at, LANES), 1)
    one[...] = turned[0:1, :size]
    two[...] = turned[1:2, :size]
    for one_load, one_store in zip(loads, stores):
        one_load.wait()
        one_store.start()
    down[...] = padded[: down.shape[0], :].astype(F32)
    for copy in stores:
        copy.wait()


def deliver(padded, chunk, gains, own_gain, ready):
    vmem, far = (pl.BlockSpec(memory_space=space) for space in (pltpu.VMEM, pl.ANY))
    small = [shape((chunk, padded.shape[1]), F32), shape((1, own_gain), F32), shape((1, own_gain), F32)]
    return pl.pallas_call(
        deliver_kernel,
        out_shape=small + [shape(one.shape, one.dtype) for one in ready],
        in_specs=[vmem, vmem] + [far] * len(ready),
        out_specs=[vmem] * 3 + [far] * len(ready),
        scratch_shapes=[pltpu.VMEM(one.shape, one.dtype) for one in ready]
        + [DMA((len(ready),)), DMA((len(ready),))],
        compiler_params=pltpu.CompilerParams(vmem_limit_bytes=VMEM_LIMIT),
    )(padded, gains, *ready)


def dot(left, right, dims=((1,), (0,))):
    return lax.dot_general(left, right, (dims, ((), ())), preferred_element_type=F32)


def pad_units(weights, axis, chunk, padded):
    shape = weights.shape
    weights = weights.reshape(shape[:axis] + (-1, chunk) + shape[axis + 1 :])
    pads = [(0, 0)] * weights.ndim
    pads[axis + 1] = (0, padded - chunk)
    return jnp.pad(weights, pads).reshape(shape[:axis] + (-1,) + shape[axis + 1 :])


def on_device(
    tokens,
    lengths,
    attn_gain,
    w_query,
    w_key,
    w_value,
    w_output,
    ffn_gain,
    w_gate,
    w_up,
    w_down,
    cotangent,
):
    count = lax.axis_size("p")
    batches, per_batch, own_len, half = tokens.shape
    rows = batches * per_batch
    own_rows = w_query.shape[0]
    heads = w_query.shape[1] // FEAT // PLANES
    chunk = w_down.shape[0]
    padded = -(-chunk // 16) * 16
    units = count * padded
    slim, broad = heads * FEAT, heads * HEAD_V

    x_half = tokens.reshape(rows * own_len, half)
    c_half = cotangent.reshape(rows * own_len, half)
    w_dn = lax.all_gather(pad_units(w_down, 0, chunk, padded), "p", axis=0, tiled=True)
    (
        normed_one,
        w_qkv,
        gains,
        att,
        norms,
        attended,
        seq,
        w_gu,
        w_out,
        normed_two,
        resid,
        inv_two,
        c_all,
    ) = front(
        x_half,
        c_half,
        attn_gain[None],
        ffn_gain[None],
        w_query,
        w_key,
        w_value,
        w_gate.T,
        w_up.T,
        w_output,
        lengths,
        units,
        0,
    )
    attended = attended.reshape(PLANES, -1, broad)
    w_gu = w_gu.reshape(-1, 2 * units)
    w_out = w_out.reshape(broad, -1)
    part, fed, out_gu, out_down = feed(normed_two, w_gu, w_dn, c_all, 1)
    out_down = lax.psum_scatter(out_down, "p", scatter_dimension=0, tiled=True)
    names = (resid, inv_two, gains, c_half, x_half, w_out, attended, seq, lengths, att, norms, w_qkv)
    if PLANES * count * own_len <= MERGED_LENGTH:
        ends = end((part, fed, out_gu, normed_one), names, w_gate.shape[1], 2)
    else:
        ends = end_in_parts((part, fed, out_gu, normed_one), names, w_gate.shape[1], (4, 5, 6))
    *ready, gain_sums = ends
    down, one, two, *ready = deliver(out_down, chunk, gain_sums, attn_gain.shape[0], ready)
    mixed, grad_tokens, out_output, out_query, out_key, out_value, out_gate, out_up = ready
    return (
        mixed.reshape(tokens.shape),
        grad_tokens.reshape(tokens.shape),
        one.reshape(-1),
        out_query,
        out_key,
        out_value,
        out_output,
        two.reshape(-1),
        out_gate.T,
        out_up.T,
        down,
    )


def solution(mesh):
    split = Mesh(mesh.devices.reshape(PLANES, -1, 2), ("z", "p", "core"))
    seq = ("z", "p")
    both = ("z", "p", "core")
    rows, columns = P(seq, "core"), P(("core", "z", "p"), None)
    tokens = P(None, None, seq, "core")
    return jax.shard_map(
        on_device,
        mesh=split,
        in_specs=(
            tokens,
            P(),
            P(both),
            rows,
            rows,
            rows,
            columns,
            P(both),
            rows,
            rows,
            columns,
            tokens,
        ),
        out_specs=(
            tokens,
            tokens,
            P(both),
            rows,
            rows,
            rows,
            columns,
            P(both),
            rows,
            rows,
            columns,
        ),
        check_vma=False,
    )
```

```python
import jax
import jax.numpy as jnp
from jax import lax
from jax.experimental import pallas as pl
from jax.experimental.pallas import tpu as pltpu
from jax.sharding import Mesh
from jax.sharding import PartitionSpec as P

FEAT = 16
HEAD_V = 128
PLANES = 4
LANES = 128
EPSILON = 1e-05
F32 = jnp.float32
BF16 = jnp.bfloat16
MESH = pl.DeviceIdType.MESH
DMA = pltpu.SemaphoreType.DMA
VMEM_LIMIT = 60 << 20
QUERY_BLOCK = 256
MERGED_LENGTH = 1024
PARTS = 2
TILE = 256
ROW_BLOCK = 32


def remote(source, target, send, receive, device):
    return pltpu.make_async_remote_copy(
        src_ref=source,
        dst_ref=target,
        send_sem=send,
        recv_sem=receive,
        device_id=device,
        device_id_type=MESH,
    )


def here():
    return tuple(lax.axis_index(name) for name in ("z", "p", "core"))


def signal(semaphore, device):
    pl.semaphore_signal(semaphore, inc=1, device_id=device, device_id_type=MESH)


def greet_column():
    plane, place, core = here()
    barrier = pltpu.get_barrier_semaphore()
    signal(barrier, (plane, place, 1 - core))
    pl.when(plane > 0)(lambda: signal(barrier, (plane - 1, place, core)))
    pl.when(plane < PLANES - 1)(lambda: signal(barrier, (plane + 1, place, core)))
    inner = (plane > 0).astype(jnp.int32) + (plane < PLANES - 1).astype(jnp.int32)
    return lambda: pl.semaphore_wait(barrier, 1 + inner)


def greet_same():
    plane, place, core = here()
    places = lax.axis_size("p")
    barrier = pltpu.get_barrier_semaphore()
    signal(barrier, (plane, place, 1 - core))
    for step in range(1, PLANES * places):
        signal(barrier, peer(step) + (core,))
    return lambda: pl.semaphore_wait(barrier, PLANES * places)


def greet_all():
    plane, place, core = here()
    count = PLANES * lax.axis_size("p")
    barrier = pltpu.get_barrier_semaphore()
    signal(barrier, (plane, place, 1 - core))
    for step in range(1, count):
        signal(barrier, peer(step) + (core,))
        signal(barrier, peer(step) + (1 - core,))
    return lambda: pl.semaphore_wait(barrier, 2 * count - 1)


def greet_cross():
    plane, place, core = here()
    places = lax.axis_size("p")
    barrier = pltpu.get_barrier_semaphore()
    for step in range(1, places):
        signal(barrier, (plane, lax.rem(place + step, places), core))
    for step in range(1, PLANES):
        signal(barrier, (lax.rem(plane + step, PLANES), place, core))
    return lambda: pl.semaphore_wait(barrier, places + PLANES - 2)


def peer(step):
    plane, place, _ = here()
    places = lax.axis_size("p")
    index = lax.rem(plane * places + place + step, PLANES * places)
    return lax.div(index, places), lax.rem(index, places)


def halves(width):
    core = lax.axis_index("core")
    half = width // 2
    return (
        pl.ds(pl.multiple_of(core * half, LANES), half),
        pl.ds(pl.multiple_of((1 - core) * half, LANES), half),
    )


def in_turn(*steps):
    steps = list(steps)
    while steps:
        steps = [one for one in steps if next(one, steps) is not steps]


def gather_scratch():
    return [DMA((PLANES,)) for _ in range(5)]


class Gather:
    def __init__(self, out, sems):
        self.out = out
        self.arrive, self.across, self.up, self.down, self.over = sems
        self.plane, self.place, self.core = here()
        self.mine, self.other = halves(out.shape[2])

    def send(self, block, sems, receive, device):
        piece = self.out.at[block, :, self.mine]
        return remote(piece, piece, sems.at[block], receive.at[block], device)

    def rise(self, block):
        return self.send(block, self.up, self.arrive, (self.plane + 1, self.place, self.core))

    def fall(self, block):
        return self.send(block, self.down, self.arrive, (self.plane - 1, self.place, self.core))

    def cross(self, block):
        return self.send(block, self.over, self.across, (self.plane, self.place, 1 - self.core))

    def start(self):
        plane = self.plane
        pl.when(plane < PLANES - 1)(lambda: self.rise(plane).start())
        pl.when(plane > 0)(lambda: self.fall(plane).start())
        self.cross(plane).start()

    def landed(self, block):
        partner = (self.plane, self.place, 1 - self.core)
        self.send(block, self.over, self.arrive, partner).wait_recv()

    def pass_on(self, far):
        plane = self.plane

        @pl.when(plane >= far)
        def _():
            self.landed(plane - far)
            pl.when(plane < PLANES - 1)(lambda: self.rise(plane - far).start())
            self.cross(plane - far).start()

        @pl.when(plane + far < PLANES)
        def _():
            self.landed(plane + far)
            pl.when(plane > 0)(lambda: self.fall(plane + far).start())
            self.cross(plane + far).start()

    def whole(self, block):
        piece = self.out.at[block, :, self.other]
        partner = (self.plane, self.place, 1 - self.core)
        remote(piece, piece, self.over.at[block], self.across.at[block], partner).wait_recv()

    def finish(self):
        plane = self.plane
        for block in range(PLANES):
            self.cross(block).wait_send()
            pl.when((plane < PLANES - 1) & (block <= plane))(lambda: self.rise(block).wait_send())
            pl.when((plane > 0) & (block >= plane))(lambda: self.fall(block).wait_send())

    def steps(self):
        self.start()
        yield
        for far in range(1, PLANES):
            self.pass_on(far)
            yield
        for block in range(PLANES):
            self.whole(block)
        self.finish()


def order_of_arrival(step):
    plane = lax.axis_index("z")
    nearest = [sorted(range(PLANES), key=lambda block: (abs(block - own), block)) for own in range(PLANES)]
    found = jnp.int32(0)
    for own in range(PLANES):
        for at in range(PLANES):
            found = jnp.where((plane == own) & (step == at), nearest[own][at], found)
    return found


def scatter_buffers(tokens, half):
    return [
        pltpu.VMEM((PLANES, tokens, half), BF16),
        pltpu.VMEM((PLANES + 1, tokens, half), BF16),
    ]


def scatter_sems():
    return [DMA((PLANES,)) for _ in range(6)]


def scatter_scratch(tokens, half):
    return scatter_buffers(tokens, half) + scatter_sems()


def column_scatter(part, scratch, total):
    twin, came, over_s, over_r, up_s, up_r, down_s, down_r = scratch
    plane, place, core = here()
    mine, other = halves(part.shape[2])

    def cross(block):
        return remote(
            part.at[block, :, other],
            twin.at[block],
            over_s.at[block],
            over_r.at[block],
            (plane, place, 1 - core),
        )

    def rise(block):
        return remote(
            came.at[block], came.at[block], up_s.at[block], up_r.at[block], (plane + 1, place, core)
        )

    def fall(block):
        last = jnp.where(block == plane - 1, PLANES, block)
        return remote(
            came.at[block], came.at[last], down_s.at[block], down_r.at[block], (plane - 1, place, core)
        )

    def own(block):
        return part[block, :, mine].astype(F32) + twin[block].astype(F32)

    def pass_on(block, link, first):
        cross(block).wait_recv()

        @pl.when(jnp.logical_not(first))
        def _():
            link(block).wait_recv()
            came[block] = (own(block) + came[block].astype(F32)).astype(BF16)

        @pl.when(first)
        def _():
            came[block] = own(block).astype(BF16)

        link(block).start()

    for far in range(PLANES - 1, 0, -1):
        pl.when(plane + far < PLANES)(lambda: cross(plane + far).start())
        pl.when(plane >= far)(lambda: cross(plane - far).start())
    cross(plane).start()
    yield
    for far in range(PLANES - 1, 0, -1):
        pl.when(plane + far < PLANES)(lambda: pass_on(plane + far, rise, plane == 0))
        pl.when(plane >= far)(lambda: pass_on(plane - far, fall, plane == PLANES - 1))
        yield
    cross(plane).wait_recv()
    total[...] = own(plane)

    @pl.when(plane > 0)
    def _():
        rise(plane).wait_recv()
        total[...] += came[plane].astype(F32)

    @pl.when(plane < PLANES - 1)
    def _():
        fall(plane).wait_recv()
        total[...] += came[PLANES].astype(F32)

    for block in range(PLANES):
        cross(block).wait_send()
        pl.when(block > plane)(lambda: rise(block).wait_send())
        pl.when(block < plane)(lambda: fall(block).wait_send())


def gathers(out, scratch):
    size = out.shape[1] // PARTS
    return [
        Gather(out.at[:, pl.ds(at * size, size)], scratch[5 * at : 5 * at + 5]).steps()
        for at in range(PARTS)
    ]


def scatters(part, scratch, total):
    size = part.shape[1] // PARTS
    return [
        column_scatter(
            part.at[:, pl.ds(at * size, size)],
            scratch[8 * at : 8 * at + 8],
            total.at[pl.ds(at * size, size)],
        )
        for at in range(PARTS)
    ]


def fold(values):
    return sum(values[:, at : at + LANES] for at in range(0, values.shape[1], LANES))


def both_cores(local, far, send, receive):
    plane, place, core = here()
    copy = remote(local, far, send, receive, (plane, place, 1 - core))
    copy.start()
    copy.wait()
    joined = local[...] + far[...]
    return [
        jnp.sum(joined[:, at : at + LANES], axis=1, keepdims=True)
        for at in range(0, joined.shape[1], LANES)
    ]


def turn_copies(blocks, spread, send, receive):
    plane, place, core = here()
    copies = []
    for step in range(1, PLANES):
        to = lax.rem(plane + step, PLANES)
        copies.append(
            remote(blocks.at[to], spread.at[plane], send.at[step], receive.at[step], (to, place, core))
        )
    return copies


def pack_units(weights, places, plane, padded):
    size = weights.shape[0] // PLANES
    chunk = size // places
    turned = weights[pl.ds(pl.multiple_of(plane * size, 16), size), :].astype(F32).T
    blank = jnp.zeros((turned.shape[0], padded - chunk), F32)
    pieces = []
    for place in range(places):
        pieces += [turned[:, place * chunk : (place + 1) * chunk], blank]
    return jnp.concatenate(pieces, axis=1)


def unpack_units(weights, places, padded, chunk):
    pieces = [weights[:, place * padded : place * padded + chunk] for place in range(places)]
    return jnp.concatenate(pieces, axis=1).T


def front_kernel(
    own,
    other,
    gain_one,
    gain_two,
    w_query,
    w_key,
    w_value,
    w_gate,
    w_up,
    w_output,
    lens,
    normed_one,
    far_weights,
    gains,
    far_att,
    far_norms,
    attended,
    far_seq,
    w_gu,
    far_out,
    normed,
    resid,
    inverse,
    whole_c,
    weights,
    att,
    norms,
    seq,
    w_out,
    whole,
    normed_in,
    qkv,
    blocks,
    spread,
    tile,
    pair,
    twin,
    tiles,
    joined,
    turned,
    low,
    part,
    local,
    far_sums,
    sum_s,
    sum_r,
    stay,
    swap_s,
    swap_r,
    turn_s,
    turn_r,
    gain_s,
    gain_r,
    spread_s,
    spread_r,
    out_s,
    out_r,
    row_s,
    row_r,
    row_l,
    back_s,
    back_r,
    back_l,
    gu_s,
    gu_r,
    gu_l,
    pass_s,
    pass_r,
    pass_l,
    keep_n,
    write,
    *rest,
):
    plane, place, core = here()
    places = lax.axis_size("p")
    count = PLANES * places
    index = plane * places + place
    width = whole.shape[2]
    mine, _ = halves(width)
    rows = attended.shape[1]
    per_row = places // rows
    gather = Gather(whole, rest[:5])
    greeted = greet_same()

    keep = pltpu.make_async_copy(own, whole.at[plane, :, mine], stay.at[0])
    keep.start()
    keep_c = pltpu.make_async_copy(other, whole_c.at[plane, :, mine], stay.at[1])
    keep_c.start()
    own_gain = gain_one.shape[1]
    tile[...] = jnp.zeros_like(tile)
    tile[0:1, :own_gain] = gain_one[...].astype(F32)
    tile[1:2, :own_gain] = gain_two[...].astype(F32)
    tile[...] = pltpu.roll(tile[...], lax.rem((2 * index + core) * own_gain, LANES), 1)
    wide = w_value.shape[1] // PLANES
    slim = w_query.shape[1] // PLANES
    for to in range(PLANES):
        pieces = [
            w_value[:, to * wide : (to + 1) * wide],
            w_query[:, to * slim : (to + 1) * slim],
            w_key[:, to * slim : (to + 1) * slim],
        ]
        joint = jnp.concatenate([piece.astype(F32) for piece in pieces], axis=1)
        blocks[to] = joint.astype(BF16)
    keep.wait()
    greeted()

    swap = remote(tile, twin, swap_s, swap_r, (plane, place, 1 - core))
    swap.start()
    turns = turn_copies(blocks, spread, turn_s, turn_r)
    for copy in turns:
        copy.start()
    gather.start()
    own_block = pltpu.make_async_copy(blocks.at[plane], spread.at[plane], stay.at[2])
    own_block.start()
    swap.wait()
    pair[...] = tile[...] + twin[...]
    tiles[index] = pair[...]
    sends = []
    for step in range(1, count):
        sends.append(
            remote(pair, tiles.at[index], gain_s.at[step], gain_r.at[step], peer(step) + (core,))
        )
        sends[-1].start()
    own_block.wait()
    for copy in turns:
        copy.wait()
    around = [
        pltpu.make_async_copy(spread, weights.at[:, place], stay.at[3]),
        pltpu.make_async_copy(w_output, w_out.at[place], stay.at[4]),
    ]
    for step in range(1, places):
        to = (plane, lax.rem(place + step, places), core)
        around.append(
            remote(spread, weights.at[:, place], spread_s.at[step], spread_r.at[step], to)
        )
        around.append(remote(w_output, w_out.at[place], out_s.at[step], out_r.at[step], to))
    for copy in around:
        copy.start()

    units = joined.shape[2] // 2
    padded = units // places
    broad = units // LANES * LANES

    def lay_out(to):
        gate = pack_units(w_gate, places, to, padded)
        up = pack_units(w_up, places, to, padded)
        joined[to, :, :broad] = gate[:, :broad].astype(BF16)
        joined[to, :, broad : 2 * broad] = up[:, :broad].astype(BF16)
        if units > broad:
            joined[to, :, 2 * broad :] = jnp.concatenate(
                [gate[:, broad:], up[:, broad:]], axis=1
            ).astype(BF16)

    def passed(step):
        block = lax.rem(plane - step + PLANES, PLANES)
        source = joined.at[plane] if step == 0 else turned.at[block]
        target = w_gu.at[block, place]
        copies = [pltpu.make_async_copy(source, target, pass_l.at[step])]
        for side in range(1, places):
            to = (plane, lax.rem(place + side, places), core)
            copies.append(
                remote(source, target, pass_s.at[step, side], pass_r.at[step, side], to)
            )
        return copies

    lay_out(plane)
    for copy in passed(0):
        copy.start()
    for step in range(1, PLANES):
        lay_out(lax.rem(plane + step, PLANES))

    gu_turns = turn_copies(joined, turned, gu_s, gu_r)

    def inward(step):
        to = lax.rem(plane + step, PLANES)
        return (jnp.abs(to - plane) == 1) & (to > 0) & (to < PLANES - 1)

    for step in range(1, PLANES):
        pl.when(inward(step))(gu_turns[step - 1].start)
    gather.pass_on(1)
    for copy in sends + around:
        copy.wait()
    each = width // count
    for at in range(0, width, LANES):
        group = range(at // each, (at + LANES) // each)
        gains[:, at : at + LANES] = sum(tiles[source] for source in group)
    gain = gains[0:1, :]

    def row_copy(block, step):
        to = lax.rem(place + step, places)
        return remote(
            qkv.at[block, lax.div(to, per_row)],
            seq.at[block, place],
            row_s.at[block, step],
            row_r.at[block, step],
            (plane, to, core),
        )

    def own_row(block):
        return pltpu.make_async_copy(
            qkv.at[block, lax.div(place, per_row)], seq.at[block, place], row_l.at[block]
        )

    def project(block):
        gather.whole(block)
        values = whole[block].astype(F32)
        scale = lax.rsqrt(jnp.mean(values * values, axis=1, keepdims=True) + EPSILON)
        normed_in[block] = (values * scale * gain).astype(BF16)
        pltpu.make_async_copy(normed_in.at[block], normed_one.at[block], keep_n.at[block]).start()
        flat_weights = weights[...].reshape(width, qkv.shape[3])
        qkv[block] = dot(normed_in[block], flat_weights).astype(BF16).reshape(qkv.shape[1:])
        for step in range(1, places):
            row_copy(block, step).start()
        own_row(block).start()

    project(order_of_arrival(0))
    for far in range(2, PLANES):
        gather.pass_on(far)
        project(order_of_arrival(far - 1))

    for step in range(1, PLANES):
        pl.when(jnp.logical_not(inward(step)))(gu_turns[step - 1].start)
    project(order_of_arrival(PLANES - 1))
    gather.finish()

    alive = alive_of(lens, att.shape[0], rows).astype(BF16)
    for block in range(PLANES):
        for step in range(1, places):
            row_copy(block, step).wait()
        own_row(block).wait()
    attend(seq, alive, att, norms)
    low[...] = att[...].astype(BF16).reshape(low.shape)
    finish = start_back(low, attended, back_s, back_r, back_l)
    finish()
    pairs = [
        (weights, far_weights),
        (att, far_att),
        (norms, far_norms),
        (seq, far_seq),
        (w_out, far_out),
    ]
    writes = [
        pltpu.make_async_copy(source, target, write.at[at])
        for at, (source, target) in enumerate(pairs)
    ]
    for copy in writes:
        copy.start()
    tokens = whole.shape[1]
    flat_out = w_out[...].reshape(-1, width)
    for block in range(PLANES):
        rows_in = attended[block].reshape(tokens, flat_out.shape[0])
        part[block] = dot(rows_in, flat_out).astype(BF16)

    def gu_flow():
        for step in range(1, PLANES):
            gu_turns[step - 1].wait()
            for copy in passed(step):
                copy.start()
            yield

    keep_c.wait()
    two = 5 + 5 * PARTS
    in_turn(*scatters(part, rest[two:], resid), *gathers(whole_c, rest[5:two]), gu_flow())
    resid[...] += own[...].astype(F32)
    local[...] = fold(resid[...] * resid[...])
    (total,) = both_cores(local, far_sums, sum_s, sum_r)
    scale = lax.rsqrt(total / width + EPSILON)
    inverse[...] = jnp.broadcast_to(scale, inverse.shape)
    normed[...] = (resid[...] * scale * gains[1:2, mine]).astype(BF16)
    for step in range(PLANES):
        for copy in passed(step):
            copy.wait()
        pltpu.make_async_copy(normed_in.at[step], normed_one.at[step], keep_n.at[step]).wait()
    for copy in writes:
        copy.wait()


def start_back(seq, out, send, receive, local):
    plane, place, core = here()
    places = lax.axis_size("p")
    rows = out.shape[1]
    per_row = places // rows
    row = lax.div(place, per_row)
    speaks = lax.rem(place, per_row) == 0

    def copy(step):
        to = lax.rem(place + step, places)
        return remote(
            seq.at[:, to], out.at[:, row], send.at[step], receive.at[row], (plane, to, core)
        )

    def stay():
        return pltpu.make_async_copy(seq.at[:, place], out.at[:, row], local)

    @pl.when(speaks)
    def _():
        for step in range(1, places):
            copy(step).start()
        stay().start()

    def finish():
        @pl.when(speaks)
        def _():
            stay().wait()
            for step in range(1, places):
                copy(step).wait_send()

        for other in range(rows):

            @pl.when(other * per_row != place)
            def _():
                remote(
                    out.at[:, other],
                    out.at[:, other],
                    send.at[0],
                    receive.at[other],
                    (plane, lax.rem(place + 1, places), core),
                ).wait_recv()

    return finish


def flat(ref):
    block = ref[...]
    return block.reshape(-1, block.shape[-1])


def columns_of(seq, heads, head):
    wide = heads * HEAD_V
    slim = seq[:, wide : wide + 2 * heads * FEAT].astype(F32)
    queries = slim[:, head * FEAT : (head + 1) * FEAT].astype(BF16)
    keys = slim[:, (heads + head) * FEAT : (heads + head + 1) * FEAT].astype(BF16)
    return queries, keys, seq[:, head * HEAD_V : (head + 1) * HEAD_V]


def causal(start, stop, values):
    queries = start + lax.broadcasted_iota(jnp.int32, values.shape, 0)
    keys = lax.broadcasted_iota(jnp.int32, values.shape, 1)
    return jnp.where(queries >= keys, values, 0.0)


def alive_of(lens, length, rows):
    row = lax.div(lax.axis_index("p"), lax.axis_size("p") // rows)
    per_batch = lens.shape[1]
    found = lens[pl.ds(lax.div(row, per_batch), 1), :].astype(F32)
    column = lax.broadcasted_iota(jnp.int32, found.shape, 1)
    limit = jnp.sum(jnp.where(column == lax.rem(row, per_batch), found, 0.0), axis=1, keepdims=True)
    positions = lax.broadcasted_iota(jnp.int32, (length, LANES), 0).astype(F32)
    return jnp.where(positions < limit, 1.0, 0.0).astype(F32)


def attend(seq, alive, att, norms):
    everything = flat(seq)
    length = everything.shape[0]
    heads = att.shape[1] // HEAD_V
    block = min(QUERY_BLOCK, length)
    for head in range(heads):
        queries, keys, values = columns_of(everything, heads, head)
        values = jnp.concatenate([values * alive, alive], axis=1)
        wide = slice(head * HEAD_V, (head + 1) * HEAD_V)
        for start in range(0, length, block):
            stop = start + block
            scores = dot(queries[start:stop], keys[:stop], ((1,), (1,)))
            half = 1.0 + 0.25 * scores
            taylor = causal(start, stop, 0.5 + 0.5 * (half * half)).astype(BF16)
            sums = dot(taylor, values[:stop])
            norm = sums[:, HEAD_V:]
            ratio = sums[:, :HEAD_V] / norm
            att[start:stop, wide] = ratio
            norms[start:stop, wide] = norm


def attend_back(seq, alive, att, norms, rows, keep, low):
    everything = flat(seq)
    length = everything.shape[0]
    heads = att.shape[1] // HEAD_V
    block = min(QUERY_BLOCK, length)
    grads = flat(rows).astype(F32)
    grad_q, grad_k = [], []
    for head in range(heads):
        queries, keys, values = columns_of(everything, heads, head)
        live_keys = (keys.astype(F32) * alive[:, :FEAT]).astype(BF16)
        wide = slice(head * HEAD_V, (head + 1) * HEAD_V)
        grad = grads[:, wide]
        norm = norms[:, wide]
        grad_num = (grad / norm).astype(BF16)
        grad_norm = -jnp.sum(grad * att[:, wide] / norm, axis=1, keepdims=True)
        parts = []
        for start in range(0, length, block):
            stop = start + block
            scores = dot(queries[start:stop], keys[:stop], ((1,), (1,)))
            half = 1.0 + 0.25 * scores
            taylor = causal(start, stop, 0.5 + 0.5 * (half * half)).astype(BF16)
            inner = dot(grad_num[start:stop], values[:stop], ((1,), (1,))) + grad_norm[start:stop]
            slope = causal(start, stop, half * inner).astype(BF16)
            parts.append(dot(slope, live_keys[:stop]) * 0.25)
            from_values = dot(taylor, grad_num[start:stop], ((0,), (0,)))
            from_keys = dot(slope, queries[start:stop], ((0,), (0,)))
            if start:
                keep[:start, wide] += from_values[:start]
                keep[:start, heads * HEAD_V + head * FEAT : heads * HEAD_V + (head + 1) * FEAT] += (
                    from_keys[:start]
                )
            keep[start:stop, wide] = from_values[start:]
            keep[start:stop, heads * HEAD_V + head * FEAT : heads * HEAD_V + (head + 1) * FEAT] = (
                from_keys[start:]
            )
        grad_q.append(jnp.concatenate(parts, axis=0))
        keep[:, wide] *= alive
    wide = heads * HEAD_V
    keys = keep[:, wide : wide + heads * FEAT] * (0.25 * alive[:, : heads * FEAT])
    result = jnp.concatenate([keep[:, :wide]] + grad_q + [keys], axis=1)
    low[...] = result.astype(BF16).reshape(low.shape)


def feed_kernel(
    own,
    w_gu,
    w_dn,
    grads,
    part,
    fed,
    out_gu,
    out_dn,
    normed,
    held_gu,
    held_dn,
    held_c,
    sum_gu,
    sum_dn,
    gate_up,
    grad_hidden,
    hidden,
    grad_gu,
    stage,
    load,
    keep,
    store,
    ending,
    *sems,
):
    plane = lax.axis_index("z")
    mine, _ = halves(normed.shape[2])
    places = lax.axis_size("p")
    units = hidden.shape[1]
    broad = units // LANES * LANES
    rest = units - broad
    rows = normed.shape[1]
    loads = [
        pltpu.make_async_copy(w_gu, held_gu, load.at[0]),
        pltpu.make_async_copy(w_dn, held_dn, load.at[1]),
        pltpu.make_async_copy(grads, held_c, load.at[2]),
    ]
    for copy in loads:
        copy.start()
    gather = Gather(normed, sems)
    greeted = greet_column()
    stay = pltpu.make_async_copy(own, normed.at[plane, :, mine], keep)
    stay.start()
    stay.wait()
    greeted()
    gather.start()
    sum_gu[...] = jnp.zeros_like(sum_gu)
    sum_dn[...] = jnp.zeros_like(sum_dn)
    for copy in loads:
        copy.wait()

    def tiles(width):
        return [slice(at, min(at + TILE, width)) for at in range(0, width, TILE)]

    def stores(block, slot):
        return (
            pltpu.make_async_copy(stage.at[0, slot], fed.at[block], store.at[0, slot]),
            pltpu.make_async_copy(stage.at[1, slot], part.at[block], store.at[1, slot]),
        )

    def middle(at):
        here_rows = pl.ds(pl.multiple_of(at * ROW_BLOCK, ROW_BLOCK), ROW_BLOCK)

        def parts(gate, up, above):
            sigmoid = jax.nn.sigmoid(gate)
            silu = gate * sigmoid
            slope = sigmoid * (1.0 + gate * (1.0 - sigmoid))
            return silu * up, above * up * slope, above * silu

        both = gate_up[here_rows, :]
        above = grad_hidden[here_rows, :]
        first, second, third = parts(
            both[:, :broad], both[:, broad : 2 * broad], above[:, :broad]
        )
        hidden[here_rows, :broad] = first.astype(BF16)
        grad_gu[here_rows, :broad] = second.astype(BF16)
        grad_gu[here_rows, broad : 2 * broad] = third.astype(BF16)
        if rest:
            last = both[:, 2 * broad :]
            turned = pltpu.roll(last, rest, 1)
            first, second, third = parts(last, turned, above[:, broad : broad + LANES])
            hidden[here_rows, broad:] = first[:, :rest].astype(BF16)
            lane = lax.broadcasted_iota(jnp.int32, last.shape, 1)
            joined = jnp.where(lane < rest, second, pltpu.roll(third, rest, 1))
            grad_gu[here_rows, 2 * broad :] = joined.astype(BF16)

    def through(step, carry):
        pl.when(step > 0)(lambda: gather.pass_on(step))
        block = order_of_arrival(step)
        slot = lax.rem(step, 2)
        gather.whole(block)
        for cut in tiles(2 * units):
            gate_up[:, cut] = dot(normed[block], held_gu[:, cut])
        grad_hidden[:, :units] = dot(held_c[block], held_dn[...], ((1,), (1,)))
        lax.fori_loop(0, rows // ROW_BLOCK, lambda at, none: (middle(at), none)[1], 0)

        @pl.when(step >= 2)
        def _():
            for copy in stores(order_of_arrival(step - 2), slot):
                copy.wait()

        for cut in tiles(normed.shape[2]):
            stage[0, slot, :, cut] = dot(hidden[...], held_dn[:, cut]).astype(BF16)
            stage[1, slot, :, cut] = dot(grad_gu[...], held_gu[cut, :], ((1,), (1,))).astype(BF16)
        for copy in stores(block, slot):
            copy.start()
        for cut in tiles(normed.shape[2]):
            sum_gu[cut, :] += dot(normed[block, :, cut], grad_gu[...], ((0,), (0,)))
            sum_dn[:, cut] += dot(hidden[...], held_c[block, :, cut], ((0,), (0,)))
        return carry

    lax.fori_loop(0, PLANES, through, 0)
    own_rows = out_gu.shape[2]
    ends = []
    for block in range(normed.shape[2] // own_rows):
        cut = pl.ds(block * own_rows, own_rows)
        held_gu[cut, :] = sum_gu[cut, :].astype(BF16)
        ends.append(
            pltpu.make_async_copy(
                held_gu.at[cut], out_gu.at[block % places, block // places], ending.at[block]
            )
        )
        ends[-1].start()
    held_dn[...] = sum_dn[...].astype(BF16)
    ends.append(pltpu.make_async_copy(held_dn, out_dn, load.at[1]))
    ends[-1].start()
    for step in (PLANES - 2, PLANES - 1):
        for copy in stores(order_of_arrival(step), step % 2):
            copy.wait()
    for copy in ends:
        copy.wait()
    gather.finish()


def to_rows(values, seq, send, receive, local):
    plane, place, core = here()
    places = lax.axis_size("p")
    per_row = places // values.shape[1]
    copies = []
    for step in range(1, places):
        to = lax.rem(place + step, places)
        row = lax.div(to, per_row)
        copies.append(
            remote(
                values.at[:, row], seq.at[:, place], send.at[step], receive.at[step], (plane, to, core)
            )
        )
    copies.append(
        pltpu.make_async_copy(values.at[:, lax.div(place, per_row)], seq.at[:, place], local)
    )
    return copies


def attend_back_kernel(
    grad_mix,
    w_out,
    attended,
    seq,
    lens,
    att,
    norms,
    blocks,
    out,
    spread,
    out_output,
    grad_att,
    rows,
    low,
    keep,
    *sems,
):
    row_s, row_r, local, back_s, back_r, back_l, turn_s, turn_r, stay_s = sems
    plane = lax.axis_index("z")
    greeted = greet_cross()
    for block in range(PLANES):
        product = dot(grad_mix[block], w_out[...], ((1,), (1,))).astype(BF16)
        grad_att[block] = product.reshape(grad_att.shape[1:])
    greeted()
    copies = to_rows(grad_att, rows, row_s, row_r, local)
    for copy in copies:
        copy.start()
    turns = turn_copies(blocks, spread, turn_s, turn_r)
    turns.append(pltpu.make_async_copy(blocks.at[plane], spread.at[plane], stay_s))
    for copy in turns:
        copy.start()
    alive = alive_of(lens, att.shape[0], grad_att.shape[1])
    for at in range(0, grad_mix.shape[2], TILE):
        cut = slice(at, at + TILE)
        product = sum(
            dot(attended[block], grad_mix[block, :, cut], ((0,), (0,))) for block in range(PLANES)
        )
        out_output[:, :, cut] = product.astype(BF16).reshape(out_output.shape[:2] + (TILE,))
    for copy in copies:
        copy.wait()
    attend_back(seq, alive, att, norms, rows, keep, low)
    finish = start_back(low, out, back_s, back_r, back_l)
    for copy in turns:
        copy.wait()
    finish()


def back_kernel(
    far_part,
    resid,
    inverse,
    gains,
    cotangent,
    far_fed,
    low,
    grad,
    gain_sum,
    mixed,
    part,
    fed,
    local,
    far,
    send,
    receive,
    load,
    total_fed,
    *rest,
):
    plane = lax.axis_index("z")
    mine, _ = halves(part.shape[2])
    one, two = 5 * PARTS, 13 * PARTS
    greeted = greet_column()
    copies = [
        pltpu.make_async_copy(far_part, part, load.at[0]),
        pltpu.make_async_copy(far_fed, fed, load.at[1]),
    ]
    for copy in copies:
        copy.start()
    copies[0].wait()
    greeted()
    in_turn(*scatters(part, rest[one:two], grad))
    copies[1].wait()
    scale = inverse[:, :1]
    values, above = resid[...], grad[...]
    scaled = above * gains[1:2, mine]
    local[...] = fold(scaled * values)
    (total,) = both_cores(local, far, send, receive)
    mean = total / part.shape[2]
    grad[...] = cotangent[...].astype(F32) + scale * scaled - values * scale**3 * mean
    low[plane, :, mine] = grad[...].astype(BF16)
    in_turn(
        *gathers(low, rest[:one]),
        *scatters(fed, rest[two:], total_fed),
        keep_sum(gain_sum, above * values * scale),
    )
    mixed[...] = (total_fed[...] + resid[...]).astype(BF16)


def keep_sum(gain_sum, values):
    yield
    gain_sum[...] = jnp.sum(values, axis=0, keepdims=True)


def last_kernel(
    grad_qkv,
    w_qkv,
    normed,
    tokens,
    gains,
    resid_grad,
    parts_out,
    joined,
    gain_two,
    grad,
    sum_out,
    grad_query,
    grad_key,
    grad_value,
    grad_gate,
    grad_up,
    out_gains,
    part,
    parts_qkv,
    sums,
    came_gains,
    local,
    far,
    send,
    receive,
    came_out,
    came_qkv,
    blocks,
    spread,
    stay,
    out_s,
    out_r,
    qkv_s,
    qkv_r,
    turn_s,
    turn_r,
    own_s,
    own_r,
    *rest,
):
    plane, place, core = here()
    places = lax.axis_size("p")
    mine, _ = halves(part.shape[2])
    own_rows = parts_qkv.shape[2]
    greeted = greet_all()
    flat_weights = w_qkv[...].reshape(part.shape[2], grad_qkv.shape[2])
    for block in range(PLANES):
        part[block] = dot(grad_qkv[block], flat_weights, ((1,), (1,))).astype(BF16)
    greeted()
    outs, shares, moves = [], [], []
    for step in range(1, places):
        to = lax.rem(place + step, places)
        device = (plane, to, core)
        outs.append(
            remote(parts_out.at[to], came_out.at[place], out_s.at[step], out_r.at[step], device)
        )
        shares.append(
            remote(
                parts_qkv.at[:, to], came_qkv.at[place], qkv_s.at[step], qkv_r.at[step], device
            )
        )
    outs.append(pltpu.make_async_copy(parts_out.at[place], came_out.at[place], stay.at[0]))
    shares.append(pltpu.make_async_copy(parts_qkv.at[:, place], came_qkv.at[place], stay.at[1]))

    def lay_out(grads, first):
        units = joined.shape[2] // 2
        broad = units // LANES * LANES
        rest = units - broad
        size = grads.shape[0] // PLANES
        for to in range(PLANES):
            piece = joined[to].astype(F32)
            low = 2 * broad + (0 if first else rest)
            start = 0 if first else broad
            pieces = [piece[:, start : start + broad]]
            if rest:
                pieces.append(piece[:, low : low + rest])
            found = jnp.concatenate(pieces, axis=1)
            grads[to * size : (to + 1) * size, :] = unpack_units(
                found, places, units // places, size // places
            )

    def others():
        for copy in outs:
            copy.start()
        yield
        tokens_all = PLANES * normed.shape[1]
        grads = grad_qkv[...].reshape(tokens_all, grad_qkv.shape[2])
        for at in range(0, part.shape[2], TILE):
            left = normed[:, :, at : at + TILE].reshape(tokens_all, TILE)
            product = dot(left, grads, ((0,), (0,))).astype(BF16)
            for row in range(0, TILE, own_rows):
                owner = (at + row) // own_rows
                parts_qkv[owner // places, owner % places] = product[row : row + own_rows]
            if at + TILE == part.shape[2] // 2:
                yield
        for copy in shares:
            copy.start()
        yield
        lay_out(grad_gate, True)
        yield
        for copy in outs:
            copy.wait()
        sum_out[...] = sum(came_out[other].astype(F32) for other in range(places))
        for copy in shares:
            copy.wait()
        blocks[...] = sum(came_qkv[other].astype(F32) for other in range(places)).astype(BF16)
        moves.extend(turn_copies(blocks, spread, turn_s, turn_r))
        moves.append(pltpu.make_async_copy(blocks.at[plane], spread.at[plane], stay.at[2]))
        for copy in moves:
            copy.start()
        yield
        lay_out(grad_up, False)

    in_turn(*scatters(part, rest, grad), others())
    values, above = tokens[...].astype(F32), grad[...]
    scaled = above * gains[0:1, mine]
    local[:, :LANES] = fold(scaled * values)
    local[:, LANES:] = fold(values * values)
    total, square = both_cores(local, far, send, receive)
    scale = lax.rsqrt(square / part.shape[2] + EPSILON)
    sums[...] = jnp.zeros_like(sums)
    sums[0:1, :] = jnp.sum(above * values * scale, axis=0, keepdims=True)
    sums[1:2, :] = gain_two[...]
    finish = to_owners(sums, came_gains, own_s, own_r)
    mean = total / part.shape[2]
    grad[...] = resid_grad[...] + scale * scaled - values * scale**3 * mean
    for copy in moves:
        copy.wait()
    wide = grad_value.shape[1] // PLANES
    slim = grad_query.shape[1] // PLANES
    found = [spread[to].astype(F32) for to in range(PLANES)]
    for to in range(PLANES):
        grad_value[:, to * wide : (to + 1) * wide] = found[to][:, :wide]
    grad_query[...] = jnp.concatenate([one[:, wide : wide + slim] for one in found], axis=1)
    grad_key[...] = jnp.concatenate([one[:, wide + slim :] for one in found], axis=1)
    finish(out_gains)


def end_kernel(
    far_part,
    far_fed,
    parts_gu,
    far_normed,
    resid,
    inverse,
    gains,
    cotangent,
    tokens,
    far_out,
    far_attended,
    far_seq,
    lens,
    far_att,
    far_norms,
    far_qkv,
    mixed,
    grad,
    sum_out,
    grad_query,
    grad_key,
    grad_value,
    grad_gate,
    grad_up,
    out_gains,
    part,
    fed,
    low,
    resid_grad,
    total_fed,
    came_gu,
    blocks_gu,
    joined,
    grad_att,
    rows_in,
    rows_out,
    keep,
    grad_qkv,
    parts_out,
    came_out,
    parts_qkv,
    came_qkv,
    blocks,
    spread,
    sums,
    came_gains,
    w_out,
    attended,
    seq,
    att,
    norms,
    w_qkv,
    local,
    far,
    local_two,
    far_two,
    sum_s,
    sum_r,
    load,
    gu_s,
    gu_r,
    gu_l,
    turn_gu_s,
    turn_gu_r,
    row_s,
    row_r,
    row_l,
    back_s,
    back_r,
    back_l,
    out_s,
    out_r,
    qkv_s,
    qkv_r,
    turn_s,
    turn_r,
    own_s,
    own_r,
    stay,
    hold,
    *rest,
):
    plane, place, core = here()
    places = lax.axis_size("p")
    mine, _ = halves(part.shape[2])
    width = part.shape[2]
    own_rows = parts_qkv.shape[2]
    rows = grad_att.shape[1]
    per_row = places // rows
    size = part.shape[1] // PARTS
    cuts = [pl.ds(at * size, size) for at in range(PARTS)]
    gather_at, first_at, fed_at, last_at = (PARTS * n for n in (0, 5, 13, 21))
    buffers = [rest[first_at + 8 * at : first_at + 8 * at + 2] for at in range(PARTS)]
    last_sems = [rest[last_at + 6 * at : last_at + 6 * at + 6] for at in range(PARTS)]
    greeted = greet_all()
    loads = [
        pltpu.make_async_copy(far_part, part, load.at[0]),
        pltpu.make_async_copy(far_fed, fed, load.at[1]),
    ]
    pairs = [
        (far_out, w_out),
        (far_attended, attended),
        (far_seq, seq),
        (far_att, att),
        (far_norms, norms),
        (far_qkv, w_qkv),
    ]
    holds = [
        pltpu.make_async_copy(source, target, hold.at[at])
        for at, (source, target) in enumerate(pairs)
    ]
    for copy in loads + holds:
        copy.start()
    plane_gu = [pltpu.make_async_copy(parts_gu.at[place], came_gu.at[place], gu_l)]
    for step in range(1, places):
        to = lax.rem(place + step, places)
        plane_gu.append(
            remote(
                parts_gu.at[to], came_gu.at[place], gu_s.at[step], gu_r.at[step], (plane, to, core)
            )
        )
    loads[0].wait()
    greeted()
    for copy in plane_gu:
        copy.start()

    in_turn(*scatters(part, rest[first_at:fed_at], resid_grad))
    loads[1].wait()
    for copy in holds:
        copy.wait()
    scale = inverse[:, :1]
    values, above = resid[...], resid_grad[...]
    scaled = above * gains[1:2, mine]
    local[...] = fold(scaled * values)
    (total,) = both_cores(local, far, sum_s.at[0], sum_r.at[0])
    mean = total / width
    resid_grad[...] = cotangent[...].astype(F32) + scale * scaled - values * scale**3 * mean
    low[plane, :, mine] = resid_grad[...].astype(BF16)
    sums[...] = jnp.zeros_like(sums)

    def row_copy(block, step):
        to = lax.rem(place + step, places)
        return remote(
            grad_att.at[block, lax.div(to, per_row)],
            rows_in.at[block, place],
            row_s.at[block, step],
            row_r.at[block, step],
            (plane, to, core),
        )

    def own_row(block):
        return pltpu.make_async_copy(
            grad_att.at[block, lax.div(place, per_row)], rows_in.at[block, place], row_l.at[block]
        )

    all_lows = [
        Gather(low.at[:, cut], rest[gather_at + 5 * at : gather_at + 5 * at + 5])
        for at, cut in enumerate(cuts)
    ]

    def to_rows(block):
        for gather in all_lows:
            gather.whole(block)
        product = dot(low[block], w_out[...], ((1,), (1,))).astype(BF16)
        grad_att[block] = product.reshape(grad_att.shape[1:])
        for step in range(1, places):
            row_copy(block, step).start()
        own_row(block).start()

    def lows():
        for gather in all_lows:
            gather.start()
        yield
        sums[1:2, :] = jnp.sum(above * values * scale, axis=0, keepdims=True)
        for step in range(1, PLANES):
            for gather in all_lows:
                gather.pass_on(step)
            to_rows(order_of_arrival(step - 1))
            yield
        to_rows(order_of_arrival(PLANES - 1))
        for gather in all_lows:
            gather.finish()

    in_turn(lows(), *scatters(fed, rest[fed_at:last_at], total_fed))
    mixed[...] = (total_fed[...] + resid[...]).astype(BF16)
    normed_load = pltpu.make_async_copy(far_normed, fed, load.at[2])
    normed_load.start()
    for copy in plane_gu:
        copy.wait()
    for to in range(PLANES):
        total_gu = sum(came_gu[other, to].astype(F32) for other in range(places))
        blocks_gu[to] = total_gu.astype(BF16)
    gu_turns = turn_copies(blocks_gu, joined, turn_gu_s, turn_gu_r)
    gu_turns.append(pltpu.make_async_copy(blocks_gu.at[plane], joined.at[plane], stay.at[3]))
    for copy in gu_turns:
        copy.start()

    alive = alive_of(lens, att.shape[0], rows)
    for block in range(PLANES):
        for step in range(1, places):
            row_copy(block, step).wait()
        own_row(block).wait()
    attend_back(seq, alive, att, norms, rows_in, keep, rows_out)
    finish = start_back(rows_out, grad_qkv, back_s, back_r, back_l)
    for at in range(0, width, TILE):
        cut = slice(at, at + TILE)
        product = sum(
            dot(attended[block], low[block, :, cut], ((0,), (0,))) for block in range(PLANES)
        )
        parts_out[:, :, cut] = product.astype(BF16).reshape(parts_out.shape[:2] + (TILE,))
    outs = [pltpu.make_async_copy(parts_out.at[place], came_out.at[place], stay.at[0])]
    shares = [pltpu.make_async_copy(parts_qkv.at[:, place], came_qkv.at[place], stay.at[1])]
    moves = []
    for step in range(1, places):
        to = lax.rem(place + step, places)
        device = (plane, to, core)
        outs.append(
            remote(parts_out.at[to], came_out.at[place], out_s.at[step], out_r.at[step], device)
        )
        shares.append(
            remote(
                parts_qkv.at[:, to], came_qkv.at[place], qkv_s.at[step], qkv_r.at[step], device
            )
        )
    finish()
    for copy in outs:
        copy.start()
    normed_load.wait()

    flat_weights = w_qkv[...].reshape(width, grad_qkv.shape[3])
    count = part.shape[1]
    for block in range(PLANES):
        rows_of = grad_qkv[block].reshape(count, grad_qkv.shape[3])
        part[block] = dot(rows_of, flat_weights, ((1,), (1,))).astype(BF16)
    def lay_out(grads, first):
        units = joined.shape[2] // 2
        broad = units // LANES * LANES
        left = units - broad
        extent = grads.shape[0] // PLANES
        for to in range(PLANES):
            piece = joined[to].astype(F32)
            low_at = 2 * broad + (0 if first else left)
            start = 0 if first else broad
            pieces = [piece[:, start : start + broad]]
            if left:
                pieces.append(piece[:, low_at : low_at + left])
            found = jnp.concatenate(pieces, axis=1)
            grads[to * extent : (to + 1) * extent, :] = unpack_units(
                found, places, units // places, extent // places
            )

    def others():
        tokens_all = PLANES * count
        grads = grad_qkv[...].reshape(tokens_all, grad_qkv.shape[3])
        for at in range(0, width, TILE):
            left = fed[:, :, at : at + TILE].reshape(tokens_all, TILE)
            product = dot(left, grads, ((0,), (0,))).astype(BF16)
            for row in range(0, TILE, own_rows):
                owner = (at + row) // own_rows
                parts_qkv[owner // places, owner % places] = product[row : row + own_rows]
        for copy in shares:
            copy.start()
        yield
        for copy in gu_turns:
            copy.wait()
        lay_out(grad_gate, True)
        yield
        for copy in shares:
            copy.wait()
        blocks[...] = sum(came_qkv[other].astype(F32) for other in range(places)).astype(BF16)
        moves.extend(turn_copies(blocks, spread, turn_s, turn_r))
        moves.append(pltpu.make_async_copy(blocks.at[plane], spread.at[plane], stay.at[2]))
        for copy in moves:
            copy.start()
        yield
        lay_out(grad_up, False)
        for copy in outs:
            copy.wait()
        sum_out[...] = sum(came_out[other].astype(F32) for other in range(places))

    lasts = [
        column_scatter(part.at[:, cut], (*buffers[at], *last_sems[at]), grad.at[cut])
        for at, cut in enumerate(cuts)
    ]
    in_turn(*lasts, others())
    values, above = tokens[...].astype(F32), grad[...]
    scaled = above * gains[0:1, mine]
    local_two[:, :LANES] = fold(scaled * values)
    local_two[:, LANES:] = fold(values * values)
    total, square = both_cores(local_two, far_two, sum_s.at[1], sum_r.at[1])
    scale = lax.rsqrt(square / width + EPSILON)
    sums[0:1, :] = jnp.sum(above * values * scale, axis=0, keepdims=True)
    finish = to_owners(sums, came_gains, own_s, own_r)
    mean = total / width
    grad[...] = resid_grad[...] + scale * scaled - values * scale**3 * mean
    for copy in moves:
        copy.wait()
    wide = grad_value.shape[1] // PLANES
    slim = grad_query.shape[1] // PLANES
    found = [spread[to].astype(F32) for to in range(PLANES)]
    for to in range(PLANES):
        grad_value[:, to * wide : (to + 1) * wide] = found[to][:, :wide]
    grad_query[...] = jnp.concatenate([one[:, wide : wide + slim] for one in found], axis=1)
    grad_key[...] = jnp.concatenate([one[:, wide + slim :] for one in found], axis=1)
    finish(out_gains)


def to_owners(sums, came, send, receive):
    plane, place, core = here()
    places = lax.axis_size("p")
    count = PLANES * places
    near = count // 2
    index = plane * places + place
    side = lax.div(index, near)
    width = sums.shape[1] // near

    def copy(step, target):
        at = step * width // LANES * LANES
        owner = core * near + step
        device = (lax.div(owner, places), lax.rem(owner, places), target)
        return remote(
            sums.at[:, pl.ds(at, LANES)],
            came.at[index],
            send.at[2 * step + target],
            receive.at[index],
            device,
        )

    def to_self(step, target):
        return (core * near + step == index) & (core == target)

    for step in range(near):
        for target in range(2):
            local = to_self(step, target)
            pl.when(jnp.logical_not(local))(lambda: copy(step, target).start())

            @pl.when(local)
            def _():
                at = step * width // LANES * LANES
                came[index] = sums[:, at : at + LANES]

    def finish(out):
        for step in range(count):
            source = lax.rem(index + step, count)

            @pl.when((step > 0) | (side != core))
            def _():
                remote(
                    came.at[source],
                    came.at[source],
                    send.at[0],
                    receive.at[source],
                    (plane, place, 1 - core),
                ).wait_recv()

        out[...] = sum(came[step] for step in range(count))
        for step in range(near):
            for target in range(2):
                local = to_self(step, target)
                pl.when(jnp.logical_not(local))(lambda: copy(step, target).wait_send())

    return finish


def call(kernel, identity, micros, outs, scratch, args, far_args=(), far_outs=()):
    def spec(far):
        return pl.BlockSpec(memory_space=pl.ANY if far else pltpu.VMEM)

    return pl.pallas_call(
        kernel,
        out_shape=outs,
        in_specs=[spec(at in far_args) for at in range(len(args))],
        out_specs=[spec(at in far_outs) for at in range(len(outs))],
        scratch_shapes=scratch,
        cost_estimate=pl.CostEstimate(
            flops=micros * 10**9, bytes_accessed=micros * 10**6, transcendentals=0
        ),
        compiler_params=pltpu.CompilerParams(
            collective_id=identity, has_side_effects=True, vmem_limit_bytes=VMEM_LIMIT
        ),
    )(*args)


def shape(dims, dtype):
    return jax.ShapeDtypeStruct(dims, dtype)


def front(x_half, c_half, gain_one, gain_two, w_query, w_key, w_value, w_gate, w_up, w_output, lens, units, identity):
    tokens, half = x_half.shape
    places = lax.axis_size("p")
    count = PLANES * places
    rows = lens.size
    positions = tokens // rows
    length = PLANES * places * positions
    own_rows = w_query.shape[0]
    wide = w_value.shape[1] // PLANES
    width = wide + 2 * (w_query.shape[1] // PLANES)
    whole = (PLANES, tokens, 2 * half)
    blocks = (PLANES, own_rows, width)
    gu = (PLANES, own_rows, 2 * units)
    return call(
        front_kernel,
        identity,
        150,
        [
            shape(whole, BF16),
            shape((PLANES, places, own_rows, width), BF16),
            shape((8, 2 * half), F32),
            shape((length, wide), F32),
            shape((length, wide), F32),
            shape((PLANES, rows, positions, wide), BF16),
            shape((PLANES, places, positions, width), BF16),
            shape((PLANES, places, own_rows, 2 * units), BF16),
            shape((places,) + w_output.shape, BF16),
            shape((tokens, half), BF16),
            shape((tokens, half), F32),
            shape((tokens, LANES), F32),
            shape(whole, BF16),
        ],
        [
            pltpu.VMEM((PLANES, places, own_rows, width), BF16),
            pltpu.VMEM((length, wide), F32),
            pltpu.VMEM((length, wide), F32),
            pltpu.VMEM((PLANES, places, positions, width), BF16),
            pltpu.VMEM((places,) + w_output.shape, BF16),
            pltpu.VMEM(whole, BF16),
            pltpu.VMEM(whole, BF16),
            pltpu.VMEM((PLANES, rows, positions, width), BF16),
            pltpu.VMEM(blocks, BF16),
            pltpu.VMEM(blocks, BF16),
            pltpu.VMEM((8, LANES), F32),
            pltpu.VMEM((8, LANES), F32),
            pltpu.VMEM((8, LANES), F32),
            pltpu.VMEM((count, 8, LANES), F32),
            pltpu.VMEM(gu, BF16),
            pltpu.VMEM(gu, BF16),
            pltpu.VMEM((PLANES, places, positions, wide), BF16),
            pltpu.VMEM(whole, BF16),
        ]
        + sums_scratch(tokens, 1)
        + [DMA((5,)), DMA, DMA]
        + [DMA((PLANES,)), DMA((PLANES,)), DMA((count,)), DMA((count,))]
        + [DMA((places,)) for _ in range(4)]
        + [DMA((PLANES, places)), DMA((PLANES, places)), DMA((PLANES,))]
        + [DMA((places,)), DMA((rows,)), DMA]
        + [DMA((PLANES,)), DMA((PLANES,)), DMA]
        + [DMA((PLANES, places)), DMA((PLANES, places)), DMA((PLANES,)), DMA((PLANES,)), DMA((5,))]
        + gather_scratch() * (1 + PARTS)
        + scatter_scratch(tokens // PARTS, half) * PARTS,
        [
            x_half,
            c_half,
            gain_one,
            gain_two,
            w_query,
            w_key,
            w_value,
            w_gate,
            w_up,
            w_output,
            lens,
        ],
        (1,),
        (0, 1, 3, 4, 6, 7, 8, 12),
    )


def sums_scratch(tokens, count):
    return [pltpu.VMEM((tokens, count * LANES), F32) for _ in range(2)] + [DMA, DMA]


def feed(own, w_gu, w_dn, grads, identity):
    tokens, half = own.shape
    units, width = w_dn.shape
    places = lax.axis_size("p")
    whole = (PLANES, tokens, width)
    return call(
        feed_kernel,
        identity,
        55,
        [
            shape(whole, BF16),
            shape(whole, BF16),
            shape((places, PLANES, width // (PLANES * places), 2 * units), BF16),
            shape(w_dn.shape, BF16),
        ],
        [
            pltpu.VMEM(whole, BF16),
            pltpu.VMEM(w_gu.shape, BF16),
            pltpu.VMEM(w_dn.shape, BF16),
            pltpu.VMEM(whole, BF16),
            pltpu.VMEM(w_gu.shape, F32),
            pltpu.VMEM(w_dn.shape, F32),
            pltpu.VMEM((tokens, 2 * units), F32),
            pltpu.VMEM((tokens, -(-units // LANES) * LANES), F32),
            pltpu.VMEM((tokens, units), BF16),
            pltpu.VMEM((tokens, 2 * units), BF16),
            pltpu.VMEM((2, 2, tokens, width), BF16),
            DMA((3,)),
            DMA,
            DMA((2, 2)),
            DMA((PLANES * places,)),
        ]
        + gather_scratch(),
        [own, w_gu, w_dn, grads],
        (1, 2, 3),
        (0, 1, 2, 3),
    )


def row_sems(rows):
    places = lax.axis_size("p")
    sems = [DMA((places,)), DMA((places,)), DMA, DMA((places,)), DMA((rows,)), DMA]
    return sems + [DMA((PLANES,)), DMA((PLANES,)), DMA]


def attend_back_alone(grad_mix, w_out, attended, seq, lens, att, norms, blocks, rows, identity):
    places = lax.axis_size("p")
    positions = grad_mix.shape[1] // rows
    wide = w_out.shape[0]
    width = seq.shape[-1]
    return call(
        attend_back_kernel,
        identity,
        35,
        [
            shape((PLANES, rows, positions, width), BF16),
            shape(blocks.shape, BF16),
            shape((places, wide // places, grad_mix.shape[2]), BF16),
        ],
        [
            pltpu.VMEM((PLANES, rows, positions, wide), BF16),
            pltpu.VMEM(seq.shape[:-1] + (wide,), BF16),
            pltpu.VMEM(seq.shape, BF16),
            pltpu.VMEM((att.shape[0], wide + LANES), F32),
        ]
        + row_sems(rows),
        [grad_mix, w_out, attended, seq, lens, att, norms, blocks],
        (7,),
        (1,),
    )


def mix_back(part, resid, inverse, gains, cotangent, fed, identity):
    tokens, half = resid.shape
    whole = (PLANES, tokens, 2 * half)
    return call(
        back_kernel,
        identity,
        95,
        [
            shape(whole, BF16),
            shape((tokens, half), F32),
            shape((1, half), F32),
            shape((tokens, half), BF16),
        ],
        [pltpu.VMEM(whole, BF16), pltpu.VMEM(whole, BF16)]
        + sums_scratch(tokens, 1)
        + [DMA((2,)), pltpu.VMEM((tokens, half), F32)]
        + gather_scratch() * PARTS
        + scatter_scratch(tokens // PARTS, half) * 2 * PARTS,
        [part, resid, inverse, gains, cotangent, fed],
        (0, 5),
    )


def last_back(grad_qkv, w_qkv, normed, tokens, gains, resid_grad, parts_out, joined, gain_two, units, identity):
    size, half = tokens.shape
    places = lax.axis_size("p")
    count = PLANES * places
    own_rows, width = w_qkv.shape[2:]
    slim = (width - parts_out.shape[0] * parts_out.shape[1]) // 2
    blocks = (PLANES, own_rows, width)
    outs = [
        (size, half),
        parts_out.shape[1:],
        (own_rows, PLANES * slim),
        (own_rows, PLANES * slim),
        (own_rows, PLANES * (width - 2 * slim)),
        (units, own_rows),
        (units, own_rows),
        (8, LANES),
    ]
    return call(
        last_kernel,
        identity,
        60,
        [shape(dims, F32) for dims in outs],
        [
            pltpu.VMEM((PLANES, size, 2 * half), BF16),
            pltpu.VMEM((PLANES, places, own_rows, width), BF16),
            pltpu.VMEM((8, half), F32),
            pltpu.VMEM((count, 8, LANES), F32),
        ]
        + sums_scratch(size, 2)
        + [
            pltpu.VMEM(parts_out.shape, BF16),
            pltpu.VMEM((places,) + blocks, BF16),
            pltpu.VMEM(blocks, BF16),
            pltpu.VMEM(blocks, BF16),
            DMA((3,)),
        ]
        + [DMA((places,)) for _ in range(4)]
        + [DMA((PLANES,)) for _ in range(2)]
        + [DMA((count,)) for _ in range(2)]
        + scatter_scratch(size // PARTS, half) * PARTS,
        [grad_qkv, w_qkv, normed, tokens, gains, resid_grad, parts_out, joined, gain_two],
    )


def end(far, near, units, identity):
    resid, seq, att, w_qkv = near[0], near[7], near[9], near[11]
    tokens, half = resid.shape
    places = lax.axis_size("p")
    count = PLANES * places
    rows = near[8].size
    positions = tokens // rows
    own_rows, width = w_qkv.shape[2:]
    wide = att.shape[1]
    slim = (width - wide) // 2
    whole = (PLANES, tokens, 2 * half)
    blocks = (PLANES, own_rows, width)
    gu = far[2].shape
    outs = [
        ((tokens, half), BF16),
        ((tokens, half), F32),
        ((wide // places, 2 * half), F32),
        ((own_rows, PLANES * slim), F32),
        ((own_rows, PLANES * slim), F32),
        ((own_rows, PLANES * wide), F32),
        ((units, own_rows), F32),
        ((units, own_rows), F32),
        ((8, LANES), F32),
    ]
    parts_out = (places, wide // places, 2 * half)
    scratch = [
        (whole, BF16),
        (whole, BF16),
        (whole, BF16),
        ((tokens, half), F32),
        ((tokens, half), F32),
        (gu, BF16),
        (gu[1:], BF16),
        (gu[1:], BF16),
        ((PLANES, rows, positions, wide), BF16),
        ((PLANES, places, positions, wide), BF16),
        (seq.shape, BF16),
        ((att.shape[0], wide + LANES), F32),
        ((PLANES, rows, positions, width), BF16),
        (parts_out, BF16),
        (parts_out, BF16),
        ((PLANES, places, own_rows, width), BF16),
        ((places,) + blocks, BF16),
        (blocks, BF16),
        (blocks, BF16),
        ((8, half), F32),
        ((count, 8, LANES), F32),
        *[(near[at].shape, near[at].dtype) for at in (5, 6, 7, 9, 10, 11)],
        ((tokens, LANES), F32),
        ((tokens, LANES), F32),
        ((tokens, 2 * LANES), F32),
        ((tokens, 2 * LANES), F32),
    ]
    sems = [(2,), (2,), (3,), (places,), (places,), (), (PLANES,), (PLANES,)]
    sems += [(PLANES, places), (PLANES, places), (PLANES,), (places,), (rows,), ()]
    sems += [(places,)] * 4 + [(PLANES,)] * 2 + [(count,)] * 2 + [(4,), (6,)]
    return call(
        end_kernel,
        identity,
        190,
        [shape(dims, kind) for dims, kind in outs],
        [pltpu.VMEM(dims, kind) for dims, kind in scratch]
        + [DMA(dims) if dims else DMA for dims in sems]
        + gather_scratch() * PARTS
        + scatter_scratch(tokens // PARTS, half) * 2 * PARTS
        + scatter_sems() * PARTS,
        [*far, *near],
        (0, 1, 2, 3, 9, 10, 11, 13, 14, 15),
    )


def end_in_parts(far, near, units, identities):
    part, fed, parts_gu, normed_one = far
    resid, inverse, gains, cotangent, tokens, w_out, attended, seq, lens, att, norms, w_qkv = near
    rows = lens.size
    blocks_gu = lax.psum_scatter(parts_gu, "p", scatter_dimension=0, tiled=False)
    grad_mix, grad_resid, gain_two, mixed = mix_back(
        part, resid, inverse, gains, cotangent, fed, identities[0]
    )
    grad_qkv, blocks_gu, out_output = attend_back_alone(
        grad_mix, w_out, attended, seq, lens, att, norms, blocks_gu, rows, identities[1]
    )
    grad_qkv = grad_qkv.reshape(PLANES, -1, grad_qkv.shape[-1])
    rest = last_back(
        grad_qkv,
        w_qkv,
        normed_one,
        tokens,
        gains,
        grad_resid,
        out_output,
        blocks_gu,
        gain_two,
        units,
        identities[2],
    )
    return (mixed, *rest)


def deliver_kernel(padded, gains, *rest):
    count = (len(rest) - 5) // 3
    ready = rest[:count]
    down, one, two = rest[count : count + 3]
    places = rest[count + 3 : 2 * count + 3]
    held = rest[2 * count + 3 : -2]
    load, store = rest[-2:]
    loads = [
        pltpu.make_async_copy(source, target, load.at[at])
        for at, (source, target) in enumerate(zip(ready, held))
    ]
    stores = [
        pltpu.make_async_copy(source, target, store.at[at])
        for at, (source, target) in enumerate(zip(held, places))
    ]
    for copy in loads:
        copy.start()
    plane, place, core = here()
    index = plane * lax.axis_size("p") + place
    size = one.shape[1]
    at = lax.rem((2 * index + core) * size, LANES)
    turned = pltpu.roll(gains[...], lax.rem(LANES - at, LANES), 1)
    one[...] = turned[0:1, :size]
    two[...] = turned[1:2, :size]
    for one_load, one_store in zip(loads, stores):
        one_load.wait()
        one_store.start()
    down[...] = padded[: down.shape[0], :].astype(F32)
    for copy in stores:
        copy.wait()


def deliver(padded, chunk, gains, own_gain, ready):
    vmem, far = (pl.BlockSpec(memory_space=space) for space in (pltpu.VMEM, pl.ANY))
    small = [shape((chunk, padded.shape[1]), F32), shape((1, own_gain), F32), shape((1, own_gain), F32)]
    return pl.pallas_call(
        deliver_kernel,
        out_shape=small + [shape(one.shape, one.dtype) for one in ready],
        in_specs=[vmem, vmem] + [far] * len(ready),
        out_specs=[vmem] * 3 + [far] * len(ready),
        scratch_shapes=[pltpu.VMEM(one.shape, one.dtype) for one in ready]
        + [DMA((len(ready),)), DMA((len(ready),))],
        compiler_params=pltpu.CompilerParams(vmem_limit_bytes=VMEM_LIMIT),
    )(padded, gains, *ready)


def dot(left, right, dims=((1,), (0,))):
    return lax.dot_general(left, right, (dims, ((), ())), preferred_element_type=F32)


def pad_units(weights, axis, chunk, padded):
    shape = weights.shape
    weights = weights.reshape(shape[:axis] + (-1, chunk) + shape[axis + 1 :])
    pads = [(0, 0)] * weights.ndim
    pads[axis + 1] = (0, padded - chunk)
    return jnp.pad(weights, pads).reshape(shape[:axis] + (-1,) + shape[axis + 1 :])


def on_device(
    tokens,
    lengths,
    attn_gain,
    w_query,
    w_key,
    w_value,
    w_output,
    ffn_gain,
    w_gate,
    w_up,
    w_down,
    cotangent,
):
    count = lax.axis_size("p")
    batches, per_batch, own_len, half = tokens.shape
    rows = batches * per_batch
    own_rows = w_query.shape[0]
    heads = w_query.shape[1] // FEAT // PLANES
    chunk = w_down.shape[0]
    padded = -(-chunk // 16) * 16
    units = count * padded
    slim, broad = heads * FEAT, heads * HEAD_V

    x_half = tokens.reshape(rows * own_len, half)
    c_half = cotangent.reshape(rows * own_len, half)
    w_dn = lax.all_gather(pad_units(w_down, 0, chunk, padded), "p", axis=0, tiled=True)
    (
        normed_one,
        w_qkv,
        gains,
        att,
        norms,
        attended,
        seq,
        w_gu,
        w_out,
        normed_two,
        resid,
        inv_two,
        c_all,
    ) = front(
        x_half,
        c_half,
        attn_gain[None],
        ffn_gain[None],
        w_query,
        w_key,
        w_value,
        w_gate.T,
        w_up.T,
        w_output,
        lengths,
        units,
        0,
    )
    attended = attended.reshape(PLANES, -1, broad)
    w_gu = w_gu.reshape(-1, 2 * units)
    w_out = w_out.reshape(broad, -1)
    part, fed, out_gu, out_down = feed(normed_two, w_gu, w_dn, c_all, 1)
    out_down = lax.psum_scatter(out_down, "p", scatter_dimension=0, tiled=True)
    names = (resid, inv_two, gains, c_half, x_half, w_out, attended, seq, lengths, att, norms, w_qkv)
    if PLANES * count * own_len <= MERGED_LENGTH:
        ends = end((part, fed, out_gu, normed_one), names, w_gate.shape[1], 2)
    else:
        ends = end_in_parts((part, fed, out_gu, normed_one), names, w_gate.shape[1], (4, 5, 6))
    *ready, gain_sums = ends
    down, one, two, *ready = deliver(out_down, chunk, gain_sums, attn_gain.shape[0], ready)
    mixed, grad_tokens, out_output, out_query, out_key, out_value, out_gate, out_up = ready
    return (
        mixed.reshape(tokens.shape),
        grad_tokens.reshape(tokens.shape),
        one.reshape(-1),
        out_query,
        out_key,
        out_value,
        out_output,
        two.reshape(-1),
        out_gate.T,
        out_up.T,
        down,
    )


def solution(mesh):
    split = Mesh(mesh.devices.reshape(PLANES, -1, 2), ("z", "p", "core"))
    seq = ("z", "p")
    both = ("z", "p", "core")
    rows, columns = P(seq, "core"), P(("core", "z", "p"), None)
    tokens = P(None, None, seq, "core")
    return jax.shard_map(
        on_device,
        mesh=split,
        in_specs=(
            tokens,
            P(),
            P(both),
            rows,
            rows,
            rows,
            columns,
            P(both),
            rows,
            rows,
            columns,
            tokens,
        ),
        out_specs=(
            tokens,
            tokens,
            P(both),
            rows,
            rows,
            rows,
            columns,
            P(both),
            rows,
            rows,
            columns,
        ),
        check_vma=False,
    )
```
